512 devices in a mesh: seq: 64 (over y, z), head: 8 (over x, core).
Axes of the slice: x: 4, y: 8, z: 8, core: 2. Of those that a mesh axis runs over, the one named last changes fastest.
Arguments:
- byte_stream: bfloat16 [8192, 2048], P('seq', 'head'), may hold values from -6 to 6
- gate_stream: bfloat16 [8192, 2048], P('seq', 'head'), may hold values from -6 to 6
- conv_weight: float32 [4, 2048], P(None, 'head'), may hold values from -3 to 3
- state_write: bfloat16 [8192, 128], P('seq'), may hold values from -6 to 6
- state_read: bfloat16 [8192, 128], P('seq'), may hold values from -0.5 to 0.5
- step_size: float32 [8192, 32], P('seq', 'head'), as said below
- decay_coef: float32 [32], P('head'), as said below
- skip_gain: float32 [32], P('head'), may hold values from 0.5 to 2
- norm_gain: float32 [2048], P('head'), may hold values from 0.25 to 1.75
- mixer_out: bfloat16 [2048, 1024], P('head'), may hold values from -0.125 to 0.125
- residual: bfloat16 [8192, 1024], P('seq'), may hold values from -6 to 6
- boundaries: int32 [64, 32], P('seq'), may hold values from 0 to 8192, as said below
- span_counts: int32 [64], P('seq'), may hold values from 8 to 32, as said below
- span_offsets: int32 [64], P('seq'), may hold values from 0 to 1016, as said below
- pad_vector: bfloat16 [3072], replicated, may hold values from -6 to 6
- main_gain: float32 [4096], replicated, may hold values from 0.25 to 1.75
- query_weight: bfloat16 [4096, 4096], P('seq', 'head')
- key_value_weight: bfloat16 [4096, 2048], P('seq', 'head')
- main_out_weight: bfloat16 [4096, 1024], P('head'), may hold values from -0.09375 to 0.09375
Outputs:
- byte_output: bfloat16 [8192, 1024], P('seq', 'head')
The draws below stay inside these ranges and needn't reach their ends.
Inputs may be any that keep to these rules, and one draw needn't show every extreme that they name: `boundaries`: row b lists span_counts[b] increasing byte positions of bytes b * 128 to (b + 1) * 128 - 1, the first being b * 128; the other entries are 8192. `span_counts`: they sum to 1024; one block holds exactly 32. `span_offsets`: the exclusive prefix sums of span_counts. `step_size`: Positive. `decay_coef`: Positive.
All inputs are finite; a program needn't handle non-finite values.
Results may differ from the reference program's by a relative error of at most 0.03.
Values may be sent and summed in bfloat16 or wider, within the bound.
A program may use at most 64 MiB of HBM per device.

```python
import math
import jax
import jax.numpy as jnp
from jax import lax

D_ENC = 1024
NH = 32
HP = 64
NSTATE = 128
KCONV = 4
NGROUP = 8
D_MAIN = 4096
QH = 32
KVH = 8
HD = 128
L_DEV = 128
CAP = 32
BYTES = 8192
SPANS = 1024
D_INNER = 2048
PAD = 3072
N_SEQ = 64


def head_rates(key, fast_share):
    flag_key, slow_key, fast_key = jax.random.split(key, 3)
    quick = jax.random.uniform(flag_key, (NH,)) < fast_share
    slow_rate = jax.random.uniform(slow_key, (NH,), minval=0.3, maxval=0.8) / BYTES
    fast_rate = jax.random.uniform(fast_key, (NH,), minval=1.0 / 50.0, maxval=1.0 / 30.0)
    return jnp.where(quick, fast_rate, slow_rate)


def draw_decay_coef(key, part):
    rates = head_rates(key, 0.5)
    return (8.0 * jnp.sqrt(rates)).astype(jnp.float32)


def draw_step_size(key, part):
    rates = head_rates(key, 0.5)
    key = jax.random.fold_in(key, 7)
    decay_factor = 8.0 * jnp.sqrt(rates)
    rough_key, device_key, spot_key, cut_key = jax.random.split(key, 4)
    rough = jax.random.uniform(rough_key, (BYTES, NH), minval=0.5, maxval=1.5)
    shard_count = BYTES // L_DEV
    device_factor = jnp.exp(jax.random.uniform(device_key, (shard_count,), minval=math.log(0.5), maxval=math.log(2.0)))
    device_factor = jnp.repeat(device_factor, L_DEV)
    initial_step_size = rough * device_factor[:, None] * jnp.sqrt(rates)[None, :] / 8.0
    spots = jax.random.randint(spot_key, (3,), 0, BYTES)
    boundary_cuts = jax.random.uniform(cut_key, (3, NH), minval=0.2, maxval=0.5)
    boundary_hits = (jnp.arange(BYTES)[:, None] == spots[None, :]).astype(jnp.float32)
    boundary_flags = jnp.sum(boundary_hits[:, :, None] * (boundary_cuts / decay_factor[None, :])[None, :, :], axis=1)
    return jnp.where(jnp.sum(boundary_hits, axis=1)[:, None] > 0, boundary_flags, initial_step_size).astype(jnp.float32)


def query_base(key):
    return jax.random.normal(key, (D_MAIN, QH * HD)) * math.sqrt(2.5 / D_MAIN)


def draw_query_weight(key, part):
    base_weight = query_base(key)
    return base_weight.astype(jnp.bfloat16)


def draw_key_value_weight(key, part):
    key = jax.random.fold_in(key, 17)
    key_key, value_key = jax.random.split(key, 2)
    key_part = jax.random.normal(key_key, (D_MAIN, KVH, HD)) * math.sqrt(2.5 / D_MAIN)
    value_part = jax.random.normal(value_key, (D_MAIN, KVH, HD)) / math.sqrt(D_MAIN)
    return jnp.stack([key_part, value_part], axis=2).reshape(D_MAIN, 2 * KVH * HD).astype(jnp.bfloat16)


def pick_positions(pick_key, wanted):
    order = jax.random.permutation(pick_key, L_DEV).astype(jnp.int32)
    place = jnp.arange(L_DEV, dtype=jnp.int32)
    order = jnp.where(place == 0, -1, order)
    ranking = jnp.argsort(jnp.argsort(order))
    chosen = ranking < wanted
    return jnp.sort(jnp.where(chosen, place, L_DEV + place))[:CAP]


def span_layout(key):
    shard_count = BYTES // L_DEV
    row_quota = L_DEV // 8
    order_key, delta_key, pick_key = jax.random.split(key, 3)
    order = jax.random.permutation(order_key, shard_count).astype(jnp.int32)
    last_spot = jnp.argmax(order == shard_count - 1).astype(jnp.int32)
    second = order[1]
    order = order.at[last_spot].set(second).at[1].set(shard_count - 1)
    delta = jax.random.randint(delta_key, ((shard_count - 4) // 2,), 0, row_quota // 2 + 1)
    paired = jnp.stack([row_quota + delta, row_quota - delta], axis=1).reshape(-1)
    leading = jnp.array([2 * row_quota, row_quota // 2, row_quota // 2, row_quota], jnp.int32)
    by_rank = jnp.concatenate([leading, paired.astype(jnp.int32)])
    counts = jnp.zeros((shard_count,), jnp.int32).at[order].set(by_rank)
    offsets = (jnp.cumsum(counts) - counts).astype(jnp.int32)
    picked = jax.vmap(pick_positions)(jax.random.split(pick_key, shard_count), counts)
    column = jnp.arange(CAP, dtype=jnp.int32)
    starts = (jnp.arange(shard_count, dtype=jnp.int32) * L_DEV)[:, None]
    bounds = jnp.where(column[None, :] < counts[:, None], picked + starts, BYTES)
    return (bounds.astype(jnp.int32), counts, offsets)


def draw_boundaries(key, part):
    layout = span_layout(key)
    return layout[0]


def draw_span_counts(key, part):
    layout = span_layout(key)
    return layout[1]


def draw_span_offsets(key, part):
    layout = span_layout(key)
    return layout[2]


def shard_levels(own_key, dims, cuts, least, top_value):
    def one(dim, blocks):
        steps = jax.random.uniform(jax.random.fold_in(jax.random.fold_in(own_key, 6), dim), (blocks,), jnp.float32, least / len(cuts), top_value / len(cuts))
        return jnp.repeat(jnp.exp(steps), dims[dim] // blocks).reshape((-1,) + (1,) * (len(dims) - dim - 1))

    loudness = one(*cuts[0])
    for cut in cuts[1:]:
        loudness = loudness * one(*cut)
    return loudness


def noise(own_key, dims, scale, reach, pieces=(), kind=jnp.bfloat16):
    level = shard_levels(own_key, dims, pieces, -0.22, 0.18) if pieces else 1.0
    result = jax.random.normal(own_key, dims, jnp.float32) * scale * level
    return jnp.minimum(jnp.maximum(result, -reach), reach).astype(kind)


def setup_inputs(seed: int = 0) -> dict:
    seeds = jax.random.split(jax.random.key(seed), 20)
    byte_stream = noise(seeds[0], (BYTES, D_INNER), 1.0, 6.0, ((0, 64), (1, 8)))
    gate_stream = noise(seeds[1], (BYTES, D_INNER), 1.0, 6.0, ((0, 64), (1, 8)))
    conv_weight = noise(seeds[2], (KCONV, D_INNER), KCONV ** -0.5, 3.0, ((1, 8),), jnp.float32)
    state_write = noise(seeds[3], (BYTES, NSTATE), 1.0, 6.0, ((0, 64),))
    state_read = noise(seeds[4], (BYTES, NSTATE), NSTATE ** -0.5, 0.5, ((0, 64),))
    step_size = draw_step_size(jax.random.fold_in(seeds[19], 71), 0)
    decay_coef = draw_decay_coef(jax.random.fold_in(seeds[19], 71), 0)
    skip_gain = jnp.clip(jnp.exp(math.log(2.0) - 1.3862944 * jax.random.uniform(seeds[7], (NH,), jnp.float32) ** shard_levels(seeds[7], (NH,), ((0, 8),), -0.2, 0.2)), 0.5, 2.0)
    norm_gain = jnp.clip(1.0 + 0.15 * jax.random.normal(seeds[8], (D_INNER,), jnp.float32), 0.25, 1.75)
    mixer_out = noise(seeds[9], (D_INNER, D_ENC), D_INNER ** -0.5, 0.125, ((0, 8),))
    residual = noise(seeds[10], (BYTES, D_ENC), 1.0, 6.0, ((0, 64),))
    boundaries = draw_boundaries(jax.random.fold_in(seeds[19], 71), 0)
    span_counts = draw_span_counts(jax.random.fold_in(seeds[19], 71), 0)
    span_offsets = draw_span_offsets(jax.random.fold_in(seeds[19], 71), 0)
    pad_vector = noise(seeds[14], (PAD,), 1.0, 6.0)
    main_gain = jnp.clip(1.0 + 0.15 * jax.random.normal(seeds[15], (D_MAIN,), jnp.float32), 0.25, 1.75)
    query_weight = draw_query_weight(jax.random.fold_in(seeds[19], 71), 0)
    key_value_weight = draw_key_value_weight(jax.random.fold_in(seeds[19], 71), 0)
    main_out_weight = noise(seeds[18], (QH * HD, D_ENC), (QH * HD) ** -0.5, 0.09375, ((0, 8),))
    return dict(byte_stream=byte_stream, gate_stream=gate_stream, conv_weight=conv_weight, state_write=state_write, state_read=state_read, step_size=step_size, decay_coef=decay_coef, skip_gain=skip_gain, norm_gain=norm_gain, mixer_out=mixer_out, residual=residual, boundaries=boundaries, span_counts=span_counts, span_offsets=span_offsets, pad_vector=pad_vector, main_gain=main_gain, query_weight=query_weight, key_value_weight=key_value_weight, main_out_weight=main_out_weight)


THETA = 500000.0
EPSILON = 1e-05
PRECISE = lax.Precision.HIGHEST

def convolve(inputs, conv_weight, front_rows):
    tap_count = conv_weight.shape[0]
    extended = jnp.concatenate([front_rows, inputs], axis=0).astype(jnp.float32)
    summed = jnp.zeros(inputs.shape, jnp.float32)
    for tap_index in range(tap_count):
        summed = summed + conv_weight[tap_index][None, :] * extended[tap_index:tap_index + inputs.shape[0]]
    return jax.nn.silu(summed).astype(jnp.bfloat16)

def scan_block(carried_state, x_block, write_block, read_block, log_decay, input_gain):
    block_size = x_block.shape[0]
    running = jnp.cumsum(log_decay, axis=0)
    affinity = jnp.dot(read_block, write_block.T, preferred_element_type=jnp.float32)
    causal = jnp.arange(block_size)[:, None] >= jnp.arange(block_size)[None, :]
    across = running.T
    spread = jnp.where(causal[None], across[:, :, None] - across[:, None, :], 0.0)
    mixing = jnp.where(causal[None], jnp.exp(spread), 0.0) * affinity[None] * input_gain.T[:, None, :]
    mixing = mixing.astype(jnp.bfloat16)
    within = jnp.einsum('hts,shp->thp', mixing.astype(jnp.float32), x_block.astype(jnp.float32))
    entering = jnp.einsum('tn,hpn->thp', read_block.astype(jnp.float32), carried_state, precision=PRECISE) * jnp.exp(running)[:, :, None]
    remaining = jnp.exp(running[-1][None, :] - running) * input_gain
    updated = jnp.exp(running[-1])[:, None, None] * carried_state + jnp.einsum('sh,shp,sn->hpn', remaining, x_block.astype(jnp.float32), write_block.astype(jnp.float32), precision=PRECISE)
    return (updated, within + entering)

def rotate(vectors, positions):
    half_size = vectors.shape[-1] // 2
    frequency = jnp.exp(jnp.arange(half_size, dtype=jnp.float32) * (-2.0 * math.log(THETA) / vectors.shape[-1]))
    angles = positions.astype(jnp.float32)[:, None] * frequency[None, :]
    cosine = jnp.cos(angles)[:, None, :]
    sine_part = jnp.sin(angles)[:, None, :]
    leading = vectors[..., :half_size]
    trailing = vectors[..., half_size:]
    return jnp.concatenate([leading * cosine - trailing * sine_part, trailing * cosine + leading * sine_part], axis=-1)

def reference(byte_stream, gate_stream, conv_weight, state_write, state_read, step_size, decay_coef, skip_gain, norm_gain, mixer_out, residual, boundaries, span_counts, span_offsets, pad_vector, main_gain, query_weight, key_value_weight, main_out_weight):
    front_rows = jnp.zeros((KCONV - 1, byte_stream.shape[1]), jnp.bfloat16)
    conv_out = convolve(byte_stream, conv_weight, front_rows)
    log_decay = -step_size * decay_coef[None, :]
    input_gain = jnp.sqrt(-jnp.expm1(2.0 * log_decay))
    block_size = min(L_DEV, 512)
    block_count = BYTES // block_size

    def advance(carried_state, items):
        return scan_block(carried_state, items[0], items[1], items[2], items[3], items[4])
    start_state = jnp.zeros((NH, HP, NSTATE), jnp.float32)
    items = (conv_out.reshape(block_count, block_size, NH, HP), state_write.reshape(block_count, block_size, NSTATE), state_read.reshape(block_count, block_size, NSTATE), log_decay.reshape(block_count, block_size, NH), input_gain.reshape(block_count, block_size, NH))
    final_state, mixed = lax.scan(advance, start_state, items)
    mixed = mixed.reshape(BYTES, NH, HP) + skip_gain[None, :, None] * conv_out.reshape(BYTES, NH, HP).astype(jnp.float32)
    gated = mixed.reshape(BYTES, NH * HP) * jax.nn.silu(gate_stream.astype(jnp.float32))
    shaped = gated.reshape(BYTES, NGROUP, NH * HP // NGROUP)
    scaled = shaped * lax.rsqrt(lax.optimization_barrier(jnp.mean(shaped * shaped, axis=-1, keepdims=True)) + EPSILON)
    normed = (scaled.reshape(BYTES, NH * HP) * norm_gain[None, :]).astype(jnp.bfloat16)
    encoded = (residual.astype(jnp.float32) + jnp.dot(normed, mixer_out, preferred_element_type=jnp.float32)).astype(jnp.bfloat16)
    slot_index = jnp.arange(CAP, dtype=jnp.int32)
    usable = slot_index[None, :] < span_counts[:, None]
    where_to = jnp.where(usable, span_offsets[:, None] + slot_index[None, :], SPANS).astype(jnp.int32)
    spots = jnp.zeros((SPANS,), jnp.int32).at[where_to.reshape(-1)].set(boundaries.reshape(-1), mode='drop')
    span_in = encoded[spots]
    lifted = jnp.concatenate([span_in.astype(jnp.float32), jnp.broadcast_to(pad_vector.astype(jnp.float32)[None, :], (SPANS, PAD))], axis=1)
    main_normed = (lifted * lax.rsqrt(lax.optimization_barrier(jnp.mean(lifted * lifted, axis=1, keepdims=True)) + EPSILON) * main_gain[None, :]).astype(jnp.bfloat16)
    query_vectors = jnp.dot(main_normed, query_weight, preferred_element_type=jnp.float32).reshape(SPANS, QH, HD)
    pairs = jnp.dot(main_normed, key_value_weight, preferred_element_type=jnp.float32).reshape(SPANS, KVH, 2, HD)
    span_place = jnp.arange(SPANS, dtype=jnp.int32)
    query_vectors = rotate(query_vectors, span_place).astype(jnp.bfloat16)
    keys = rotate(pairs[:, :, 0], span_place).astype(jnp.bfloat16)
    values = pairs[:, :, 1].astype(jnp.bfloat16)
    group_size = QH // KVH
    query_vectors = query_vectors.reshape(SPANS, KVH, group_size, HD)
    causal = span_place[:, None] >= span_place[None, :]

    def one_head(items):
        query_head, key_head, value_head = items
        scores = jnp.einsum('qgd,kd->gqk', query_head.astype(jnp.float32), key_head.astype(jnp.float32)) / math.sqrt(HD)
        highest = lax.optimization_barrier(jnp.max(jnp.where(causal[None], scores, -1e+30), axis=-1, keepdims=True))
        weights = jnp.where(causal[None], jnp.exp(scores - highest), 0.0)
        total = lax.optimization_barrier(jnp.sum(weights, axis=-1))
        weighted = jnp.einsum('gqk,kd->gqd', weights.astype(jnp.bfloat16).astype(jnp.float32), value_head.astype(jnp.float32))
        return (weighted / total[..., None]).astype(jnp.bfloat16)
    attended = lax.map(one_head, (query_vectors.transpose(1, 0, 2, 3), keys.transpose(1, 0, 2), values.transpose(1, 0, 2)))
    attended = attended.transpose(2, 0, 1, 3).reshape(SPANS, QH * HD)
    main = (span_in.astype(jnp.float32) + jnp.dot(attended, main_out_weight, preferred_element_type=jnp.float32)).astype(jnp.bfloat16)
    block_starts = (jnp.arange(N_SEQ, dtype=jnp.int32) * L_DEV)[:, None]
    local_place = boundaries - block_starts
    byte_place = jnp.arange(L_DEV, dtype=jnp.int32)
    before = lax.optimization_barrier(jnp.sum(((local_place[:, None, :] <= byte_place[None, :, None]) & usable[:, None, :]).astype(jnp.int32), axis=-1))
    which = (span_offsets[:, None] + before - 1).reshape(-1).astype(jnp.int32)
    return (encoded.astype(jnp.float32) + main[which].astype(jnp.float32)).astype(jnp.bfloat16)
```

```python
import functools
import math

import jax
import jax.numpy as jnp
from jax import lax
from jax.experimental import pallas as pl
from jax.experimental.pallas import tpu as pltpu
from jax.sharding import PartitionSpec as P

F32 = jnp.float32
BF16 = jnp.bfloat16
MESH = pl.DeviceIdType.MESH
EXACT = lax.Precision.HIGHEST

NY = 8
NZ = 8
NHD = 8
L = 128
HEADS = 4
HP = 64
CAP = 32
HD = 128
D_MAIN = 4096
THETA = 500000.0
EPSILON = 1e-05

(
    STATS_Z,
    STATS_Y,
    W_AZ,
    W_BY,
    W_AY,
    W_BZ,
    SCAN1,
    SCAN2,
    SCAN3,
    SPAN_RS,
    SPAN_AG,
    ENC_RS,
    K_Z,
    V_Y,
    K_Y,
    V_Z,
    MAIN_RS,
    N_EX,
) = range(18)


def nn(a, b, precision=None):
    return lax.dot_general(
        a, b, (((1,), (0,)), ((), ())), precision=precision, preferred_element_type=F32
    )


def nt(a, b, precision=None):
    return lax.dot_general(
        a, b, (((1,), (1,)), ((), ())), precision=precision, preferred_element_type=F32
    )


def tn(a, b, precision=None):
    return lax.dot_general(
        a, b, (((0,), (0,)), ((), ())), precision=precision, preferred_element_type=F32
    )


def iota(shape, dim):
    return lax.broadcasted_iota(jnp.int32, shape, dim)


def silu(v):
    return v / (1.0 + jnp.exp(-v))


def one_minus_exp(u):
    series = u * (
        1.0
        - u
        * (
            1.0 / 2
            - u * (1.0 / 6 - u * (1.0 / 24 - u * (1.0 / 120 - u * (1.0 / 720 - u / 5040))))
        )
    )
    return jnp.where(u < 0.3, series, 1.0 - jnp.exp(-u))


def kernel(
    x_hbm,
    gate_hbm,
    convw_ref,
    b_hbm,
    c_hbm,
    step_ref,
    decay_ref,
    skip_ref,
    ngain_ref,
    mo_hbm,
    res_hbm,
    bnd_ref,
    cnt_ref,
    off_ref,
    pad_ref,
    mgain_ref,
    wq_hbm,
    wkv_hbm,
    mw_hbm,
    out_ref,
    x_ref,
    gate_ref,
    b_ref,
    c_ref,
    mo_ref,
    res_ref,
    wq_ref,
    wkv_ref,
    mw_ref,
    halo,
    ext,
    stats_z,
    stats_y,
    wbuf,
    s1_send,
    s1,
    s2,
    s3_send,
    s3,
    sp_send,
    sp_recv,
    ag,
    en_send,
    en_recv,
    kbuf,
    vbuf,
    mn_send,
    mn_recv,
    local_sem,
    halo_sem,
    w0_send,
    w0_recv,
    send_sem,
    recv_sem,
):
    s = lax.axis_index("seq")
    hd = lax.axis_index("head")
    y = s // NZ
    z = s % NZ

    def at_z(p):
        return (y * NZ + p, hd)

    def at_y(p):
        return (p * NZ + z, hd)

    def at_h(p):
        return (s, p)

    nxt = (lax.rem(s + 1, NY * NZ), hd)
    prv = (lax.rem(s + NY * NZ - 1, NY * NZ), hd)

    barrier = pltpu.get_barrier_semaphore()
    for d in range(1, 8):
        for to in (at_z(lax.rem(z + d, NZ)), at_y(lax.rem(y + d, NY)), at_h(lax.rem(hd + d, NHD))):
            pl.semaphore_signal(barrier, inc=1, device_id=to, device_id_type=MESH)
    pl.semaphore_signal(barrier, inc=1, device_id=prv, device_id_type=MESH)

    loads = [
        (b_hbm, b_ref),
        (c_hbm, c_ref),
        (wq_hbm, wq_ref),
        (wkv_hbm, wkv_ref),
        (x_hbm, x_ref),
        (gate_hbm, gate_ref),
        (mo_hbm, mo_ref),
        (res_hbm.at[:, pl.ds(pl.multiple_of(hd * 128, 128), 128)], res_ref),
        (mw_hbm, mw_ref),
    ]
    load = [pltpu.make_async_copy(a, b, local_sem.at[i]) for i, (a, b) in enumerate(loads)]
    for copy in load:
        copy.start()
    l_b, l_c, l_wq, l_wkv, l_x, l_gate, l_mo, l_res, l_mw = load

    pending = []

    def send_all(ex, me, where, src, dst):
        for d in range(1, 8):
            p = lax.rem(me + d, 8)
            copy = pltpu.make_async_remote_copy(
                src_ref=src(p),
                dst_ref=dst,
                send_sem=send_sem.at[ex, d],
                recv_sem=recv_sem.at[ex, me],
                device_id=where(p),
                device_id_type=MESH,
            )
            copy.start()
            pending.append(copy)

    def recv_all(ex, me, where, slot):
        for d in range(1, 8):
            p = lax.rem(me + 8 - d, 8)
            pltpu.make_async_remote_copy(
                src_ref=slot(p),
                dst_ref=slot(p),
                send_sem=send_sem.at[ex, d],
                recv_sem=recv_sem.at[ex, p],
                device_id=where(p),
                device_id_type=MESH,
            ).wait_recv()

    row4 = iota((HEADS, L), 0)
    coef = jnp.zeros((HEADS, L), F32)
    for h in range(HEADS):
        coef = jnp.where(row4 == h, decay_ref[h], coef)
    rate = step_ref[...] * coef
    log_decay = -rate
    gain_row = jnp.sqrt(one_minus_exp(2.0 * rate))
    ti = iota((L, L), 0)
    si = iota((L, L), 1)
    causal = ti >= si
    tri = jnp.where(causal, 1.0, 0.0).astype(F32)
    run_row = nt(log_decay, tri, EXACT)
    run_col = [
        nt(tri, jnp.broadcast_to(log_decay[h : h + 1, :], (L, L)), EXACT) for h in range(HEADS)
    ]
    rem_row = jnp.exp(run_row[:, L - 1 : L] - run_row) * gain_row
    first = si < HP
    eye = jnp.where(ti == si, 1.0, 0.0).astype(BF16)
    top = ti < HP
    rem_x = [
        nt(
            eye,
            jnp.where(
                top,
                jnp.broadcast_to(rem_row[2 * i : 2 * i + 1, :], (L, L)),
                jnp.broadcast_to(rem_row[2 * i + 1 : 2 * i + 2, :], (L, L)),
            ).astype(BF16),
        )
        for i in range(2)
    ]
    run_x = jnp.concatenate(
        [jnp.where(first, run_col[2 * i], run_col[2 * i + 1]) for i in range(2)], axis=1
    )

    l_wq.wait()
    l_wkv.wait()
    prow = s // 2 - 8
    padf = pad_ref[...].astype(F32)
    mg = mgain_ref[...]
    pad_one = jnp.sum(jnp.where(iota((24, 128), 0) == prow, padf, 0.0), axis=0, keepdims=True)
    gain_one = jnp.sum(jnp.where(iota((32, 128), 0) == s // 2, mg, 0.0), axis=0, keepdims=True)
    both = pad_one * gain_one
    half = jnp.where(s % 2 == 1, both[:, 64:], both[:, :64])
    half = jnp.broadcast_to(half, (16, 64)).astype(BF16)
    pq = nn(half, wq_ref[...])
    pkv = nn(half, wkv_ref[...])
    pad_sq = jnp.sum(jnp.sum(padf * padf, axis=1, keepdims=True), axis=0, keepdims=True)
    lane1 = iota((1, 128), 1)
    count = cnt_ref[0].astype(F32)
    last = jnp.zeros((1, 128), F32)
    for h in range(HEADS):
        last = jnp.where(lane1 == h, run_col[h][L - 1 : L, :], last)
    rows = [
        pq[0:1, 0:128],
        pq[0:1, 128:256],
        pkv[0:1, 0:128],
        pq[0:1, 256:384],
        pq[0:1, 384:512],
        pkv[0:1, 128:256],
        jnp.where(lane1 == z, count, 0.0),
        last,
    ]
    for i, row in enumerate(rows):
        stats_z[z, i : i + 1, :] = row

    pl.semaphore_wait(barrier, 22)

    halo_copy = pltpu.make_async_remote_copy(
        src_ref=x_hbm.at[pl.ds(L - 16, 16), :],
        dst_ref=halo,
        send_sem=halo_sem.at[0],
        recv_sem=halo_sem.at[1],
        device_id=nxt,
        device_id_type=MESH,
    )
    halo_copy.start()
    send_all(STATS_Z, z, at_z, lambda p: stats_z.at[z], stats_z.at[z])

    def w0_parts(yp):
        rg = lax.rem(yp, 4)
        ch = yp // 4
        r = pl.ds(pl.multiple_of(16 * rg, 16), 16)
        return (
            (
                wq_hbm.at[r, pl.ds(pl.multiple_of(256 * ch, 256), 256)],
                wbuf.at[ch, y, z, rg, :, pl.ds(0, 256)],
            ),
            (
                wkv_hbm.at[r, pl.ds(pl.multiple_of(128 * ch, 128), 128)],
                wbuf.at[ch, y, z, rg, :, pl.ds(256, 128)],
            ),
        )

    def w0_copies():
        copies = []
        for d in range(1, 8):
            yp = lax.rem(y + d, NY)
            for i, (src, dst) in enumerate(w0_parts(yp)):
                copies.append(
                    pltpu.make_async_remote_copy(
                        src_ref=src,
                        dst_ref=dst,
                        send_sem=w0_send.at[i, d],
                        recv_sem=w0_recv.at[i, y],
                        device_id=at_y(yp),
                        device_id_type=MESH,
                    )
                )
        return copies

    @pl.when(y < 2)
    def _():
        for copy in w0_copies():
            copy.start()
        for i, (src, dst) in enumerate(w0_parts(y)):
            pltpu.make_async_copy(src, dst, w0_recv.at[i, y]).start()

    l_b.wait()
    l_c.wait()
    bm = b_ref[...]
    cm = c_ref[...]
    affinity = jnp.where(causal, nt(cm, bm), 0.0)
    mix = []
    for h in range(HEADS):
        spread = jnp.where(causal, run_col[h] - run_row[h : h + 1, :], 0.0)
        mix.append((jnp.exp(spread) * (affinity * gain_row[h : h + 1, :])).astype(BF16))

    l_x.wait()
    halo_copy.wait()
    ext[16:, :] = x_ref[...].astype(F32)
    ext[0:16, :] = jnp.where(s == 0, 0.0, halo[...].astype(F32))
    cw = convw_ref[...]
    summed = cw[0:1, :] * ext[13 : 13 + L, :]
    for k in range(1, 4):
        summed = summed + cw[k : k + 1, :] * ext[13 + k : 13 + k + L, :]
    conv = silu(summed).astype(BF16)
    conv_f = conv.astype(F32)

    weighted = (conv_f * jnp.concatenate(rem_x, axis=1)).astype(BF16)
    state = tn(bm, weighted).astype(BF16)
    s1_send[...] = state.reshape(8, 16, 256)
    send_all(SCAN1, z, at_z, lambda p: s1_send.at[p], s1.at[z])
    s1[z] = s1_send[z]

    recv_all(STATS_Z, z, at_z, lambda p: stats_z.at[p])
    tiles = stats_z[...]
    stats_y[y] = jnp.sum(tiles, axis=0)
    send_all(STATS_Y, y, at_y, lambda p: stats_y.at[y], stats_y.at[y])

    for b in range(2):
        for i, (src, dst) in enumerate(w0_parts(y)):
            rg = lax.rem(y, 4)
            ch = y // 4
            cols = pl.ds(0, 256) if i == 0 else pl.ds(256, 128)
            slot = wbuf.at[ch, b, z, rg, :, cols]
            pltpu.make_async_copy(slot, slot, w0_recv.at[i, b]).wait()
    rg_me = lax.rem(y, 4)
    ch_me = y // 4
    send_all(
        W_AZ, z, at_z, lambda p: wbuf.at[ch_me, 0, z, rg_me], wbuf.at[ch_me, 0, z, rg_me]
    )
    send_all(
        W_BY, y, at_y, lambda p: wbuf.at[ch_me, 1, z, rg_me], wbuf.at[ch_me, 1, z, rg_me]
    )

    within = []
    zero = jnp.zeros((), BF16)
    for i in range(2):
        pair = conv[:, 128 * i : 128 * (i + 1)]
        stacked = jnp.concatenate(
            [jnp.where(first, pair, zero), jnp.where(first, zero, pair)], axis=0
        )
        within.append(nn(jnp.concatenate([mix[2 * i], mix[2 * i + 1]], axis=1), stacked))
    skip = jnp.zeros((1, 256), F32)
    head_of = iota((1, 256), 1) // HP
    for h in range(HEADS):
        skip = jnp.where(head_of == h, skip_ref[h], skip)
    mixed_near = jnp.concatenate(within, axis=1) + skip * conv_f
    exp_run = jnp.exp(run_x)
    l_gate.wait()
    gate = silu(gate_ref[...].astype(F32))

    spread_head = jnp.where(iota((128, 256), 0) == iota((128, 256), 1) // HP, 1.0, 0.0)
    spread_head = spread_head.astype(F32)
    lz = nn(tiles[:, 7, :], spread_head, EXACT)
    recv_all(SCAN1, z, at_z, lambda p: s1.at[p])
    acc = jnp.zeros((16, 256), F32)
    cum = jnp.zeros((1, 256), F32)
    before, cums = [], []
    for j in range(NZ):
        before.append(acc)
        cums.append(cum)
        acc = jnp.exp(lz[j : j + 1, :]) * acc + s1[j].astype(F32)
        cum = cum + lz[j : j + 1, :]
    s2[y] = acc.astype(BF16)
    send_all(SCAN2, y, at_y, lambda p: s2.at[y], s2.at[y])

    recv_all(STATS_Y, y, at_y, lambda p: stats_y.at[p])
    ytiles = stats_y[...]
    pad_total = jnp.sum(ytiles, axis=0)
    ly = nn(ytiles[:, 7, :], spread_head, EXACT)

    recv_all(W_AZ, z, at_z, lambda p: wbuf.at[ch_me, 0, p, rg_me])
    send_all(W_AY, y, at_y, lambda p: wbuf.at[ch_me, 0, :, rg_me], wbuf.at[ch_me, 0, :, rg_me])
    recv_all(W_BY, y, at_y, lambda p: wbuf.at[p // 4, 1, z, lax.rem(p, 4)])
    send_all(W_BZ, z, at_z, lambda p: wbuf.at[:, 1, z], wbuf.at[:, 1, z])

    recv_all(SCAN2, y, at_y, lambda p: s2.at[p])
    rows_before = jnp.zeros((16, 256), F32)
    for j in range(NY - 1):
        longer = jnp.exp(ly[j : j + 1, :]) * rows_before + s2[j].astype(F32)
        rows_before = jnp.where(j < y, longer, rows_before)
    for j in range(NZ):
        s3_send[j] = (before[j] + jnp.exp(cums[j]) * rows_before).astype(BF16)
    send_all(SCAN3, z, at_z, lambda p: s3_send.at[p], s3.at[z])
    s3[z] = s3_send[z]

    bnd = bnd_ref[...] - s * L
    byte_at = iota((L, CAP), 0)
    slot_at = iota((L, CAP), 1)
    usable = slot_at < cnt_ref[0]
    picker = jnp.where((byte_at == bnd) & usable, 1.0, 0.0).astype(BF16)
    upto = jnp.where((bnd <= byte_at) & usable, 1.0, 0.0)
    newest = jnp.sum(upto, axis=1, keepdims=True) - 1.0
    spreader = jnp.where(slot_at.astype(F32) == newest, 1.0, 0.0).astype(BF16)
    l_res.wait()
    res = res_ref[...]
    res_span = tn(picker, res)

    lane = iota((CAP, 128), 1)
    place = (iota((CAP, 128), 0) + off_ref[0]).astype(F32)
    freq = jnp.exp(
        lax.rem(lane, HD // 2).astype(F32) * (-2.0 * math.log(THETA) / HD)
    )
    angle = place * freq
    cosine = jnp.cos(angle)
    sine = jnp.where(lane < HD // 2, -jnp.sin(angle), jnp.sin(angle))

    recv_all(SCAN3, z, at_z, lambda p: s3.at[p])
    entering = nn(cm, s3[...].reshape(128, 256)) * exp_run
    gated = (mixed_near + entering) * gate
    mean_sq = jnp.sum(gated * gated, axis=1, keepdims=True) * (1.0 / 256)
    normed = (gated * lax.rsqrt(mean_sq + EPSILON) * ngain_ref[...]).astype(BF16)
    l_mo.wait()
    picked = tn(picker, normed).astype(BF16)
    span_part = nn(picked, mo_ref[...]).astype(BF16)
    for j in range(NHD):
        sp_send[j] = span_part[:, 128 * j : 128 * (j + 1)]
    send_all(SPAN_RS, hd, at_h, lambda p: sp_send.at[p], sp_recv.at[hd])
    sp_recv[hd] = sp_send[hd]
    enc_part = nn(normed, mo_ref[...]).astype(BF16)
    for j in range(NHD):
        en_send[j] = enc_part[:, 128 * j : 128 * (j + 1)]
    en_recv[hd] = en_send[hd]

    recv_all(SPAN_RS, hd, at_h, lambda p: sp_recv.at[p])
    span_share = (res_span + jnp.sum(sp_recv[...].astype(F32), axis=0)).astype(BF16)
    ag[hd] = span_share
    send_all(SPAN_AG, hd, at_h, lambda p: ag.at[hd], ag.at[hd])

    expand = jnp.where(
        iota((128, 2048), 0) == lax.rem(iota((128, 2048), 1) // CAP, NZ), 1.0, 0.0
    ).astype(BF16)
    per_row = nn(ytiles[:, 6, :].astype(BF16), expand)
    key_lane = iota((8, 2048), 1)
    counts = jnp.sum(
        jnp.where(key_lane // (CAP * NZ) == iota((8, 2048), 0), per_row, 0.0),
        axis=0,
        keepdims=True,
    )
    key1 = iota((1, 2048), 1)
    key_owner = key1 // CAP
    key_slot = key1 - key_owner * CAP
    known = key_slot.astype(F32) < counts
    limit = jnp.where(key_owner < s, -1, jnp.where(key_owner == s, key_slot, CAP))
    limit = jnp.where(known, limit, CAP)

    recv_all(SPAN_AG, hd, at_h, lambda p: ag.at[p])
    send_all(ENC_RS, hd, at_h, lambda p: en_send.at[p], en_recv.at[hd])
    sq = jnp.zeros((CAP, 1), F32)
    pieces = []
    for j in range(NHD):
        piece = ag[j].astype(F32)
        sq = sq + jnp.sum(piece * piece, axis=1, keepdims=True)
        pieces.append((piece * mg[j : j + 1, :]).astype(BF16))
    scale = lax.rsqrt((sq + pad_sq) * (1.0 / D_MAIN) + EPSILON)
    span_x = jnp.concatenate(pieces, axis=1)
    recv_all(W_AY, y, at_y, lambda p: wbuf.at[p // 4, 0, :, lax.rem(p, 4)])
    recv_all(W_BZ, z, at_z, lambda p: wbuf.at[:, 1, p])
    proj = [nn(span_x, wbuf[ch].reshape(1024, 384)) for ch in range(2)]

    def column(i):
        part = proj[i // 3][:, 128 * (i % 3) : 128 * (i % 3 + 1)]
        return (part + pad_total[i : i + 1, :]) * scale

    def rotate(v):
        return (v * cosine + pltpu.roll(v, HD // 2, 1) * sine).astype(BF16)

    kbuf[y, z] = rotate(column(2))
    vbuf[y, z] = column(5).astype(BF16)
    send_all(K_Z, z, at_z, lambda p: kbuf.at[y, z], kbuf.at[y, z])
    send_all(V_Y, y, at_y, lambda p: vbuf.at[y, z], vbuf.at[y, z])
    queries = jnp.concatenate([rotate(column(i)) for i in (0, 1, 3, 4)], axis=0)

    recv_all(K_Z, z, at_z, lambda p: kbuf.at[y, p])
    send_all(K_Y, y, at_y, lambda p: kbuf.at[y], kbuf.at[y])
    recv_all(V_Y, y, at_y, lambda p: vbuf.at[p, z])
    send_all(V_Z, z, at_z, lambda p: vbuf.at[:, z], vbuf.at[:, z])

    recv_all(ENC_RS, hd, at_h, lambda p: en_recv.at[p])
    encoded = (res.astype(F32) + jnp.sum(en_recv[...].astype(F32), axis=0)).astype(BF16)

    recv_all(K_Y, y, at_y, lambda p: kbuf.at[p])
    scores = nt(queries, kbuf[...].reshape(2048, HD)) * (1.0 / math.sqrt(HD))
    allowed = limit <= lax.rem(iota((128, 2048), 0), CAP)
    scores = jnp.where(allowed, scores, -1e30)
    highest = jnp.max(scores, axis=1, keepdims=True)
    weights = jnp.exp(scores - highest)
    total = jnp.sum(weights, axis=1, keepdims=True)
    recv_all(V_Z, z, at_z, lambda p: vbuf.at[:, p])
    attended = (nn(weights.astype(BF16), vbuf[...].reshape(2048, HD)) / total).astype(BF16)
    l_mw.wait()
    att = jnp.concatenate([attended[CAP * i : CAP * (i + 1), :] for i in range(4)], axis=1)
    main_part = nn(att, mw_ref[...]).astype(BF16)
    for j in range(NHD):
        mn_send[j] = main_part[:, 128 * j : 128 * (j + 1)]
    send_all(MAIN_RS, hd, at_h, lambda p: mn_send.at[p], mn_recv.at[hd])
    mn_recv[hd] = mn_send[hd]
    recv_all(MAIN_RS, hd, at_h, lambda p: mn_recv.at[p])
    main_rows = (span_share.astype(F32) + jnp.sum(mn_recv[...].astype(F32), axis=0)).astype(BF16)
    out_ref[...] = (encoded.astype(F32) + nn(spreader, main_rows)).astype(BF16)

    for copy in pending:
        copy.wait_send()

    @pl.when(y < 2)
    def _():
        for copy in w0_copies():
            copy.wait_send()


def shards(
    byte_stream,
    gate_stream,
    conv_weight,
    state_write,
    state_read,
    step_size,
    decay_coef,
    skip_gain,
    norm_gain,
    mixer_out,
    residual,
    boundaries,
    span_counts,
    span_offsets,
    pad_vector,
    main_gain,
    query_weight,
    key_value_weight,
    main_out_weight,
):
    far = pl.BlockSpec(memory_space=pl.ANY)
    near = pl.BlockSpec(memory_space=pltpu.VMEM)
    scalar = pl.BlockSpec(memory_space=pltpu.SMEM)
    vm = pltpu.VMEM
    dma = pltpu.SemaphoreType.DMA
    return pl.pallas_call(
        kernel,
        out_shape=jax.ShapeDtypeStruct((L, 128), BF16),
        in_specs=[
            far,
            far,
            near,
            far,
            far,
            near,
            scalar,
            scalar,
            near,
            far,
            far,
            near,
            scalar,
            scalar,
            near,
            near,
            far,
            far,
            far,
        ],
        out_specs=near,
        scratch_shapes=[
            vm((L, 256), BF16),
            vm((L, 256), BF16),
            vm((L, 128), BF16),
            vm((L, 128), BF16),
            vm((256, 1024), BF16),
            vm((L, 128), BF16),
            vm((64, 512), BF16),
            vm((64, 256), BF16),
            vm((512, 1024), BF16),
            vm((16, 256), BF16),
            vm((L + 16, 256), F32),
            vm((8, 8, 128), F32),
            vm((8, 8, 128), F32),
            vm((2, 2, 8, 4, 16, 384), BF16),
            vm((8, 16, 256), BF16),
            vm((8, 16, 256), BF16),
            vm((8, 16, 256), BF16),
            vm((8, 16, 256), BF16),
            vm((8, 16, 256), BF16),
            vm((8, CAP, 128), BF16),
            vm((8, CAP, 128), BF16),
            vm((8, CAP, 128), BF16),
            vm((8, L, 128), BF16),
            vm((8, L, 128), BF16),
            vm((8, 8, CAP, 128), BF16),
            vm((8, 8, CAP, 128), BF16),
            vm((8, CAP, 128), BF16),
            vm((8, CAP, 128), BF16),
            dma((9,)),
            dma((2,)),
            dma((2, 8)),
            dma((2, 2)),
            dma((N_EX, 8)),
            dma((N_EX, 8)),
        ],
        compiler_params=pltpu.CompilerParams(
            collective_id=0, has_side_effects=True, vmem_limit_bytes=40 * 1024 * 1024
        ),
        cost_estimate=pl.CostEstimate(flops=10**9, bytes_accessed=4 * 10**6, transcendentals=10**6),
    )(
        byte_stream,
        gate_stream,
        conv_weight,
        state_write,
        state_read,
        step_size.T,
        decay_coef,
        skip_gain,
        norm_gain.reshape(1, 256),
        mixer_out,
        residual,
        boundaries,
        span_counts,
        span_offsets,
        pad_vector.reshape(24, 128),
        main_gain.reshape(32, 128),
        query_weight,
        key_value_weight,
        main_out_weight,
    )


def solution(mesh):
    in_specs = (
        P("seq", "head"),
        P("seq", "head"),
        P(None, "head"),
        P("seq", None),
        P("seq", None),
        P("seq", "head"),
        P("head"),
        P("head"),
        P("head"),
        P("head", None),
        P("seq", None),
        P("seq", None),
        P("seq"),
        P("seq"),
        P(),
        P(),
        P("seq", "head"),
        P("seq", "head"),
        P("head", None),
    )
    out_specs = P("seq", "head")
    return jax.shard_map(shards, mesh=mesh, in_specs=in_specs, out_specs=out_specs, check_vma=False)
```

```python
import functools
import math

import jax
import jax.numpy as jnp
from jax import lax
from jax.experimental import pallas as pl
from jax.experimental.pallas import tpu as pltpu
from jax.sharding import PartitionSpec as P

F32 = jnp.float32
BF16 = jnp.bfloat16
MESH = pl.DeviceIdType.MESH
EXACT = lax.Precision.HIGHEST

NY = 8
NZ = 8
NHD = 8
L = 128
HEADS = 4
HP = 64
CAP = 32
HD = 128
D_MAIN = 4096
THETA = 500000.0
EPSILON = 1e-05

(
    STATS_Z,
    STATS_Y,
    W_AZ,
    W_BY,
    W_AY,
    W_BZ,
    SCAN1,
    SCAN2,
    SCAN3,
    SPAN_RS,
    SPAN_AG,
    ENC_RS,
    K_Z,
    V_Y,
    K_Y,
    V_Z,
    MAIN_RS,
    N_EX,
) = range(18)


def nn(a, b, precision=None):
    return lax.dot_general(
        a, b, (((1,), (0,)), ((), ())), precision=precision, preferred_element_type=F32
    )


def nt(a, b, precision=None):
    return lax.dot_general(
        a, b, (((1,), (1,)), ((), ())), precision=precision, preferred_element_type=F32
    )


def tn(a, b, precision=None):
    return lax.dot_general(
        a, b, (((0,), (0,)), ((), ())), precision=precision, preferred_element_type=F32
    )


def iota(shape, dim):
    return lax.broadcasted_iota(jnp.int32, shape, dim)


def silu(v):
    return v / (1.0 + jnp.exp(-v))


def one_minus_exp(u):
    series = u * (
        1.0
        - u
        * (
            1.0 / 2
            - u * (1.0 / 6 - u * (1.0 / 24 - u * (1.0 / 120 - u * (1.0 / 720 - u / 5040))))
        )
    )
    return jnp.where(u < 0.3, series, 1.0 - jnp.exp(-u))


def kernel(
    x_hbm,
    gate_hbm,
    convw_ref,
    b_hbm,
    c_hbm,
    step_ref,
    decay_ref,
    skip_ref,
    ngain_ref,
    mo_hbm,
    res_hbm,
    bnd_ref,
    cnt_ref,
    off_ref,
    pad_ref,
    mgain_ref,
    wq_hbm,
    wkv_hbm,
    mw_hbm,
    out_ref,
    x_ref,
    gate_ref,
    b_ref,
    c_ref,
    mo_ref,
    res_ref,
    wq_ref,
    wkv_ref,
    mw_ref,
    halo,
    ext,
    stats_z,
    stats_y,
    wbuf,
    s1_send,
    s1,
    s2,
    s3_send,
    s3,
    sp_send,
    sp_recv,
    ag,
    en_send,
    en_recv,
    kbuf,
    vbuf,
    mn_send,
    mn_recv,
    local_sem,
    halo_sem,
    w0_send,
    w0_recv,
    send_sem,
    recv_sem,
):
    s = lax.axis_index("seq")
    hd = lax.axis_index("head")
    y = s // NZ
    z = s % NZ

    def at_z(p):
        return (y * NZ + p, hd)

    def at_y(p):
        return (p * NZ + z, hd)

    def at_h(p):
        return (s, p)

    nxt = (lax.rem(s + 1, NY * NZ), hd)
    prv = (lax.rem(s + NY * NZ - 1, NY * NZ), hd)

    barrier = pltpu.get_barrier_semaphore()
    for d in range(1, 8):
        for to in (at_z(lax.rem(z + d, NZ)), at_y(lax.rem(y + d, NY)), at_h(lax.rem(hd + d, NHD))):
            pl.semaphore_signal(barrier, inc=1, device_id=to, device_id_type=MESH)
    pl.semaphore_signal(barrier, inc=1, device_id=prv, device_id_type=MESH)

    loads = [
        (b_hbm, b_ref),
        (c_hbm, c_ref),
        (wq_hbm, wq_ref),
        (wkv_hbm, wkv_ref),
        (x_hbm, x_ref),
        (gate_hbm, gate_ref),
        (mo_hbm, mo_ref),
        (res_hbm.at[:, pl.ds(pl.multiple_of(hd * 128, 128), 128)], res_ref),
        (mw_hbm, mw_ref),
    ]
    load = [pltpu.make_async_copy(a, b, local_sem.at[i]) for i, (a, b) in enumerate(loads)]
    for copy in load:
        copy.start()
    l_b, l_c, l_wq, l_wkv, l_x, l_gate, l_mo, l_res, l_mw = load

    pending = []

    def send_all(ex, me, where, src, dst):
        for d in range(1, 8):
            p = lax.rem(me + d, 8)
            copy = pltpu.make_async_remote_copy(
                src_ref=src(p),
                dst_ref=dst,
                send_sem=send_sem.at[ex, d],
                recv_sem=recv_sem.at[ex, me],
                device_id=where(p),
                device_id_type=MESH,
            )
            copy.start()
            pending.append(copy)

    def recv_all(ex, me, where, slot):
        for d in range(1, 8):
            p = lax.rem(me + 8 - d, 8)
            pltpu.make_async_remote_copy(
                src_ref=slot(p),
                dst_ref=slot(p),
                send_sem=send_sem.at[ex, d],
                recv_sem=recv_sem.at[ex, p],
                device_id=where(p),
                device_id_type=MESH,
            ).wait_recv()

    row4 = iota((HEADS, L), 0)
    coef = jnp.zeros((HEADS, L), F32)
    for h in range(HEADS):
        coef = jnp.where(row4 == h, decay_ref[h], coef)
    rate = step_ref[...] * coef
    log_decay = -rate
    gain_row = jnp.sqrt(one_minus_exp(2.0 * rate))
    ti = iota((L, L), 0)
    si = iota((L, L), 1)
    causal = ti >= si
    tri = jnp.where(causal, 1.0, 0.0).astype(F32)
    run_row = nt(log_decay, tri, EXACT)
    run_col = [
        nt(tri, jnp.broadcast_to(log_decay[h : h + 1, :], (L, L)), EXACT) for h in range(HEADS)
    ]
    rem_row = jnp.exp(run_row[:, L - 1 : L] - run_row) * gain_row
    first = si < HP
    eye = jnp.where(ti == si, 1.0, 0.0).astype(BF16)
    top = ti < HP
    rem_x = [
        nt(
            eye,
            jnp.where(
                top,
                jnp.broadcast_to(rem_row[2 * i : 2 * i + 1, :], (L, L)),
                jnp.broadcast_to(rem_row[2 * i + 1 : 2 * i + 2, :], (L, L)),
            ).astype(BF16),
        )
        for i in range(2)
    ]
    run_x = jnp.concatenate(
        [jnp.where(first, run_col[2 * i], run_col[2 * i + 1]) for i in range(2)], axis=1
    )

    l_wq.wait()
    l_wkv.wait()
    prow = s // 2 - 8
    padf = pad_ref[...].astype(F32)
    mg = mgain_ref[...]
    pad_one = jnp.sum(jnp.where(iota((24, 128), 0) == prow, padf, 0.0), axis=0, keepdims=True)
    gain_one = jnp.sum(jnp.where(iota((32, 128), 0) == s // 2, mg, 0.0), axis=0, keepdims=True)
    both = pad_one * gain_one
    half = jnp.where(s % 2 == 1, both[:, 64:], both[:, :64])
    half = jnp.broadcast_to(half, (16, 64)).astype(BF16)
    pq = nn(half, wq_ref[...])
    pkv = nn(half, wkv_ref[...])
    pad_sq = jnp.sum(jnp.sum(padf * padf, axis=1, keepdims=True), axis=0, keepdims=True)
    lane1 = iota((1, 128), 1)
    count = cnt_ref[0].astype(F32)
    last = jnp.zeros((1, 128), F32)
    for h in range(HEADS):
        last = jnp.where(lane1 == h, run_col[h][L - 1 : L, :], last)
    rows = [
        pq[0:1, 0:128],
        pq[0:1, 128:256],
        pkv[0:1, 0:128],
        pq[0:1, 256:384],
        pq[0:1, 384:512],
        pkv[0:1, 128:256],
        jnp.where(lane1 == z, count, 0.0),
        last,
    ]
    for i, row in enumerate(rows):
        stats_z[z, i : i + 1, :] = row

    pl.semaphore_wait(barrier, 22)

    halo_copy = pltpu.make_async_remote_copy(
        src_ref=x_hbm.at[pl.ds(L - 16, 16), :],
        dst_ref=halo,
        send_sem=halo_sem.at[0],
        recv_sem=halo_sem.at[1],
        device_id=nxt,
        device_id_type=MESH,
    )
    halo_copy.start()
    send_all(STATS_Z, z, at_z, lambda p: stats_z.at[z], stats_z.at[z])

    def w0_parts(yp):
        rg = lax.rem(yp, 4)
        ch = yp // 4
        r = pl.ds(pl.multiple_of(16 * rg, 16), 16)
        return (
            (
                wq_hbm.at[r, pl.ds(pl.multiple_of(256 * ch, 256), 256)],
                wbuf.at[ch, y, z, rg, :, pl.ds(0, 256)],
            ),
            (
                wkv_hbm.at[r, pl.ds(pl.multiple_of(128 * ch, 128), 128)],
                wbuf.at[ch, y, z, rg, :, pl.ds(256, 128)],
            ),
        )

    def w0_copies():
        copies = []
        for d in range(1, 8):
            yp = lax.rem(y + d, NY)
            for i, (src, dst) in enumerate(w0_parts(yp)):
                copies.append(
                    pltpu.make_async_remote_copy(
                        src_ref=src,
                        dst_ref=dst,
                        send_sem=w0_send.at[i, d],
                        recv_sem=w0_recv.at[i, y],
                        device_id=at_y(yp),
                        device_id_type=MESH,
                    )
                )
        return copies

    @pl.when(y < 2)
    def _():
        for copy in w0_copies():
            copy.start()
        for i, (src, dst) in enumerate(w0_parts(y)):
            pltpu.make_async_copy(src, dst, w0_recv.at[i, y]).start()

    l_b.wait()
    l_c.wait()
    bm = b_ref[...]
    cm = c_ref[...]
    affinity = jnp.where(causal, nt(cm, bm), 0.0)
    mix = []
    for h in range(HEADS):
        spread = jnp.where(causal, run_col[h] - run_row[h : h + 1, :], 0.0)
        mix.append((jnp.exp(spread) * (affinity * gain_row[h : h + 1, :])).astype(BF16))

    l_x.wait()
    halo_copy.wait()
    ext[16:, :] = x_ref[...].astype(F32)
    ext[0:16, :] = jnp.where(s == 0, 0.0, halo[...].astype(F32))
    cw = convw_ref[...]
    summed = cw[0:1, :] * ext[13 : 13 + L, :]
    for k in range(1, 4):
        summed = summed + cw[k : k + 1, :] * ext[13 + k : 13 + k + L, :]
    conv = silu(summed).astype(BF16)
    conv_f = conv.astype(F32)

    weighted = (conv_f * jnp.concatenate(rem_x, axis=1)).astype(BF16)
    state = tn(bm, weighted).astype(BF16)
    s1_send[...] = state.reshape(8, 16, 256)
    send_all(SCAN1, z, at_z, lambda p: s1_send.at[p], s1.at[z])
    s1[z] = s1_send[z]

    recv_all(STATS_Z, z, at_z, lambda p: stats_z.at[p])
    tiles = stats_z[...]
    stats_y[y] = jnp.sum(tiles, axis=0)
    send_all(STATS_Y, y, at_y, lambda p: stats_y.at[y], stats_y.at[y])

    for b in range(2):
        for i, (src, dst) in enumerate(w0_parts(y)):
            rg = lax.rem(y, 4)
            ch = y // 4
            cols = pl.ds(0, 256) if i == 0 else pl.ds(256, 128)
            slot = wbuf.at[ch, b, z, rg, :, cols]
            pltpu.make_async_copy(slot, slot, w0_recv.at[i, b]).wait()
    rg_me = lax.rem(y, 4)
    ch_me = y // 4
    send_all(
        W_AZ, z, at_z, lambda p: wbuf.at[ch_me, 0, z, rg_me], wbuf.at[ch_me, 0, z, rg_me]
    )
    send_all(
        W_BY, y, at_y, lambda p: wbuf.at[ch_me, 1, z, rg_me], wbuf.at[ch_me, 1, z, rg_me]
    )

    within = []
    zero = jnp.zeros((), BF16)
    for i in range(2):
        pair = conv[:, 128 * i : 128 * (i + 1)]
        stacked = jnp.concatenate(
            [jnp.where(first, pair, zero), jnp.where(first, zero, pair)], axis=0
        )
        within.append(nn(jnp.concatenate([mix[2 * i], mix[2 * i + 1]], axis=1), stacked))
    skip = jnp.zeros((1, 256), F32)
    head_of = iota((1, 256), 1) // HP
    for h in range(HEADS):
        skip = jnp.where(head_of == h, skip_ref[h], skip)
    mixed_near = jnp.concatenate(within, axis=1) + skip * conv_f
    exp_run = jnp.exp(run_x)
    l_gate.wait()
    gate = silu(gate_ref[...].astype(F32))

    spread_head = jnp.where(iota((128, 256), 0) == iota((128, 256), 1) // HP, 1.0, 0.0)
    spread_head = spread_head.astype(F32)
    lz = nn(tiles[:, 7, :], spread_head, EXACT)
    recv_all(SCAN1, z, at_z, lambda p: s1.at[p])
    acc = jnp.zeros((16, 256), F32)
    cum = jnp.zeros((1, 256), F32)
    before, cums = [], []
    for j in range(NZ):
        before.append(acc)
        cums.append(cum)
        acc = jnp.exp(lz[j : j + 1, :]) * acc + s1[j].astype(F32)
        cum = cum + lz[j : j + 1, :]
    s2[y] = acc.astype(BF16)
    send_all(SCAN2, y, at_y, lambda p: s2.at[y], s2.at[y])

    recv_all(STATS_Y, y, at_y, lambda p: stats_y.at[p])
    ytiles = stats_y[...]
    pad_total = jnp.sum(ytiles, axis=0)
    ly = nn(ytiles[:, 7, :], spread_head, EXACT)

    recv_all(W_AZ, z, at_z, lambda p: wbuf.at[ch_me, 0, p, rg_me])
    send_all(W_AY, y, at_y, lambda p: wbuf.at[ch_me, 0, :, rg_me], wbuf.at[ch_me, 0, :, rg_me])
    recv_all(W_BY, y, at_y, lambda p: wbuf.at[p // 4, 1, z, lax.rem(p, 4)])
    send_all(W_BZ, z, at_z, lambda p: wbuf.at[:, 1, z], wbuf.at[:, 1, z])

    recv_all(SCAN2, y, at_y, lambda p: s2.at[p])
    rows_before = jnp.zeros((16, 256), F32)
    for j in range(NY - 1):
        longer = jnp.exp(ly[j : j + 1, :]) * rows_before + s2[j].astype(F32)
        rows_before = jnp.where(j < y, longer, rows_before)
    for j in range(NZ):
        s3_send[j] = (before[j] + jnp.exp(cums[j]) * rows_before).astype(BF16)
    send_all(SCAN3, z, at_z, lambda p: s3_send.at[p], s3.at[z])
    s3[z] = s3_send[z]

    bnd = bnd_ref[...] - s * L
    byte_at = iota((L, CAP), 0)
    slot_at = iota((L, CAP), 1)
    usable = slot_at < cnt_ref[0]
    picker = jnp.where((byte_at == bnd) & usable, 1.0, 0.0).astype(BF16)
    upto = jnp.where((bnd <= byte_at) & usable, 1.0, 0.0)
    newest = jnp.sum(upto, axis=1, keepdims=True) - 1.0
    spreader = jnp.where(slot_at.astype(F32) == newest, 1.0, 0.0).astype(BF16)
    l_res.wait()
    res = res_ref[...]
    res_span = tn(picker, res)

    lane = iota((CAP, 128), 1)
    place = (iota((CAP, 128), 0) + off_ref[0]).astype(F32)
    freq = jnp.exp(
        lax.rem(lane, HD // 2).astype(F32) * (-2.0 * math.log(THETA) / HD)
    )
    angle = place * freq
    cosine = jnp.cos(angle)
    sine = jnp.where(lane < HD // 2, -jnp.sin(angle), jnp.sin(angle))

    recv_all(SCAN3, z, at_z, lambda p: s3.at[p])
    entering = nn(cm, s3[...].reshape(128, 256)) * exp_run
    gated = (mixed_near + entering) * gate
    mean_sq = jnp.sum(gated * gated, axis=1, keepdims=True) * (1.0 / 256)
    normed = (gated * lax.rsqrt(mean_sq + EPSILON) * ngain_ref[...]).astype(BF16)
    l_mo.wait()
    picked = tn(picker, normed).astype(BF16)
    span_part = nn(picked, mo_ref[...]).astype(BF16)
    for j in range(NHD):
        sp_send[j] = span_part[:, 128 * j : 128 * (j + 1)]
    send_all(SPAN_RS, hd, at_h, lambda p: sp_send.at[p], sp_recv.at[hd])
    sp_recv[hd] = sp_send[hd]
    enc_part = nn(normed, mo_ref[...]).astype(BF16)
    for j in range(NHD):
        en_send[j] = enc_part[:, 128 * j : 128 * (j + 1)]
    en_recv[hd] = en_send[hd]

    recv_all(SPAN_RS, hd, at_h, lambda p: sp_recv.at[p])
    span_share = (res_span + jnp.sum(sp_recv[...].astype(F32), axis=0)).astype(BF16)
    ag[hd] = span_share
    send_all(SPAN_AG, hd, at_h, lambda p: ag.at[hd], ag.at[hd])

    expand = jnp.where(
        iota((128, 2048), 0) == lax.rem(iota((128, 2048), 1) // CAP, NZ), 1.0, 0.0
    ).astype(BF16)
    per_row = nn(ytiles[:, 6, :].astype(BF16), expand)
    key_lane = iota((8, 2048), 1)
    counts = jnp.sum(
        jnp.where(key_lane // (CAP * NZ) == iota((8, 2048), 0), per_row, 0.0),
        axis=0,
        keepdims=True,
    )
    key1 = iota((1, 2048), 1)
    key_owner = key1 // CAP
    key_slot = key1 - key_owner * CAP
    known = key_slot.astype(F32) < counts
    limit = jnp.where(key_owner < s, -1, jnp.where(key_owner == s, key_slot, CAP))
    limit = jnp.where(known, limit, CAP)

    recv_all(SPAN_AG, hd, at_h, lambda p: ag.at[p])
    send_all(ENC_RS, hd, at_h, lambda p: en_send.at[p], en_recv.at[hd])
    sq = jnp.zeros((CAP, 1), F32)
    pieces = []
    for j in range(NHD):
        piece = ag[j].astype(F32)
        sq = sq + jnp.sum(piece * piece, axis=1, keepdims=True)
        pieces.append((piece * mg[j : j + 1, :]).astype(BF16))
    scale = lax.rsqrt((sq + pad_sq) * (1.0 / D_MAIN) + EPSILON)
    span_x = jnp.concatenate(pieces, axis=1)
    recv_all(W_AY, y, at_y, lambda p: wbuf.at[p // 4, 0, :, lax.rem(p, 4)])
    recv_all(W_BZ, z, at_z, lambda p: wbuf.at[:, 1, p])
    proj = [nn(span_x, wbuf[ch].reshape(1024, 384)) for ch in range(2)]

    def column(i):
        part = proj[i // 3][:, 128 * (i % 3) : 128 * (i % 3 + 1)]
        return (part + pad_total[i : i + 1, :]) * scale

    def rotate(v):
        return (v * cosine + pltpu.roll(v, HD // 2, 1) * sine).astype(BF16)

    kbuf[y, z] = rotate(column(2))
    vbuf[y, z] = column(5).astype(BF16)
    send_all(K_Z, z, at_z, lambda p: kbuf.at[y, z], kbuf.at[y, z])
    send_all(V_Y, y, at_y, lambda p: vbuf.at[y, z], vbuf.at[y, z])
    queries = jnp.concatenate([rotate(column(i)) for i in (0, 1, 3, 4)], axis=0)

    recv_all(K_Z, z, at_z, lambda p: kbuf.at[y, p])
    send_all(K_Y, y, at_y, lambda p: kbuf.at[y], kbuf.at[y])
    recv_all(V_Y, y, at_y, lambda p: vbuf.at[p, z])
    send_all(V_Z, z, at_z, lambda p: vbuf.at[:, z], vbuf.at[:, z])

    recv_all(ENC_RS, hd, at_h, lambda p: en_recv.at[p])
    encoded = (res.astype(F32) + jnp.sum(en_recv[...].astype(F32), axis=0)).astype(BF16)

    recv_all(K_Y, y, at_y, lambda p: kbuf.at[p])
    scores = nt(queries, kbuf[...].reshape(2048, HD)) * (1.0 / math.sqrt(HD))
    allowed = limit <= lax.rem(iota((128, 2048), 0), CAP)
    scores = jnp.where(allowed, scores, -1e30)
    highest = jnp.max(scores, axis=1, keepdims=True)
    weights = jnp.exp(scores - highest)
    total = jnp.sum(weights, axis=1, keepdims=True)
    recv_all(V_Z, z, at_z, lambda p: vbuf.at[:, p])
    attended = (nn(weights.astype(BF16), vbuf[...].reshape(2048, HD)) / total).astype(BF16)
    l_mw.wait()
    att = jnp.concatenate([attended[CAP * i : CAP * (i + 1), :] for i in range(4)], axis=1)
    main_part = nn(att, mw_ref[...]).astype(BF16)
    for j in range(NHD):
        mn_send[j] = main_part[:, 128 * j : 128 * (j + 1)]
    send_all(MAIN_RS, hd, at_h, lambda p: mn_send.at[p], mn_recv.at[hd])
    mn_recv[hd] = mn_send[hd]
    recv_all(MAIN_RS, hd, at_h, lambda p: mn_recv.at[p])
    main_rows = (span_share.astype(F32) + jnp.sum(mn_recv[...].astype(F32), axis=0)).astype(BF16)
    out_ref[...] = (encoded.astype(F32) + nn(spreader, main_rows)).astype(BF16)

    for copy in pending:
        copy.wait_send()

    @pl.when(y < 2)
    def _():
        for copy in w0_copies():
            copy.wait_send()


def shards(
    byte_stream,
    gate_stream,
    conv_weight,
    state_write,
    state_read,
    step_size,
    decay_coef,
    skip_gain,
    norm_gain,
    mixer_out,
    residual,
    boundaries,
    span_counts,
    span_offsets,
    pad_vector,
    main_gain,
    query_weight,
    key_value_weight,
    main_out_weight,
):
    far = pl.BlockSpec(memory_space=pl.ANY)
    near = pl.BlockSpec(memory_space=pltpu.VMEM)
    scalar = pl.BlockSpec(memory_space=pltpu.SMEM)
    vm = pltpu.VMEM
    dma = pltpu.SemaphoreType.DMA
    return pl.pallas_call(
        kernel,
        out_shape=jax.ShapeDtypeStruct((L, 128), BF16),
        in_specs=[
            far,
            far,
            near,
            far,
            far,
            near,
            scalar,
            scalar,
            near,
            far,
            far,
            near,
            scalar,
            scalar,
            near,
            near,
            far,
            far,
            far,
        ],
        out_specs=near,
        scratch_shapes=[
            vm((L, 256), BF16),
            vm((L, 256), BF16),
            vm((L, 128), BF16),
            vm((L, 128), BF16),
            vm((256, 1024), BF16),
            vm((L, 128), BF16),
            vm((64, 512), BF16),
            vm((64, 256), BF16),
            vm((512, 1024), BF16),
            vm((16, 256), BF16),
            vm((L + 16, 256), F32),
            vm((8, 8, 128), F32),
            vm((8, 8, 128), F32),
            vm((2, 2, 8, 4, 16, 384), BF16),
            vm((8, 16, 256), BF16),
            vm((8, 16, 256), BF16),
            vm((8, 16, 256), BF16),
            vm((8, 16, 256), BF16),
            vm((8, 16, 256), BF16),
            vm((8, CAP, 128), BF16),
            vm((8, CAP, 128), BF16),
            vm((8, CAP, 128), BF16),
            vm((8, L, 128), BF16),
            vm((8, L, 128), BF16),
            vm((8, 8, CAP, 128), BF16),
            vm((8, 8, CAP, 128), BF16),
            vm((8, CAP, 128), BF16),
            vm((8, CAP, 128), BF16),
            dma((9,)),
            dma((2,)),
            dma((2, 8)),
            dma((2, 2)),
            dma((N_EX, 8)),
            dma((N_EX, 8)),
        ],
        compiler_params=pltpu.CompilerParams(
            collective_id=0, has_side_effects=True, vmem_limit_bytes=56 * 1024 * 1024
        ),
        cost_estimate=pl.CostEstimate(flops=10**9, bytes_accessed=4 * 10**6, transcendentals=10**6),
    )(
        byte_stream,
        gate_stream,
        conv_weight,
        state_write,
        state_read,
        step_size.T,
        decay_coef,
        skip_gain,
        norm_gain.reshape(1, 256),
        mixer_out,
        residual,
        boundaries,
        span_counts,
        span_offsets,
        pad_vector.reshape(24, 128),
        main_gain.reshape(32, 128),
        query_weight,
        key_value_weight,
        main_out_weight,
    )


def solution(mesh):
    in_specs = (
        P("seq", "head"),
        P("seq", "head"),
        P(None, "head"),
        P("seq", None),
        P("seq", None),
        P("seq", "head"),
        P("head"),
        P("head"),
        P("head"),
        P("head", None),
        P("seq", None),
        P("seq", None),
        P("seq"),
        P("seq"),
        P(),
        P(),
        P("seq", "head"),
        P("seq", "head"),
        P("head", None),
    )
    out_specs = P("seq", "head")
    return jax.shard_map(shards, mesh=mesh, in_specs=in_specs, out_specs=out_specs, check_vma=False)
```

```python
import functools
import math

import jax
import jax.numpy as jnp
from jax import lax
from jax.experimental import pallas as pl
from jax.experimental.pallas import tpu as pltpu
from jax.sharding import PartitionSpec as P

F32 = jnp.float32
BF16 = jnp.bfloat16
MESH = pl.DeviceIdType.MESH
EXACT = lax.Precision.HIGHEST

NY = 8
NZ = 8
NHD = 8
L = 128
HEADS = 4
HP = 64
CAP = 32
HD = 128
D_MAIN = 4096
THETA = 500000.0
EPSILON = 1e-05

(
    STATS_Z,
    STATS_Y,
    W_AZ,
    W_BY,
    RING_A,
    RING_B,
    SCAN1,
    SCAN2,
    SCAN3,
    SPAN_RS,
    SPAN_AG,
    ENC_RS,
    MAIN_RS,
    N_EX,
) = range(14)


def nn(a, b, precision=None):
    return lax.dot_general(
        a, b, (((1,), (0,)), ((), ())), precision=precision, preferred_element_type=F32
    )


def nt(a, b, precision=None):
    return lax.dot_general(
        a, b, (((1,), (1,)), ((), ())), precision=precision, preferred_element_type=F32
    )


def tn(a, b, precision=None):
    return lax.dot_general(
        a, b, (((0,), (0,)), ((), ())), precision=precision, preferred_element_type=F32
    )


def iota(shape, dim):
    return lax.broadcasted_iota(jnp.int32, shape, dim)


def silu(v):
    return v / (1.0 + jnp.exp(-v))


def one_minus_exp(u):
    series = u * (
        1.0
        - u
        * (
            1.0 / 2
            - u * (1.0 / 6 - u * (1.0 / 24 - u * (1.0 / 120 - u * (1.0 / 720 - u / 5040))))
        )
    )
    return jnp.where(u < 0.3, series, 1.0 - jnp.exp(-u))


def kernel(
    x_hbm,
    gate_hbm,
    convw_ref,
    b_hbm,
    c_hbm,
    step_ref,
    decay_ref,
    skip_ref,
    ngain_ref,
    mo_hbm,
    res_hbm,
    bnd_ref,
    cnt_ref,
    off_ref,
    pad_ref,
    mgain_ref,
    wq_hbm,
    wkv_hbm,
    mw_hbm,
    out_ref,
    x_ref,
    gate_ref,
    b_ref,
    c_ref,
    mo_ref,
    res_ref,
    wq_ref,
    wkv_ref,
    mw_ref,
    halo,
    ext,
    stats_z,
    stats_y,
    wbuf,
    s1_send,
    s1,
    s2,
    s3_send,
    s3,
    sp_send,
    sp_recv,
    ag,
    en_send,
    en_recv,
    kvbuf,
    qbuf,
    key_ranks,
    o_send,
    m_send,
    o_recv,
    m_recv,
    mn_send,
    mn_recv,
    local_sem,
    halo_sem,
    w0_send,
    w0_recv,
    kv_sem,
    group_sem,
    send_sem,
    recv_sem,
):
    s = lax.axis_index("seq")
    hd = lax.axis_index("head")
    y = s // NZ
    z = s % NZ

    def at_z(p):
        return (y * NZ + p, hd)

    def at_y(p):
        return (p * NZ + z, hd)

    def at_h(p):
        return (s, p)

    nxt = (lax.rem(s + 1, NY * NZ), hd)
    prv = (lax.rem(s + NY * NZ - 1, NY * NZ), hd)

    py, pz = lax.rem(y, 2), lax.rem(z, 2)
    yi, zi = y // 2, z // 2

    def at_class(dy, dz):
        yc, zc = 2 * lax.rem(yi + dy, 4) + py, 2 * lax.rem(zi + dz, 4) + pz
        return (yc * NZ + zc, hd)

    def member(e):
        yc = y + 1 - 2 * py if e // 2 else y
        zc = z + 1 - 2 * pz if e % 2 else z
        return (yc * NZ + zc, hd), 2 * lax.rem(yc, 2) + lax.rem(zc, 2)

    barrier = pltpu.get_barrier_semaphore()
    greet = [prv, member(3)[0]]
    for d in range(1, 8):
        greet += [at_z(lax.rem(z + d, NZ)), at_y(lax.rem(y + d, NY)), at_h(lax.rem(hd + d, NHD))]
    for dy in range(1, 4):
        for dz in range(1, 4):
            greet.append(at_class(dy, dz))
    for to in greet:
        pl.semaphore_signal(barrier, inc=1, device_id=to, device_id_type=MESH)

    loads = [
        (b_hbm, b_ref),
        (c_hbm, c_ref),
        (x_hbm, x_ref),
        (wq_hbm, wq_ref),
        (wkv_hbm, wkv_ref),
        (gate_hbm, gate_ref),
        (mo_hbm, mo_ref),
        (res_hbm.at[:, pl.ds(pl.multiple_of(hd * 128, 128), 128)], res_ref),
        (mw_hbm, mw_ref),
    ]
    load = [pltpu.make_async_copy(a, b, local_sem.at[i]) for i, (a, b) in enumerate(loads)]
    for copy in load:
        copy.start()
    l_b, l_c, l_x, l_wq, l_wkv, l_gate, l_mo, l_res, l_mw = load

    pending = []

    def send_all(ex, me, where, src, dst):
        for d in range(1, 8):
            p = lax.rem(me + d, 8)
            copy = pltpu.make_async_remote_copy(
                src_ref=src(p),
                dst_ref=dst,
                send_sem=send_sem.at[ex, d],
                recv_sem=recv_sem.at[ex, me],
                device_id=where(p),
                device_id_type=MESH,
            )
            copy.start()
            pending.append(copy)

    def recv_all(ex, me, where, slot):
        for d in range(1, 8):
            p = lax.rem(me + 8 - d, 8)
            pltpu.make_async_remote_copy(
                src_ref=slot(p),
                dst_ref=slot(p),
                send_sem=send_sem.at[ex, d],
                recv_sem=recv_sem.at[ex, p],
                device_id=where(p),
                device_id_type=MESH,
            ).wait_recv()

    row4 = iota((HEADS, L), 0)
    coef = jnp.zeros((HEADS, L), F32)
    for h in range(HEADS):
        coef = jnp.where(row4 == h, decay_ref[h], coef)
    rate = step_ref[...] * coef
    log_decay = -rate
    gain_row = jnp.sqrt(one_minus_exp(2.0 * rate))
    ti = iota((L, L), 0)
    si = iota((L, L), 1)
    causal = ti >= si
    tri = jnp.where(causal, 1.0, 0.0).astype(F32)
    run_row = nt(log_decay, tri, EXACT)
    run_col = [
        nt(tri, jnp.broadcast_to(log_decay[h : h + 1, :], (L, L)), EXACT) for h in range(HEADS)
    ]
    rem_row = jnp.exp(run_row[:, L - 1 : L] - run_row) * gain_row
    first = si < HP
    eye = jnp.where(ti == si, 1.0, 0.0).astype(BF16)
    top = ti < HP
    rem_x = [
        nt(
            eye,
            jnp.where(
                top,
                jnp.broadcast_to(rem_row[2 * i : 2 * i + 1, :], (L, L)),
                jnp.broadcast_to(rem_row[2 * i + 1 : 2 * i + 2, :], (L, L)),
            ).astype(BF16),
        )
        for i in range(2)
    ]
    run_x = jnp.concatenate(
        [jnp.where(first, run_col[2 * i], run_col[2 * i + 1]) for i in range(2)], axis=1
    )

    pl.semaphore_wait(barrier, len(greet))

    halo_copy = pltpu.make_async_remote_copy(
        src_ref=x_hbm.at[pl.ds(L - 16, 16), :],
        dst_ref=halo,
        send_sem=halo_sem.at[0],
        recv_sem=halo_sem.at[1],
        device_id=nxt,
        device_id_type=MESH,
    )
    halo_copy.start()

    def w0_parts(yp):
        rg = lax.rem(yp, 4)
        ch = yp // 4
        r = pl.ds(pl.multiple_of(16 * rg, 16), 16)
        return (
            (
                wq_hbm.at[r, pl.ds(pl.multiple_of(256 * ch, 256), 256)],
                wbuf.at[ch, y, z, rg, :, pl.ds(0, 256)],
            ),
            (
                wkv_hbm.at[r, pl.ds(pl.multiple_of(128 * ch, 128), 128)],
                wbuf.at[ch, y, z, rg, :, pl.ds(256, 128)],
            ),
        )

    def w0_copies():
        copies = []
        for d in range(1, 8):
            yp = lax.rem(y + d, NY)
            for i, (src, dst) in enumerate(w0_parts(yp)):
                copies.append(
                    pltpu.make_async_remote_copy(
                        src_ref=src,
                        dst_ref=dst,
                        send_sem=w0_send.at[i, d],
                        recv_sem=w0_recv.at[i, y],
                        device_id=at_y(yp),
                        device_id_type=MESH,
                    )
                )
        return copies

    @pl.when(y < 2)
    def _():
        for copy in w0_copies():
            copy.start()
        for i, (src, dst) in enumerate(w0_parts(y)):
            pltpu.make_async_copy(src, dst, w0_recv.at[i, y]).start()

    l_b.wait()
    l_c.wait()
    bm = b_ref[...]
    cm = c_ref[...]
    affinity = jnp.where(causal, nt(cm, bm), 0.0)
    mix = []
    for h in range(HEADS):
        spread = jnp.where(causal, run_col[h] - run_row[h : h + 1, :], 0.0)
        mix.append((jnp.exp(spread) * (affinity * gain_row[h : h + 1, :])).astype(BF16))

    l_wq.wait()
    l_wkv.wait()
    prow = s // 2 - 8
    padf = pad_ref[...].astype(F32)
    mg = mgain_ref[...]
    pad_one = jnp.sum(jnp.where(iota((24, 128), 0) == prow, padf, 0.0), axis=0, keepdims=True)
    gain_one = jnp.sum(jnp.where(iota((32, 128), 0) == s // 2, mg, 0.0), axis=0, keepdims=True)
    both = pad_one * gain_one
    half = jnp.where(s % 2 == 1, both[:, 64:], both[:, :64])
    half = jnp.broadcast_to(half, (16, 64)).astype(BF16)
    pq = nn(half, wq_ref[...])
    pkv = nn(half, wkv_ref[...])
    pad_sq = jnp.sum(jnp.sum(padf * padf, axis=1, keepdims=True), axis=0, keepdims=True)
    lane1 = iota((1, 128), 1)
    count = cnt_ref[0].astype(F32)
    last = jnp.zeros((1, 128), F32)
    for h in range(HEADS):
        last = jnp.where(lane1 == h, run_col[h][L - 1 : L, :], last)
    rows = [
        pq[0:1, 0:128],
        pq[0:1, 128:256],
        pkv[0:1, 0:128],
        pq[0:1, 256:384],
        pq[0:1, 384:512],
        pkv[0:1, 128:256],
        jnp.where(lane1 == z, count, 0.0),
        last,
    ]
    for i, row in enumerate(rows):
        stats_z[z, i : i + 1, :] = row
    send_all(STATS_Z, z, at_z, lambda p: stats_z.at[z], stats_z.at[z])

    l_x.wait()
    halo_copy.wait()
    ext[16:, :] = x_ref[...].astype(F32)
    ext[0:16, :] = jnp.where(s == 0, 0.0, halo[...].astype(F32))
    cw = convw_ref[...]
    summed = cw[0:1, :] * ext[13 : 13 + L, :]
    for k in range(1, 4):
        summed = summed + cw[k : k + 1, :] * ext[13 + k : 13 + k + L, :]
    conv = silu(summed).astype(BF16)
    conv_f = conv.astype(F32)

    weighted = (conv_f * jnp.concatenate(rem_x, axis=1)).astype(BF16)
    state = tn(bm, weighted).astype(BF16)
    s1_send[...] = state.reshape(8, 16, 256)
    send_all(SCAN1, z, at_z, lambda p: s1_send.at[p], s1.at[z])
    s1[z] = s1_send[z]

    recv_all(STATS_Z, z, at_z, lambda p: stats_z.at[p])
    tiles = stats_z[...]
    stats_y[y] = jnp.sum(tiles, axis=0)
    send_all(STATS_Y, y, at_y, lambda p: stats_y.at[y], stats_y.at[y])

    for b in range(2):
        for i, (src, dst) in enumerate(w0_parts(y)):
            rg = lax.rem(y, 4)
            ch = y // 4
            cols = pl.ds(0, 256) if i == 0 else pl.ds(256, 128)
            slot = wbuf.at[ch, b, z, rg, :, cols]
            pltpu.make_async_copy(slot, slot, w0_recv.at[i, b]).wait()
    rg_me = lax.rem(y, 4)
    ch_me = y // 4
    send_all(
        W_AZ, z, at_z, lambda p: wbuf.at[ch_me, 0, z, rg_me], wbuf.at[ch_me, 0, z, rg_me]
    )
    send_all(
        W_BY, y, at_y, lambda p: wbuf.at[ch_me, 1, z, rg_me], wbuf.at[ch_me, 1, z, rg_me]
    )

    within = []
    zero = jnp.zeros((), BF16)
    for i in range(2):
        pair = conv[:, 128 * i : 128 * (i + 1)]
        stacked = jnp.concatenate(
            [jnp.where(first, pair, zero), jnp.where(first, zero, pair)], axis=0
        )
        within.append(nn(jnp.concatenate([mix[2 * i], mix[2 * i + 1]], axis=1), stacked))
    skip = jnp.zeros((1, 256), F32)
    head_of = iota((1, 256), 1) // HP
    for h in range(HEADS):
        skip = jnp.where(head_of == h, skip_ref[h], skip)
    mixed_near = jnp.concatenate(within, axis=1) + skip * conv_f
    exp_run = jnp.exp(run_x)
    l_gate.wait()
    gate = silu(gate_ref[...].astype(F32))

    spread_head = jnp.where(iota((128, 256), 0) == iota((128, 256), 1) // HP, 1.0, 0.0)
    spread_head = spread_head.astype(F32)
    lz = nn(tiles[:, 7, :], spread_head, EXACT)
    recv_all(SCAN1, z, at_z, lambda p: s1.at[p])
    acc = jnp.zeros((16, 256), F32)
    cum = jnp.zeros((1, 256), F32)
    before, cums = [], []
    for j in range(NZ):
        before.append(acc)
        cums.append(cum)
        acc = jnp.exp(lz[j : j + 1, :]) * acc + s1[j].astype(F32)
        cum = cum + lz[j : j + 1, :]
    s2[y] = acc.astype(BF16)
    send_all(SCAN2, y, at_y, lambda p: s2.at[y], s2.at[y])

    def block_a(p, lo=0, n=8):
        return wbuf.at[p // 4, 0, pl.ds(lo, n), lax.rem(p, 4)]

    def block_b(p, lo=0, n=2):
        return wbuf.at[pl.ds(lo, n), 1, p]

    def rings(step, wait):
        for ex, me, where, block, whole in (
            (RING_A, y, at_y, block_a, 8),
            (RING_B, z, at_z, block_b, 2),
        ):
            for way in range(2):
                ahead = lax.rem(me + (1 if way == 0 else 7), 8)
                moved = step + (1 if wait else 0)
                of = lax.rem(me + (8 - moved if way == 0 else moved), 8)
                if step == 3:
                    part = block(of, way * whole // 2, whole // 2)
                else:
                    part = block(of)
                copy = pltpu.make_async_remote_copy(
                    src_ref=part,
                    dst_ref=part,
                    send_sem=send_sem.at[ex, 2 * step + way],
                    recv_sem=recv_sem.at[ex, 2 * step + way],
                    device_id=where(ahead),
                    device_id_type=MESH,
                )
                if wait:
                    copy.wait_recv()
                else:
                    copy.start()
                    pending.append(copy)

    recv_all(W_AZ, z, at_z, lambda p: wbuf.at[ch_me, 0, p, rg_me])
    recv_all(W_BY, y, at_y, lambda p: wbuf.at[p // 4, 1, z, lax.rem(p, 4)])
    rings(0, False)

    recv_all(STATS_Y, y, at_y, lambda p: stats_y.at[p])
    ytiles = stats_y[...]
    pad_total = jnp.sum(ytiles, axis=0)
    ly = nn(ytiles[:, 7, :], spread_head, EXACT)

    recv_all(SCAN2, y, at_y, lambda p: s2.at[p])
    rows_before = jnp.zeros((16, 256), F32)
    for j in range(NY - 1):
        longer = jnp.exp(ly[j : j + 1, :]) * rows_before + s2[j].astype(F32)
        rows_before = jnp.where(j < y, longer, rows_before)
    for j in range(NZ):
        s3_send[j] = (before[j] + jnp.exp(cums[j]) * rows_before).astype(BF16)
    send_all(SCAN3, z, at_z, lambda p: s3_send.at[p], s3.at[z])
    s3[z] = s3_send[z]

    rings(0, True)
    rings(1, False)

    bnd = bnd_ref[...] - s * L
    byte_at = iota((L, CAP), 0)
    slot_at = iota((L, CAP), 1)
    usable = slot_at < cnt_ref[0]
    picker = jnp.where((byte_at == bnd) & usable, 1.0, 0.0).astype(BF16)
    upto = jnp.where((bnd <= byte_at) & usable, 1.0, 0.0)
    newest = jnp.sum(upto, axis=1, keepdims=True) - 1.0
    spreader = jnp.where(slot_at.astype(F32) == newest, 1.0, 0.0).astype(BF16)
    l_res.wait()
    res = res_ref[...]
    res_span = tn(picker, res)

    lane = iota((CAP, 128), 1)
    place = (iota((CAP, 128), 0) + off_ref[0]).astype(F32)
    freq = jnp.exp(
        lax.rem(lane, HD // 2).astype(F32) * (-2.0 * math.log(THETA) / HD)
    )
    angle = place * freq
    cosine = jnp.cos(angle)
    sine = jnp.where(lane < HD // 2, -jnp.sin(angle), jnp.sin(angle))

    recv_all(SCAN3, z, at_z, lambda p: s3.at[p])
    entering = nn(cm, s3[...].reshape(128, 256)) * exp_run
    gated = (mixed_near + entering) * gate
    mean_sq = jnp.sum(gated * gated, axis=1, keepdims=True) * (1.0 / 256)
    normed = (gated * lax.rsqrt(mean_sq + EPSILON) * ngain_ref[...]).astype(BF16)
    l_mo.wait()
    picked = tn(picker, normed).astype(BF16)
    span_part = nn(picked, mo_ref[...]).astype(BF16)
    for j in range(NHD):
        sp_send[j] = span_part[:, 128 * j : 128 * (j + 1)]
    send_all(SPAN_RS, hd, at_h, lambda p: sp_send.at[p], sp_recv.at[hd])
    sp_recv[hd] = sp_send[hd]

    rings(1, True)
    rings(2, False)

    enc_part = nn(normed, mo_ref[...]).astype(BF16)
    for j in range(NHD):
        en_send[j] = enc_part[:, 128 * j : 128 * (j + 1)]
    en_recv[hd] = en_send[hd]

    recv_all(SPAN_RS, hd, at_h, lambda p: sp_recv.at[p])
    span_share = (res_span + jnp.sum(sp_recv[...].astype(F32), axis=0)).astype(BF16)
    ag[hd] = span_share
    send_all(SPAN_AG, hd, at_h, lambda p: ag.at[hd], ag.at[hd])

    rings(2, True)
    rings(3, False)

    key = iota((512, 128), 0)
    key_y, key_z = 2 * (key // 128) + py, 2 * lax.rem(key // CAP, 4) + pz
    expand = jnp.where(iota((512, 128), 1) == key_z, 1.0, 0.0).astype(BF16)
    per_row = nt(expand, jnp.concatenate([ytiles[:, 6, :], ytiles[:, 6, :]], axis=0).astype(BF16))
    lane16 = iota((512, 16), 1)
    key_count = jnp.sum(
        jnp.where(lane16 == 2 * (iota((512, 16), 0) // 128) + py, per_row, 0.0),
        axis=1,
        keepdims=True,
    )
    key_slot = lax.rem(key, CAP)
    key_rank = (key_y * NZ + key_z) * CAP + key_slot
    key_rank = jnp.where(key_slot.astype(F32) < key_count, key_rank, NY * NZ * CAP)
    key_ranks[...] = key_rank
    query = iota((1, 512), 1)
    query_rank = (
        ((y - py + query // 256) * NZ + z - pz + lax.rem(query // 128, 2)) * CAP
        + lax.rem(query, CAP)
    )

    recv_all(SPAN_AG, hd, at_h, lambda p: ag.at[p])
    send_all(ENC_RS, hd, at_h, lambda p: en_send.at[p], en_recv.at[hd])
    sq = jnp.zeros((CAP, 1), F32)
    pieces = []
    for j in range(NHD):
        piece = ag[j].astype(F32)
        sq = sq + jnp.sum(piece * piece, axis=1, keepdims=True)
        pieces.append((piece * mg[j : j + 1, :]).astype(BF16))
    scale = lax.rsqrt((sq + pad_sq) * (1.0 / D_MAIN) + EPSILON)
    span_x = jnp.concatenate(pieces, axis=1)
    rings(3, True)
    proj = [nn(span_x, wbuf[ch].reshape(1024, 384)) for ch in range(2)]

    def column(i):
        part = proj[i // 3][:, 128 * (i % 3) : 128 * (i % 3 + 1)]
        return (part + pad_total[i : i + 1, :]) * scale

    def rotate(v):
        return (v * cosine + pltpu.roll(v, HD // 2, 1) * sine).astype(BF16)

    kvbuf[yi, zi, 0] = rotate(column(2))
    kvbuf[yi, zi, 1] = column(5).astype(BF16)
    kv_copies = []
    for dy in range(4):
        for dz in range(4):
            if dy + dz > 0:
                kv_copies.append(
                    pltpu.make_async_remote_copy(
                        src_ref=kvbuf.at[yi, zi],
                        dst_ref=kvbuf.at[yi, zi],
                        send_sem=kv_sem.at[0, 4 * dy + dz],
                        recv_sem=kv_sem.at[1, 4 * dy + dz],
                        device_id=at_class(dy, dz),
                        device_id_type=MESH,
                    )
                )
    for copy in kv_copies:
        copy.start()
        pending.append(copy)
    mine = 2 * py + pz
    qbuf[mine] = jnp.concatenate([rotate(column(i)) for i in (0, 1, 3, 4)], axis=0)

    def group_copy(i, e, src, dst):
        return pltpu.make_async_remote_copy(
            src_ref=src,
            dst_ref=dst,
            send_sem=group_sem.at[0, i, e],
            recv_sem=group_sem.at[1, i, e],
            device_id=member(e)[0],
            device_id_type=MESH,
        )

    for e in range(1, 4):
        copy = group_copy(0, e, qbuf.at[mine], qbuf.at[mine])
        copy.start()
        pending.append(copy)

    recv_all(ENC_RS, hd, at_h, lambda p: en_recv.at[p])
    encoded = (res.astype(F32) + jnp.sum(en_recv[...].astype(F32), axis=0)).astype(BF16)

    for e in range(1, 4):
        slot = qbuf.at[member(e)[1]]
        group_copy(0, e, slot, slot).wait_recv()
    for dy in range(4):
        for dz in range(4):
            if dy + dz > 0:
                slot = kvbuf.at[lax.rem(yi + 4 - dy, 4), lax.rem(zi + 4 - dz, 4)]
                pltpu.make_async_remote_copy(
                    src_ref=slot,
                    dst_ref=slot,
                    send_sem=kv_sem.at[0, 4 * dy + dz],
                    recv_sem=kv_sem.at[1, 4 * dy + dz],
                    device_id=at_class(dy, dz),
                    device_id_type=MESH,
                ).wait_recv()

    kv = kvbuf[...]
    keys = kv[:, :, 0].reshape(512, HD)
    values = kv[:, :, 1].reshape(512, HD)
    ranks = key_ranks[...]
    unit = 1.0 / math.sqrt(HD)
    for m in range(4):
        scores = nt(keys, qbuf[m])
        allowed = ranks <= query_rank[:, 128 * m : 128 * (m + 1)]
        scores = jnp.where(allowed, scores * unit, -1e30)
        top = jnp.max(scores, axis=0, keepdims=True)
        weights = jnp.exp(scores - top)
        o_send[m] = tn(values, weights.astype(BF16)).astype(BF16)
        m_send[m, 0:1, :] = top
        m_send[m, 1:2, :] = jnp.sum(weights, axis=0, keepdims=True)

    for e in range(1, 4):
        place_e = member(e)[1]
        for i, (src, dst) in enumerate(((o_send, o_recv), (m_send, m_recv))):
            copy = group_copy(1 + i, e, src.at[place_e], dst.at[e])
            copy.start()
            pending.append(copy)
    o_recv[0] = o_send[mine]
    m_recv[0] = m_send[mine]

    for e in range(1, 4):
        group_copy(1, e, o_recv.at[e], o_recv.at[e]).wait_recv()
        group_copy(2, e, m_recv.at[e], m_recv.at[e]).wait_recv()

    tops = m_recv[:, 0, :]
    highest = jnp.max(tops, axis=0, keepdims=True)
    shrink = jnp.exp(tops - highest)
    total = jnp.sum(shrink * m_recv[:, 1, :], axis=0, keepdims=True)
    summed_o = jnp.zeros((HD, 128), F32)
    for e in range(4):
        summed_o = summed_o + shrink[e : e + 1, :] * o_recv[e].astype(F32)
    attended = (summed_o / total).T.astype(BF16)

    l_mw.wait()
    att = jnp.concatenate([attended[CAP * i : CAP * (i + 1), :] for i in range(4)], axis=1)
    main_part = nn(att, mw_ref[...]).astype(BF16)
    for j in range(NHD):
        mn_send[j] = main_part[:, 128 * j : 128 * (j + 1)]
    send_all(MAIN_RS, hd, at_h, lambda p: mn_send.at[p], mn_recv.at[hd])
    mn_recv[hd] = mn_send[hd]
    recv_all(MAIN_RS, hd, at_h, lambda p: mn_recv.at[p])
    main_rows = (span_share.astype(F32) + jnp.sum(mn_recv[...].astype(F32), axis=0)).astype(BF16)
    out_ref[...] = (encoded.astype(F32) + nn(spreader, main_rows)).astype(BF16)

    for copy in pending:
        copy.wait_send()

    @pl.when(y < 2)
    def _():
        for copy in w0_copies():
            copy.wait_send()


def shards(
    byte_stream,
    gate_stream,
    conv_weight,
    state_write,
    state_read,
    step_size,
    decay_coef,
    skip_gain,
    norm_gain,
    mixer_out,
    residual,
    boundaries,
    span_counts,
    span_offsets,
    pad_vector,
    main_gain,
    query_weight,
    key_value_weight,
    main_out_weight,
):
    far = pl.BlockSpec(memory_space=pl.ANY)
    near = pl.BlockSpec(memory_space=pltpu.VMEM)
    scalar = pl.BlockSpec(memory_space=pltpu.SMEM)
    vm = pltpu.VMEM
    dma = pltpu.SemaphoreType.DMA
    return pl.pallas_call(
        kernel,
        out_shape=jax.ShapeDtypeStruct((L, 128), BF16),
        in_specs=[
            far,
            far,
            near,
            far,
            far,
            near,
            scalar,
            scalar,
            near,
            far,
            far,
            near,
            scalar,
            scalar,
            near,
            near,
            far,
            far,
            far,
        ],
        out_specs=near,
        scratch_shapes=[
            vm((L, 256), BF16),
            vm((L, 256), BF16),
            vm((L, 128), BF16),
            vm((L, 128), BF16),
            vm((256, 1024), BF16),
            vm((L, 128), BF16),
            vm((64, 512), BF16),
            vm((64, 256), BF16),
            vm((512, 1024), BF16),
            vm((16, 256), BF16),
            vm((L + 16, 256), F32),
            vm((8, 8, 128), F32),
            vm((8, 8, 128), F32),
            vm((2, 2, 8, 4, 16, 384), BF16),
            vm((8, 16, 256), BF16),
            vm((8, 16, 256), BF16),
            vm((8, 16, 256), BF16),
            vm((8, 16, 256), BF16),
            vm((8, 16, 256), BF16),
            vm((8, CAP, 128), BF16),
            vm((8, CAP, 128), BF16),
            vm((8, CAP, 128), BF16),
            vm((8, L, 128), BF16),
            vm((8, L, 128), BF16),
            vm((4, 4, 2, CAP, 128), BF16),
            vm((4, 128, 128), BF16),
            vm((512, 128), jnp.int32),
            vm((4, 128, 128), BF16),
            vm((4, 8, 128), F32),
            vm((4, 128, 128), BF16),
            vm((4, 8, 128), F32),
            vm((8, CAP, 128), BF16),
            vm((8, CAP, 128), BF16),
            dma((9,)),
            dma((2,)),
            dma((2, 8)),
            dma((2, 2)),
            dma((2, 16)),
            dma((2, 3, 4)),
            dma((N_EX, 8)),
            dma((N_EX, 8)),
        ],
        compiler_params=pltpu.CompilerParams(
            collective_id=0, has_side_effects=True, vmem_limit_bytes=56 * 1024 * 1024
        ),
        cost_estimate=pl.CostEstimate(flops=10**9, bytes_accessed=4 * 10**6, transcendentals=10**6),
    )(
        byte_stream,
        gate_stream,
        conv_weight,
        state_write,
        state_read,
        step_size.T,
        decay_coef,
        skip_gain,
        norm_gain.reshape(1, 256),
        mixer_out,
        residual,
        boundaries,
        span_counts,
        span_offsets,
        pad_vector.reshape(24, 128),
        main_gain.reshape(32, 128),
        query_weight,
        key_value_weight,
        main_out_weight,
    )


def solution(mesh):
    in_specs = (
        P("seq", "head"),
        P("seq", "head"),
        P(None, "head"),
        P("seq", None),
        P("seq", None),
        P("seq", "head"),
        P("head"),
        P("head"),
        P("head"),
        P("head", None),
        P("seq", None),
        P("seq", None),
        P("seq"),
        P("seq"),
        P(),
        P(),
        P("seq", "head"),
        P("seq", "head"),
        P("head", None),
    )
    out_specs = P("seq", "head")
    return jax.shard_map(shards, mesh=mesh, in_specs=in_specs, out_specs=out_specs, check_vma=False)
```

```python
import functools
import math

import jax
import jax.numpy as jnp
from jax import lax
from jax.experimental import pallas as pl
from jax.experimental.pallas import tpu as pltpu
from jax.sharding import PartitionSpec as P

F32 = jnp.float32
BF16 = jnp.bfloat16
MESH = pl.DeviceIdType.MESH
EXACT = lax.Precision.HIGHEST

NY = 8
NZ = 8
NHD = 8
L = 128
HEADS = 4
HP = 64
CAP = 32
HD = 128
D_MAIN = 4096
THETA = 500000.0
EPSILON = 1e-05
FAR_FIRST = (4, 3, 5, 2, 6, 1, 7)
SLOTS = sorted(((i, j) for i in range(4) for j in range(4) if i + j > 0), key=lambda t: -t[0] - t[1])

(
    STATS_Z,
    STATS_Y,
    W_AZ,
    W_BY,
    RING_A,
    RING_B,
    SCAN1,
    SCAN2,
    SCAN3,
    SPAN_RS,
    SPAN_AG,
    ENC_RS,
    MAIN_RS,
    N_EX,
) = range(14)


def nn(a, b, precision=None):
    return lax.dot_general(
        a, b, (((1,), (0,)), ((), ())), precision=precision, preferred_element_type=F32
    )


def nt(a, b, precision=None):
    return lax.dot_general(
        a, b, (((1,), (1,)), ((), ())), precision=precision, preferred_element_type=F32
    )


def tn(a, b, precision=None):
    return lax.dot_general(
        a, b, (((0,), (0,)), ((), ())), precision=precision, preferred_element_type=F32
    )


def iota(shape, dim):
    return lax.broadcasted_iota(jnp.int32, shape, dim)


def silu(v):
    return v / (1.0 + jnp.exp(-v))


def one_minus_exp(u):
    series = u * (
        1.0
        - u
        * (
            1.0 / 2
            - u * (1.0 / 6 - u * (1.0 / 24 - u * (1.0 / 120 - u * (1.0 / 720 - u / 5040))))
        )
    )
    return jnp.where(u < 0.3, series, 1.0 - jnp.exp(-u))


def kernel(
    x_hbm,
    gate_hbm,
    convw_ref,
    b_hbm,
    c_hbm,
    step_ref,
    decay_ref,
    skip_ref,
    ngain_ref,
    mo_hbm,
    res_hbm,
    bnd_ref,
    cnt_ref,
    off_ref,
    pad_ref,
    mgain_ref,
    wq_hbm,
    wkv_hbm,
    mw_hbm,
    out_ref,
    x_ref,
    gate_ref,
    b_ref,
    c_ref,
    mo_ref,
    res_ref,
    wq_ref,
    wkv_ref,
    mw_ref,
    halo,
    ext,
    stats_z,
    stats_y,
    wbuf,
    s1_send,
    s1,
    s2,
    s3_send,
    s3,
    sp_send,
    sp_recv,
    ag,
    en_send,
    en_recv,
    kvbuf,
    qbuf,
    key_ranks,
    o_send,
    m_send,
    o_recv,
    m_recv,
    mn_send,
    mn_recv,
    local_sem,
    halo_sem,
    w0_send,
    w0_recv,
    kv_sem,
    group_sem,
    send_sem,
    recv_sem,
):
    s = lax.axis_index("seq")
    hd = lax.axis_index("head")
    y = s // NZ
    z = s % NZ

    def at_z(p):
        return (y * NZ + p, hd)

    def at_y(p):
        return (p * NZ + z, hd)

    def at_h(p):
        return (s, p)

    nxt = (lax.rem(s + 1, NY * NZ), hd)
    prv = (lax.rem(s + NY * NZ - 1, NY * NZ), hd)

    py, pz = lax.rem(y, 2), lax.rem(z, 2)
    sy, sz = 1 - 2 * py, 1 - 2 * pz

    def at_slot(i, j):
        yc = lax.rem(y + 8 + (0, -1, 2, -3)[i] * sy, NY)
        zc = lax.rem(z + 8 + (0, -1, 2, -3)[j] * sz, NZ)
        return (yc * NZ + zc, hd)

    def member(e):
        yc = y + 1 - 2 * py if e // 2 else y
        zc = z + 1 - 2 * pz if e % 2 else z
        return (yc * NZ + zc, hd), 2 * lax.rem(yc, 2) + lax.rem(zc, 2)

    barrier = pltpu.get_barrier_semaphore()
    greet = [prv]
    for d in range(1, 8):
        greet += [at_z(lax.rem(z + d, NZ)), at_y(lax.rem(y + d, NY)), at_h(lax.rem(hd + d, NHD))]
    for to in greet:
        pl.semaphore_signal(barrier, inc=1, device_id=to, device_id_type=MESH)

    loads = [
        (b_hbm, b_ref),
        (c_hbm, c_ref),
        (x_hbm, x_ref),
        (wq_hbm, wq_ref),
        (wkv_hbm, wkv_ref),
        (gate_hbm, gate_ref),
        (mo_hbm, mo_ref),
        (res_hbm.at[:, pl.ds(pl.multiple_of(hd * 128, 128), 128)], res_ref),
        (mw_hbm, mw_ref),
    ]
    load = [pltpu.make_async_copy(a, b, local_sem.at[i]) for i, (a, b) in enumerate(loads)]
    for copy in load:
        copy.start()
    l_b, l_c, l_x, l_wq, l_wkv, l_gate, l_mo, l_res, l_mw = load

    pending = []

    def send_all(ex, me, where, src, dst):
        for d in FAR_FIRST:
            p = lax.rem(me + d, 8)
            copy = pltpu.make_async_remote_copy(
                src_ref=src(p),
                dst_ref=dst,
                send_sem=send_sem.at[ex, d],
                recv_sem=recv_sem.at[ex, me],
                device_id=where(p),
                device_id_type=MESH,
            )
            copy.start()
            pending.append(copy)

    def recv_all(ex, me, where, slot):
        for d in range(1, 8):
            p = lax.rem(me + 8 - d, 8)
            pltpu.make_async_remote_copy(
                src_ref=slot(p),
                dst_ref=slot(p),
                send_sem=send_sem.at[ex, d],
                recv_sem=recv_sem.at[ex, p],
                device_id=where(p),
                device_id_type=MESH,
            ).wait_recv()

    row4 = iota((HEADS, L), 0)
    coef = jnp.zeros((HEADS, L), F32)
    for h in range(HEADS):
        coef = jnp.where(row4 == h, decay_ref[h], coef)
    rate = step_ref[...] * coef
    log_decay = -rate
    gain_row = jnp.sqrt(one_minus_exp(2.0 * rate))
    ti = iota((L, L), 0)
    si = iota((L, L), 1)
    causal = ti >= si
    tri = jnp.where(causal, 1.0, 0.0).astype(F32)
    run_row = nt(log_decay, tri, EXACT)
    run_col = [
        nt(tri, jnp.broadcast_to(log_decay[h : h + 1, :], (L, L)), EXACT) for h in range(HEADS)
    ]
    rem_row = jnp.exp(run_row[:, L - 1 : L] - run_row) * gain_row
    first = si < HP
    eye = jnp.where(ti == si, 1.0, 0.0).astype(BF16)
    top = ti < HP
    rem_x = [
        nt(
            eye,
            jnp.where(
                top,
                jnp.broadcast_to(rem_row[2 * i : 2 * i + 1, :], (L, L)),
                jnp.broadcast_to(rem_row[2 * i + 1 : 2 * i + 2, :], (L, L)),
            ).astype(BF16),
        )
        for i in range(2)
    ]
    run_x = jnp.concatenate(
        [jnp.where(first, run_col[2 * i], run_col[2 * i + 1]) for i in range(2)], axis=1
    )

    pl.semaphore_wait(barrier, len(greet))

    halo_copy = pltpu.make_async_remote_copy(
        src_ref=x_hbm.at[pl.ds(L - 16, 16), :],
        dst_ref=halo,
        send_sem=halo_sem.at[0],
        recv_sem=halo_sem.at[1],
        device_id=nxt,
        device_id_type=MESH,
    )
    halo_copy.start()

    def w0_parts(yp):
        rg = lax.rem(yp, 4)
        ch = yp // 4
        r = pl.ds(pl.multiple_of(16 * rg, 16), 16)
        return (
            (
                wq_hbm.at[r, pl.ds(pl.multiple_of(256 * ch, 256), 256)],
                wbuf.at[ch, y, z, rg, :, pl.ds(0, 256)],
            ),
            (
                wkv_hbm.at[r, pl.ds(pl.multiple_of(128 * ch, 128), 128)],
                wbuf.at[ch, y, z, rg, :, pl.ds(256, 128)],
            ),
        )

    def w0_copies():
        copies = []
        for d in FAR_FIRST:
            yp = lax.rem(y + d, NY)
            for i, (src, dst) in enumerate(w0_parts(yp)):
                copies.append(
                    pltpu.make_async_remote_copy(
                        src_ref=src,
                        dst_ref=dst,
                        send_sem=w0_send.at[i, d],
                        recv_sem=w0_recv.at[i, y],
                        device_id=at_y(yp),
                        device_id_type=MESH,
                    )
                )
        return copies

    @pl.when(y < 2)
    def _():
        for copy in w0_copies():
            copy.start()
        for i, (src, dst) in enumerate(w0_parts(y)):
            pltpu.make_async_copy(src, dst, w0_recv.at[i, y]).start()

    l_b.wait()
    l_c.wait()
    bm = b_ref[...]
    cm = c_ref[...]
    affinity = jnp.where(causal, nt(cm, bm), 0.0)
    mix = []
    for h in range(HEADS):
        spread = jnp.where(causal, run_col[h] - run_row[h : h + 1, :], 0.0)
        mix.append((jnp.exp(spread) * (affinity * gain_row[h : h + 1, :])).astype(BF16))

    l_wq.wait()
    l_wkv.wait()
    prow = s // 2 - 8
    padf = pad_ref[...].astype(F32)
    mg = mgain_ref[...]
    pad_one = jnp.sum(jnp.where(iota((24, 128), 0) == prow, padf, 0.0), axis=0, keepdims=True)
    gain_one = jnp.sum(jnp.where(iota((32, 128), 0) == s // 2, mg, 0.0), axis=0, keepdims=True)
    both = pad_one * gain_one
    half = jnp.where(s % 2 == 1, both[:, 64:], both[:, :64])
    half = jnp.broadcast_to(half, (16, 64)).astype(BF16)
    pq = nn(half, wq_ref[...])
    pkv = nn(half, wkv_ref[...])
    pad_sq = jnp.sum(jnp.sum(padf * padf, axis=1, keepdims=True), axis=0, keepdims=True)
    lane1 = iota((1, 128), 1)
    count = cnt_ref[0].astype(F32)
    last = jnp.zeros((1, 128), F32)
    for h in range(HEADS):
        last = jnp.where(lane1 == h, run_col[h][L - 1 : L, :], last)
    rows = [
        pq[0:1, 0:128],
        pq[0:1, 128:256],
        pkv[0:1, 0:128],
        pq[0:1, 256:384],
        pq[0:1, 384:512],
        pkv[0:1, 128:256],
        jnp.where(lane1 == z, count, 0.0),
        last,
    ]
    for i, row in enumerate(rows):
        stats_z[z, i : i + 1, :] = row
    send_all(STATS_Z, z, at_z, lambda p: stats_z.at[z], stats_z.at[z])

    l_x.wait()
    halo_copy.wait()
    ext[16:, :] = x_ref[...].astype(F32)
    ext[0:16, :] = jnp.where(s == 0, 0.0, halo[...].astype(F32))
    cw = convw_ref[...]
    summed = cw[0:1, :] * ext[13 : 13 + L, :]
    for k in range(1, 4):
        summed = summed + cw[k : k + 1, :] * ext[13 + k : 13 + k + L, :]
    conv = silu(summed).astype(BF16)
    conv_f = conv.astype(F32)

    weighted = (conv_f * jnp.concatenate(rem_x, axis=1)).astype(BF16)
    state = tn(bm, weighted).astype(BF16)
    s1_send[...] = state.reshape(8, 16, 256)
    send_all(SCAN1, z, at_z, lambda p: s1_send.at[p], s1.at[z])
    s1[z] = s1_send[z]

    recv_all(STATS_Z, z, at_z, lambda p: stats_z.at[p])
    tiles = stats_z[...]
    stats_y[y] = jnp.sum(tiles, axis=0)
    send_all(STATS_Y, y, at_y, lambda p: stats_y.at[y], stats_y.at[y])

    for b in range(2):
        for i, (src, dst) in enumerate(w0_parts(y)):
            rg = lax.rem(y, 4)
            ch = y // 4
            cols = pl.ds(0, 256) if i == 0 else pl.ds(256, 128)
            slot = wbuf.at[ch, b, z, rg, :, cols]
            pltpu.make_async_copy(slot, slot, w0_recv.at[i, b]).wait()
    rg_me = lax.rem(y, 4)
    ch_me = y // 4
    send_all(
        W_AZ, z, at_z, lambda p: wbuf.at[ch_me, 0, z, rg_me], wbuf.at[ch_me, 0, z, rg_me]
    )
    send_all(
        W_BY, y, at_y, lambda p: wbuf.at[ch_me, 1, z, rg_me], wbuf.at[ch_me, 1, z, rg_me]
    )

    within = []
    zero = jnp.zeros((), BF16)
    for i in range(2):
        pair = conv[:, 128 * i : 128 * (i + 1)]
        stacked = jnp.concatenate(
            [jnp.where(first, pair, zero), jnp.where(first, zero, pair)], axis=0
        )
        within.append(nn(jnp.concatenate([mix[2 * i], mix[2 * i + 1]], axis=1), stacked))
    skip = jnp.zeros((1, 256), F32)
    head_of = iota((1, 256), 1) // HP
    for h in range(HEADS):
        skip = jnp.where(head_of == h, skip_ref[h], skip)
    mixed_near = jnp.concatenate(within, axis=1) + skip * conv_f
    exp_run = jnp.exp(run_x)
    l_gate.wait()
    gate = silu(gate_ref[...].astype(F32))

    spread_head = jnp.where(iota((128, 256), 0) == iota((128, 256), 1) // HP, 1.0, 0.0)
    spread_head = spread_head.astype(F32)
    lz = nn(tiles[:, 7, :], spread_head, EXACT)
    recv_all(SCAN1, z, at_z, lambda p: s1.at[p])
    acc = jnp.zeros((16, 256), F32)
    cum = jnp.zeros((1, 256), F32)
    before, cums = [], []
    for j in range(NZ):
        before.append(acc)
        cums.append(cum)
        acc = jnp.exp(lz[j : j + 1, :]) * acc + s1[j].astype(F32)
        cum = cum + lz[j : j + 1, :]
    s2[y] = acc.astype(BF16)
    send_all(SCAN2, y, at_y, lambda p: s2.at[y], s2.at[y])

    def block_a(p, lo=0, n=8):
        return wbuf.at[p // 4, 0, pl.ds(lo, n), lax.rem(p, 4)]

    def block_b(p, lo=0, n=2):
        return wbuf.at[pl.ds(lo, n), 1, p]

    def rings(step, wait):
        for ex, me, where, block, whole in (
            (RING_A, y, at_y, block_a, 8),
            (RING_B, z, at_z, block_b, 2),
        ):
            for way in range(2):
                ahead = lax.rem(me + (1 if way == 0 else 7), 8)
                moved = step + (1 if wait else 0)
                of = lax.rem(me + (8 - moved if way == 0 else moved), 8)
                if step == 3:
                    part = block(of, way * whole // 2, whole // 2)
                else:
                    part = block(of)
                copy = pltpu.make_async_remote_copy(
                    src_ref=part,
                    dst_ref=part,
                    send_sem=send_sem.at[ex, 2 * step + way],
                    recv_sem=recv_sem.at[ex, 2 * step + way],
                    device_id=where(ahead),
                    device_id_type=MESH,
                )
                if wait:
                    copy.wait_recv()
                else:
                    copy.start()
                    pending.append(copy)

    recv_all(W_AZ, z, at_z, lambda p: wbuf.at[ch_me, 0, p, rg_me])
    recv_all(W_BY, y, at_y, lambda p: wbuf.at[p // 4, 1, z, lax.rem(p, 4)])
    rings(0, False)

    recv_all(STATS_Y, y, at_y, lambda p: stats_y.at[p])
    ytiles = stats_y[...]
    pad_total = jnp.sum(ytiles, axis=0)
    ly = nn(ytiles[:, 7, :], spread_head, EXACT)

    recv_all(SCAN2, y, at_y, lambda p: s2.at[p])
    rows_before = jnp.zeros((16, 256), F32)
    for j in range(NY - 1):
        longer = jnp.exp(ly[j : j + 1, :]) * rows_before + s2[j].astype(F32)
        rows_before = jnp.where(j < y, longer, rows_before)
    for j in range(NZ):
        s3_send[j] = (before[j] + jnp.exp(cums[j]) * rows_before).astype(BF16)
    send_all(SCAN3, z, at_z, lambda p: s3_send.at[p], s3.at[z])
    s3[z] = s3_send[z]

    rings(0, True)
    rings(1, False)

    bnd = bnd_ref[...] - s * L
    byte_at = iota((L, CAP), 0)
    slot_at = iota((L, CAP), 1)
    usable = slot_at < cnt_ref[0]
    picker = jnp.where((byte_at == bnd) & usable, 1.0, 0.0).astype(BF16)
    upto = jnp.where((bnd <= byte_at) & usable, 1.0, 0.0)
    newest = jnp.sum(upto, axis=1, keepdims=True) - 1.0
    spreader = jnp.where(slot_at.astype(F32) == newest, 1.0, 0.0).astype(BF16)
    l_res.wait()
    res = res_ref[...]
    res_span = tn(picker, res)

    lane = iota((CAP, 128), 1)
    place = (iota((CAP, 128), 0) + off_ref[0]).astype(F32)
    freq = jnp.exp(
        lax.rem(lane, HD // 2).astype(F32) * (-2.0 * math.log(THETA) / HD)
    )
    angle = place * freq
    cosine = jnp.cos(angle)
    sine = jnp.where(lane < HD // 2, -jnp.sin(angle), jnp.sin(angle))

    recv_all(SCAN3, z, at_z, lambda p: s3.at[p])
    entering = nn(cm, s3[...].reshape(128, 256)) * exp_run
    gated = (mixed_near + entering) * gate
    mean_sq = jnp.sum(gated * gated, axis=1, keepdims=True) * (1.0 / 256)
    normed = (gated * lax.rsqrt(mean_sq + EPSILON) * ngain_ref[...]).astype(BF16)
    l_mo.wait()
    picked = tn(picker, normed).astype(BF16)
    span_part = nn(picked, mo_ref[...]).astype(BF16)
    for j in range(NHD):
        sp_send[j] = span_part[:, 128 * j : 128 * (j + 1)]
    send_all(SPAN_RS, hd, at_h, lambda p: sp_send.at[p], sp_recv.at[hd])
    sp_recv[hd] = sp_send[hd]

    rings(1, True)
    rings(2, False)

    enc_part = nn(normed, mo_ref[...]).astype(BF16)
    for j in range(NHD):
        en_send[j] = enc_part[:, 128 * j : 128 * (j + 1)]
    en_recv[hd] = en_send[hd]

    recv_all(SPAN_RS, hd, at_h, lambda p: sp_recv.at[p])
    span_share = (res_span + jnp.sum(sp_recv[...].astype(F32), axis=0)).astype(BF16)
    ag[hd] = span_share
    send_all(SPAN_AG, hd, at_h, lambda p: ag.at[hd], ag.at[hd])

    rings(2, True)
    rings(3, False)

    key = iota((512, 128), 0)
    key_y = lax.rem(y + 16 - (key // 128) * sy, NY)
    key_z = lax.rem(z + 16 - lax.rem(key // CAP, 4) * sz, NZ)
    expand = jnp.where(iota((512, 128), 1) == key_z, 1.0, 0.0).astype(BF16)
    per_row = nt(expand, jnp.concatenate([ytiles[:, 6, :], ytiles[:, 6, :]], axis=0).astype(BF16))
    lane16 = iota((512, 16), 1)
    key_count = jnp.sum(
        jnp.where(lane16 == lax.rem(y + 16 - (iota((512, 16), 0) // 128) * sy, NY), per_row, 0.0),
        axis=1,
        keepdims=True,
    )
    key_slot = lax.rem(key, CAP)
    key_rank = (key_y * NZ + key_z) * CAP + key_slot
    key_rank = jnp.where(key_slot.astype(F32) < key_count, key_rank, NY * NZ * CAP)
    key_ranks[...] = key_rank
    query = iota((1, 512), 1)
    query_rank = (
        ((y - py + query // 256) * NZ + z - pz + lax.rem(query // 128, 2)) * CAP
        + lax.rem(query, CAP)
    )

    recv_all(SPAN_AG, hd, at_h, lambda p: ag.at[p])
    sq = jnp.zeros((CAP, 1), F32)
    pieces = []
    for j in range(NHD):
        piece = ag[j].astype(F32)
        sq = sq + jnp.sum(piece * piece, axis=1, keepdims=True)
        pieces.append((piece * mg[j : j + 1, :]).astype(BF16))
    scale = lax.rsqrt((sq + pad_sq) * (1.0 / D_MAIN) + EPSILON)
    span_x = jnp.concatenate(pieces, axis=1)
    rings(3, True)
    proj = [nn(span_x, wbuf[ch].reshape(1024, 384)) for ch in range(2)]

    def column(i):
        part = proj[i // 3][:, 128 * (i % 3) : 128 * (i % 3 + 1)]
        return (part + pad_total[i : i + 1, :]) * scale

    def rotate(v):
        return (v * cosine + pltpu.roll(v, HD // 2, 1) * sine).astype(BF16)

    kvbuf[0, 0, 0] = rotate(column(2))
    kvbuf[0, 0, 1] = column(5).astype(BF16)

    def kv_copy(i, j):
        return pltpu.make_async_remote_copy(
            src_ref=kvbuf.at[0, 0],
            dst_ref=kvbuf.at[i, j],
            send_sem=kv_sem.at[0, 4 * i + j],
            recv_sem=kv_sem.at[1, 4 * i + j],
            device_id=at_slot(i, j),
            device_id_type=MESH,
        )

    kv_copies = [kv_copy(i, j) for i, j in SLOTS]
    for copy in kv_copies:
        copy.start()
        pending.append(copy)
    mine = 2 * py + pz
    qbuf[mine] = jnp.concatenate([rotate(column(i)) for i in (0, 1, 3, 4)], axis=0)

    def group_copy(i, e, src, dst):
        return pltpu.make_async_remote_copy(
            src_ref=src,
            dst_ref=dst,
            send_sem=group_sem.at[0, i, e],
            recv_sem=group_sem.at[1, i, e],
            device_id=member(e)[0],
            device_id_type=MESH,
        )

    for e in range(1, 4):
        copy = group_copy(0, e, qbuf.at[mine], qbuf.at[mine])
        copy.start()
        pending.append(copy)

    send_all(ENC_RS, hd, at_h, lambda p: en_send.at[p], en_recv.at[hd])

    recv_all(ENC_RS, hd, at_h, lambda p: en_recv.at[p])
    encoded = (res.astype(F32) + jnp.sum(en_recv[...].astype(F32), axis=0)).astype(BF16)

    for e in range(1, 4):
        slot = qbuf.at[member(e)[1]]
        group_copy(0, e, slot, slot).wait_recv()
    for copy in kv_copies:
        copy.wait_recv()

    kv = kvbuf[...]
    keys = kv[:, :, 0].reshape(512, HD)
    values = kv[:, :, 1].reshape(512, HD)
    ranks = key_ranks[...]
    unit = 1.0 / math.sqrt(HD)
    for m in range(4):
        scores = nt(keys, qbuf[m])
        allowed = ranks <= query_rank[:, 128 * m : 128 * (m + 1)]
        scores = jnp.where(allowed, scores * unit, -1e30)
        top = jnp.max(scores, axis=0, keepdims=True)
        weights = jnp.exp(scores - top)
        o_send[m] = tn(values, weights.astype(BF16)).astype(BF16)
        m_send[m, 0:1, :] = top
        m_send[m, 1:2, :] = jnp.sum(weights, axis=0, keepdims=True)

    for e in range(1, 4):
        place_e = member(e)[1]
        for i, (src, dst) in enumerate(((o_send, o_recv), (m_send, m_recv))):
            copy = group_copy(1 + i, e, src.at[place_e], dst.at[e])
            copy.start()
            pending.append(copy)
    o_recv[0] = o_send[mine]
    m_recv[0] = m_send[mine]

    for e in range(1, 4):
        group_copy(1, e, o_recv.at[e], o_recv.at[e]).wait_recv()
        group_copy(2, e, m_recv.at[e], m_recv.at[e]).wait_recv()

    tops = m_recv[:, 0, :]
    highest = jnp.max(tops, axis=0, keepdims=True)
    shrink = jnp.exp(tops - highest)
    total = jnp.sum(shrink * m_recv[:, 1, :], axis=0, keepdims=True)
    summed_o = jnp.zeros((HD, 128), F32)
    for e in range(4):
        summed_o = summed_o + shrink[e : e + 1, :] * o_recv[e].astype(F32)
    attended = (summed_o / total).T.astype(BF16)

    l_mw.wait()
    att = jnp.concatenate([attended[CAP * i : CAP * (i + 1), :] for i in range(4)], axis=1)
    main_part = nn(att, mw_ref[...]).astype(BF16)
    for j in range(NHD):
        mn_send[j] = main_part[:, 128 * j : 128 * (j + 1)]
    send_all(MAIN_RS, hd, at_h, lambda p: mn_send.at[p], mn_recv.at[hd])
    mn_recv[hd] = mn_send[hd]
    recv_all(MAIN_RS, hd, at_h, lambda p: mn_recv.at[p])
    main_rows = (span_share.astype(F32) + jnp.sum(mn_recv[...].astype(F32), axis=0)).astype(BF16)
    out_ref[...] = (encoded.astype(F32) + nn(spreader, main_rows)).astype(BF16)

    for copy in pending:
        copy.wait_send()

    @pl.when(y < 2)
    def _():
        for copy in w0_copies():
            copy.wait_send()


def shards(
    byte_stream,
    gate_stream,
    conv_weight,
    state_write,
    state_read,
    step_size,
    decay_coef,
    skip_gain,
    norm_gain,
    mixer_out,
    residual,
    boundaries,
    span_counts,
    span_offsets,
    pad_vector,
    main_gain,
    query_weight,
    key_value_weight,
    main_out_weight,
):
    far = pl.BlockSpec(memory_space=pl.ANY)
    near = pl.BlockSpec(memory_space=pltpu.VMEM)
    scalar = pl.BlockSpec(memory_space=pltpu.SMEM)
    vm = pltpu.VMEM
    dma = pltpu.SemaphoreType.DMA
    return pl.pallas_call(
        kernel,
        out_shape=jax.ShapeDtypeStruct((L, 128), BF16),
        in_specs=[
            far,
            far,
            near,
            far,
            far,
            near,
            scalar,
            scalar,
            near,
            far,
            far,
            near,
            scalar,
            scalar,
            near,
            near,
            far,
            far,
            far,
        ],
        out_specs=near,
        scratch_shapes=[
            vm((L, 256), BF16),
            vm((L, 256), BF16),
            vm((L, 128), BF16),
            vm((L, 128), BF16),
            vm((256, 1024), BF16),
            vm((L, 128), BF16),
            vm((64, 512), BF16),
            vm((64, 256), BF16),
            vm((512, 1024), BF16),
            vm((16, 256), BF16),
            vm((L + 16, 256), F32),
            vm((8, 8, 128), F32),
            vm((8, 8, 128), F32),
            vm((2, 2, 8, 4, 16, 384), BF16),
            vm((8, 16, 256), BF16),
            vm((8, 16, 256), BF16),
            vm((8, 16, 256), BF16),
            vm((8, 16, 256), BF16),
            vm((8, 16, 256), BF16),
            vm((8, CAP, 128), BF16),
            vm((8, CAP, 128), BF16),
            vm((8, CAP, 128), BF16),
            vm((8, L, 128), BF16),
            vm((8, L, 128), BF16),
            vm((4, 4, 2, CAP, 128), BF16),
            vm((4, 128, 128), BF16),
            vm((512, 128), jnp.int32),
            vm((4, 128, 128), BF16),
            vm((4, 8, 128), F32),
            vm((4, 128, 128), BF16),
            vm((4, 8, 128), F32),
            vm((8, CAP, 128), BF16),
            vm((8, CAP, 128), BF16),
            dma((9,)),
            dma((2,)),
            dma((2, 8)),
            dma((2, 2)),
            dma((2, 16)),
            dma((2, 3, 4)),
            dma((N_EX, 8)),
            dma((N_EX, 8)),
        ],
        compiler_params=pltpu.CompilerParams(
            collective_id=0, has_side_effects=True, vmem_limit_bytes=56 * 1024 * 1024
        ),
        cost_estimate=pl.CostEstimate(flops=10**9, bytes_accessed=4 * 10**6, transcendentals=10**6),
    )(
        byte_stream,
        gate_stream,
        conv_weight,
        state_write,
        state_read,
        step_size.T,
        decay_coef,
        skip_gain,
        norm_gain.reshape(1, 256),
        mixer_out,
        residual,
        boundaries,
        span_counts,
        span_offsets,
        pad_vector.reshape(24, 128),
        main_gain.reshape(32, 128),
        query_weight,
        key_value_weight,
        main_out_weight,
    )


def solution(mesh):
    in_specs = (
        P("seq", "head"),
        P("seq", "head"),
        P(None, "head"),
        P("seq", None),
        P("seq", None),
        P("seq", "head"),
        P("head"),
        P("head"),
        P("head"),
        P("head", None),
        P("seq", None),
        P("seq", None),
        P("seq"),
        P("seq"),
        P(),
        P(),
        P("seq", "head"),
        P("seq", "head"),
        P("head", None),
    )
    out_specs = P("seq", "head")
    return jax.shard_map(shards, mesh=mesh, in_specs=in_specs, out_specs=out_specs, check_vma=False)
```

```python
import functools
import math

import jax
import jax.numpy as jnp
from jax import lax
from jax.experimental import pallas as pl
from jax.experimental.pallas import tpu as pltpu
from jax.sharding import PartitionSpec as P

F32 = jnp.float32
BF16 = jnp.bfloat16
MESH = pl.DeviceIdType.MESH
EXACT = lax.Precision.HIGHEST

NY = 8
NZ = 8
NHD = 8
L = 128
HEADS = 4
HP = 64
CAP = 32
HD = 128
D_MAIN = 4096
THETA = 500000.0
EPSILON = 1e-05
FAR_FIRST = (4, 3, 5, 2, 6, 1, 7)
SLOTS = sorted(((i, j) for i in range(4) for j in range(4) if i + j > 0), key=lambda t: -t[0] - t[1])

(
    EDGE,
    STATS_Y,
    W_AZ,
    W_BY,
    RING_A,
    RING_B,
    SCAN1,
    SCAN2,
    SCAN3,
    SPAN_RS,
    SPAN_AG,
    ENC_RS,
    MAIN_RS,
    N_EX,
) = range(14)


def nn(a, b, precision=None):
    return lax.dot_general(
        a, b, (((1,), (0,)), ((), ())), precision=precision, preferred_element_type=F32
    )


def nt(a, b, precision=None):
    return lax.dot_general(
        a, b, (((1,), (1,)), ((), ())), precision=precision, preferred_element_type=F32
    )


def tn(a, b, precision=None):
    return lax.dot_general(
        a, b, (((0,), (0,)), ((), ())), precision=precision, preferred_element_type=F32
    )


def iota(shape, dim):
    return lax.broadcasted_iota(jnp.int32, shape, dim)


def silu(v):
    return v / (1.0 + jnp.exp(-v))


def one_minus_exp(u):
    series = u * (
        1.0
        - u
        * (
            1.0 / 2
            - u * (1.0 / 6 - u * (1.0 / 24 - u * (1.0 / 120 - u * (1.0 / 720 - u / 5040))))
        )
    )
    return jnp.where(u < 0.3, series, 1.0 - jnp.exp(-u))


def kernel(
    x_hbm,
    gate_hbm,
    convw_hbm,
    b_hbm,
    c_hbm,
    step_hbm,
    decay_hbm,
    skip_hbm,
    ngain_hbm,
    mo_hbm,
    res_hbm,
    bnd_hbm,
    pad_hbm,
    mgain_hbm,
    wq_hbm,
    wkv_hbm,
    mw_hbm,
    out_ref,
    convw_ref,
    step_ref,
    decay_ref,
    skip_ref,
    ngain_ref,
    bnd_ref,
    pad_ref,
    mgain_ref,
    x_ref,
    gate_ref,
    b_ref,
    c_ref,
    mo_ref,
    res_ref,
    wq_ref,
    wkv_ref,
    mw_ref,
    ext,
    ebuf,
    stats_y,
    wbuf,
    s1_send,
    s1,
    s2,
    s3_send,
    s3,
    sp_send,
    sp_recv,
    ag,
    en_send,
    en_recv,
    kvbuf,
    qbuf,
    key_ranks,
    o_send,
    m_send,
    o_recv,
    m_recv,
    mn_send,
    mn_recv,
    local_sem,
    prev_send,
    prev_recv,
    w0_send,
    w0_recv,
    kv_sem,
    group_sem,
    send_sem,
    recv_sem,
):
    s = lax.axis_index("seq")
    hd = lax.axis_index("head")
    y = s // NZ
    z = s % NZ

    def at_z(p):
        return (y * NZ + p, hd)

    def at_y(p):
        return (p * NZ + z, hd)

    def at_h(p):
        return (s, p)

    py, pz = lax.rem(y, 2), lax.rem(z, 2)
    sy, sz = 1 - 2 * py, 1 - 2 * pz

    def at_slot(i, j):
        yc = lax.rem(y + 8 + (0, -1, 2, -3)[i] * sy, NY)
        zc = lax.rem(z + 8 + (0, -1, 2, -3)[j] * sz, NZ)
        return (yc * NZ + zc, hd)

    def member(e):
        yc = y + 1 - 2 * py if e // 2 else y
        zc = z + 1 - 2 * pz if e % 2 else z
        return (yc * NZ + zc, hd), 2 * lax.rem(yc, 2) + lax.rem(zc, 2)

    barrier = pltpu.get_barrier_semaphore()
    greet = [(lax.rem(y + NY - 1, NY) * NZ + NZ - 1, hd)]
    for d in range(1, 8):
        greet += [at_z(lax.rem(z + d, NZ)), at_y(lax.rem(y + d, NY)), at_h(lax.rem(hd + d, NHD))]
    for to in greet:
        pl.semaphore_signal(barrier, inc=1, device_id=to, device_id_type=MESH)

    loads = [
        (step_hbm, step_ref),
        (decay_hbm, decay_ref),
        (x_hbm, x_ref),
        (convw_hbm, convw_ref),
        (b_hbm, b_ref),
        (wq_hbm, wq_ref),
        (wkv_hbm, wkv_ref),
        (pad_hbm, pad_ref),
        (mgain_hbm, mgain_ref),
        (bnd_hbm, bnd_ref),
        (c_hbm, c_ref),
        (gate_hbm, gate_ref),
        (skip_hbm, skip_ref),
        (ngain_hbm, ngain_ref),
        (res_hbm.at[:, pl.ds(pl.multiple_of(hd * 128, 128), 128)], res_ref),
        (mo_hbm, mo_ref),
        (mw_hbm, mw_ref),
    ]
    load = [pltpu.make_async_copy(a, b, local_sem.at[i]) for i, (a, b) in enumerate(loads)]
    for copy in load[:10]:
        copy.start()
    l_step, l_decay, l_x, l_convw, l_b, l_wq, l_wkv, l_pad, l_mgain, l_bnd = load[:10]
    l_c, l_gate, l_skip, l_ngain, l_res, l_mo, l_mw = load[10:]

    pending = []

    def send_all(ex, me, where, src, dst):
        for d in FAR_FIRST:
            p = lax.rem(me + d, 8)
            copy = pltpu.make_async_remote_copy(
                src_ref=src(p),
                dst_ref=dst,
                send_sem=send_sem.at[ex, d],
                recv_sem=recv_sem.at[ex, me],
                device_id=where(p),
                device_id_type=MESH,
            )
            copy.start()
            pending.append(copy)

    def recv_all(ex, me, where, slot):
        for d in range(1, 8):
            p = lax.rem(me + 8 - d, 8)
            pltpu.make_async_remote_copy(
                src_ref=slot(p),
                dst_ref=slot(p),
                send_sem=send_sem.at[ex, d],
                recv_sem=recv_sem.at[ex, p],
                device_id=where(p),
                device_id_type=MESH,
            ).wait_recv()

    l_step.wait()
    l_decay.wait()
    dec = decay_ref[...]
    row4 = iota((HEADS, L), 0)
    coef = jnp.zeros((HEADS, L), F32)
    for h in range(HEADS):
        coef = jnp.where(row4 == h, dec[:, h : h + 1], coef)
    rate = step_ref[...] * coef
    log_decay = -rate
    gain_row = jnp.sqrt(one_minus_exp(2.0 * rate))
    ti = iota((L, L), 0)
    si = iota((L, L), 1)
    causal = ti >= si
    tri = jnp.where(causal, 1.0, 0.0).astype(F32)
    run_row = nt(log_decay, tri, EXACT)
    run_col = [
        nt(tri, jnp.broadcast_to(log_decay[h : h + 1, :], (L, L)), EXACT) for h in range(HEADS)
    ]
    rem_row = jnp.exp(run_row[:, L - 1 : L] - run_row) * gain_row
    first = si < HP
    eye = jnp.where(ti == si, 1.0, 0.0).astype(BF16)
    top = ti < HP
    rem_x = [
        nt(
            eye,
            jnp.where(
                top,
                jnp.broadcast_to(rem_row[2 * i : 2 * i + 1, :], (L, L)),
                jnp.broadcast_to(rem_row[2 * i + 1 : 2 * i + 2, :], (L, L)),
            ).astype(BF16),
        )
        for i in range(2)
    ]
    run_x = jnp.concatenate(
        [jnp.where(first, run_col[2 * i], run_col[2 * i + 1]) for i in range(2)], axis=1
    )

    l_x.wait()
    l_convw.wait()
    l_b.wait()
    ext[0:8, :] = jnp.zeros((8, 256), F32)
    ext[8 : 8 + L, :] = x_ref[...].astype(F32)
    ext[8 + L :, :] = jnp.zeros((8, 256), F32)
    cw = convw_ref[...]
    summed = cw[0:1, :] * ext[5 : 13 + L, :]
    for k in range(1, 4):
        summed = summed + cw[k : k + 1, :] * ext[5 + k : 13 + k + L, :]
    conv_own = silu(summed[:L]).astype(BF16).astype(F32)

    bm = b_ref[...]
    inner = iota((L, 256), 0) >= 3
    weighted = jnp.where(inner, conv_own * jnp.concatenate(rem_x, axis=1), 0.0).astype(BF16)
    state = tn(bm, weighted).astype(BF16)
    s1_send[...] = state.reshape(8, 16, 256)
    head_b = bm[0:16, :].astype(F32)
    ebuf[1 + z, 0:3, 0:256] = summed[0:3]
    ebuf[1 + z, 3:6, 0:256] = summed[L : L + 3]
    ebuf[1 + z, 6:7, 0:128] = head_b[0:1, :]
    ebuf[1 + z, 6:7, 128:256] = head_b[1:2, :]
    ebuf[1 + z, 7:8, 0:128] = head_b[2:3, :]
    ebuf[1 + z, 7:8, 128:256] = jnp.zeros((1, 128), F32)

    l_wq.wait()
    l_wkv.wait()
    l_pad.wait()
    l_mgain.wait()
    l_bnd.wait()
    prow = s // 2 - 8
    padf = pad_ref[...].astype(F32)
    mg = mgain_ref[...]
    pad_one = jnp.sum(jnp.where(iota((24, 128), 0) == prow, padf, 0.0), axis=0, keepdims=True)
    gain_one = jnp.sum(jnp.where(iota((32, 128), 0) == s // 2, mg, 0.0), axis=0, keepdims=True)
    both = pad_one * gain_one
    half = jnp.where(s % 2 == 1, both[:, 64:], both[:, :64])
    half = jnp.broadcast_to(half, (16, 64)).astype(BF16)
    pq = nn(half, wq_ref[...])
    pkv = nn(half, wkv_ref[...])
    pad_sq = jnp.sum(jnp.sum(padf * padf, axis=1, keepdims=True), axis=0, keepdims=True)
    lane1 = iota((1, 128), 1)
    bounds = bnd_ref[...]
    count = jnp.sum(jnp.where(bounds < NY * NZ * L, 1.0, 0.0), axis=1, keepdims=True)
    last = jnp.zeros((1, 128), F32)
    for h in range(HEADS):
        last = jnp.where(lane1 == h, run_col[h][L - 1 : L, :], last)
        for t in range(3):
            last = jnp.where(lane1 == 16 + 4 * t + h, rem_row[h : h + 1, t : t + 1], last)
    rows = [
        pq[0:1, 0:128],
        pq[0:1, 128:256],
        pkv[0:1, 0:128],
        pq[0:1, 256:384],
        pq[0:1, 384:512],
        pkv[0:1, 128:256],
        jnp.where(lane1 == z, count, 0.0),
        last,
    ]
    for i, row in enumerate(rows):
        ebuf[1 + z, i : i + 1, 256:384] = row

    pl.semaphore_wait(barrier, jnp.where(z == NZ - 1, 21 + NZ, 21))

    send_all(SCAN1, z, at_z, lambda p: s1_send.at[p], s1.at[z])
    send_all(EDGE, z, at_z, lambda p: ebuf.at[1 + z], ebuf.at[1 + z])

    def prev_copy(p):
        return pltpu.make_async_remote_copy(
            src_ref=ebuf.at[1 + z],
            dst_ref=ebuf.at[0],
            send_sem=prev_send.at[p],
            recv_sem=prev_recv.at[0],
            device_id=(lax.rem(y + 1, NY) * NZ + p, hd),
            device_id_type=MESH,
        )

    @pl.when(z == NZ - 1)
    def _():
        for p in range(NZ):
            prev_copy(p).start()

    s1[z] = s1_send[z]

    def w0_parts(yp):
        rg = lax.rem(yp, 4)
        ch = yp // 4
        r = pl.ds(pl.multiple_of(16 * rg, 16), 16)
        return (
            (
                wq_hbm.at[r, pl.ds(pl.multiple_of(256 * ch, 256), 256)],
                wbuf.at[ch, y, z, rg, :, pl.ds(0, 256)],
            ),
            (
                wkv_hbm.at[r, pl.ds(pl.multiple_of(128 * ch, 128), 128)],
                wbuf.at[ch, y, z, rg, :, pl.ds(256, 128)],
            ),
        )

    def w0_copies():
        copies = []
        for d in FAR_FIRST:
            yp = lax.rem(y + d, NY)
            for i, (src, dst) in enumerate(w0_parts(yp)):
                copies.append(
                    pltpu.make_async_remote_copy(
                        src_ref=src,
                        dst_ref=dst,
                        send_sem=w0_send.at[i, d],
                        recv_sem=w0_recv.at[i, y],
                        device_id=at_y(yp),
                        device_id_type=MESH,
                    )
                )
        return copies

    @pl.when(y < 2)
    def _():
        for copy in w0_copies():
            copy.start()
        for i, (src, dst) in enumerate(w0_parts(y)):
            pltpu.make_async_copy(src, dst, w0_recv.at[i, y]).start()

    for copy in load[10:]:
        copy.start()

    l_c.wait()
    cm = c_ref[...]
    affinity = jnp.where(causal, nt(cm, bm), 0.0)
    mix = []
    for h in range(HEADS):
        spread = jnp.where(causal, run_col[h] - run_row[h : h + 1, :], 0.0)
        mix.append((jnp.exp(spread) * (affinity * gain_row[h : h + 1, :])).astype(BF16))

    recv_all(EDGE, z, at_z, lambda p: ebuf.at[1 + p])
    prev_copy(0).wait_recv()
    edges = ebuf[...]
    tiles = edges[1:, :, 256:384]
    stats_y[y] = jnp.sum(tiles, axis=0)
    send_all(STATS_Y, y, at_y, lambda p: stats_y.at[y], stats_y.at[y])

    for b in range(2):
        for i, (src, dst) in enumerate(w0_parts(y)):
            rg = lax.rem(y, 4)
            ch = y // 4
            cols = pl.ds(0, 256) if i == 0 else pl.ds(256, 128)
            slot = wbuf.at[ch, b, z, rg, :, cols]
            pltpu.make_async_copy(slot, slot, w0_recv.at[i, b]).wait()
    rg_me = lax.rem(y, 4)
    ch_me = y // 4
    send_all(
        W_AZ, z, at_z, lambda p: wbuf.at[ch_me, 0, z, rg_me], wbuf.at[ch_me, 0, z, rg_me]
    )
    send_all(
        W_BY, y, at_y, lambda p: wbuf.at[ch_me, 1, z, rg_me], wbuf.at[ch_me, 1, z, rg_me]
    )

    before_rows = pltpu.roll(ebuf[z, :, 0:256], 5, 0)
    lead = (iota((8, 256), 0) < 3) & (s > 0)
    top_rows = silu(summed[0:8] + jnp.where(lead, before_rows, 0.0)).astype(BF16).astype(F32)
    conv_f = jnp.concatenate([top_rows, conv_own[8:]], axis=0)
    conv = conv_f.astype(BF16)

    within = []
    zero = jnp.zeros((), BF16)
    for i in range(2):
        pair = conv[:, 128 * i : 128 * (i + 1)]
        stacked = jnp.concatenate(
            [jnp.where(first, pair, zero), jnp.where(first, zero, pair)], axis=0
        )
        within.append(nn(jnp.concatenate([mix[2 * i], mix[2 * i + 1]], axis=1), stacked))
    l_skip.wait()
    skip_v = skip_ref[...]
    skip = jnp.zeros((1, 256), F32)
    head_of = iota((1, 256), 1) // HP
    for h in range(HEADS):
        skip = jnp.where(head_of == h, skip_v[:, h : h + 1], skip)
    mixed_near = jnp.concatenate(within, axis=1) + skip * conv_f
    exp_run = jnp.exp(run_x)
    l_gate.wait()
    gate = silu(gate_ref[...].astype(F32))

    col = iota((128, 1024), 1)
    part_of = col // 256
    lane_of = lax.rem(col, 256) // HP + jnp.where(part_of > 0, 12 + 4 * part_of, 0)
    spread_head = jnp.where(iota((128, 1024), 0) == lane_of, 1.0, 0.0).astype(F32)
    by_head = nn(tiles[:, 7, :], spread_head, EXACT)
    lz = by_head[:, 0:256]

    nothing = (iota((8, 256), 0) + y) == 0
    edge_x, edge_b = [], []
    for t in range(3):
        earlier = jnp.where(nothing, 0.0, edges[0:8, 3 + t, 0:256])
        conv_t = silu(edges[1:, t, 0:256] + earlier).astype(BF16).astype(F32)
        edge_x.append(conv_t * by_head[:, 256 * (1 + t) : 256 * (2 + t)])
        edge_b.append(edges[1:, 6 + t // 2, 128 * (t % 2) : 128 * (t % 2 + 1)])
    edge_x = jnp.concatenate(edge_x, axis=0).astype(BF16)
    edge_b = jnp.concatenate(edge_b, axis=0).astype(BF16)
    pick_n = jnp.where(si == 16 * z + lax.rem(ti, 16), 1.0, 0.0).astype(BF16)
    spots = nt(pick_n, edge_b)
    same = iota((L, 24), 0) // 16 == lax.rem(iota((L, 24), 1), 8)
    added = nn(jnp.where(same, spots, 0.0).astype(BF16), edge_x).reshape(8, 16, 256)
    recv_all(SCAN1, z, at_z, lambda p: s1.at[p])
    acc = jnp.zeros((16, 256), F32)
    cum = jnp.zeros((1, 256), F32)
    before, cums = [], []
    for j in range(NZ):
        before.append(acc)
        cums.append(cum)
        acc = jnp.exp(lz[j : j + 1, :]) * acc + (s1[j].astype(F32) + added[j])
        cum = cum + lz[j : j + 1, :]
    s2[y] = acc.astype(BF16)
    send_all(SCAN2, y, at_y, lambda p: s2.at[y], s2.at[y])

    def block_a(p, lo=0, n=8):
        return wbuf.at[p // 4, 0, pl.ds(lo, n), lax.rem(p, 4)]

    def block_b(p, lo=0, n=2):
        return wbuf.at[pl.ds(lo, n), 1, p]

    def rings(step, wait):
        for ex, me, where, block, whole in (
            (RING_A, y, at_y, block_a, 8),
            (RING_B, z, at_z, block_b, 2),
        ):
            for way in range(2):
                ahead = lax.rem(me + (1 if way == 0 else 7), 8)
                moved = step + (1 if wait else 0)
                of = lax.rem(me + (8 - moved if way == 0 else moved), 8)
                if step == 3:
                    part = block(of, way * whole // 2, whole // 2)
                else:
                    part = block(of)
                copy = pltpu.make_async_remote_copy(
                    src_ref=part,
                    dst_ref=part,
                    send_sem=send_sem.at[ex, 2 * step + way],
                    recv_sem=recv_sem.at[ex, 2 * step + way],
                    device_id=where(ahead),
                    device_id_type=MESH,
                )
                if wait:
                    copy.wait_recv()
                else:
                    copy.start()
                    pending.append(copy)

    recv_all(W_AZ, z, at_z, lambda p: wbuf.at[ch_me, 0, p, rg_me])
    recv_all(W_BY, y, at_y, lambda p: wbuf.at[p // 4, 1, z, lax.rem(p, 4)])
    rings(0, False)

    recv_all(STATS_Y, y, at_y, lambda p: stats_y.at[p])
    ytiles = stats_y[...]
    pad_total = jnp.sum(ytiles, axis=0)
    ly = nn(ytiles[:, 7, :], spread_head[:, 0:256], EXACT)

    recv_all(SCAN2, y, at_y, lambda p: s2.at[p])
    rows_before = jnp.zeros((16, 256), F32)
    for j in range(NY - 1):
        longer = jnp.exp(ly[j : j + 1, :]) * rows_before + s2[j].astype(F32)
        rows_before = jnp.where(j < y, longer, rows_before)
    for j in range(NZ):
        s3_send[j] = (before[j] + jnp.exp(cums[j]) * rows_before).astype(BF16)
    send_all(SCAN3, z, at_z, lambda p: s3_send.at[p], s3.at[z])
    s3[z] = s3_send[z]

    rings(0, True)
    rings(1, False)

    l_ngain.wait()
    bnd = bounds - s * L
    byte_at = iota((L, CAP), 0)
    slot_at = iota((L, CAP), 1)
    usable = bounds < NY * NZ * L
    picker = jnp.where((byte_at == bnd) & usable, 1.0, 0.0).astype(BF16)
    upto = jnp.where((bnd <= byte_at) & usable, 1.0, 0.0)
    newest = jnp.sum(upto, axis=1, keepdims=True) - 1.0
    spreader = jnp.where(slot_at.astype(F32) == newest, 1.0, 0.0).astype(BF16)
    l_res.wait()
    res = res_ref[...]
    res_span = tn(picker, res)

    lane = iota((CAP, 128), 1)
    counts = ytiles[:, 6, :]
    lane8 = iota((8, 128), 1)
    ahead = (lane8 < NZ) & (iota((8, 128), 0) * NZ + lane8 < s)
    offset = jnp.sum(jnp.where(ahead, counts, 0.0), axis=0, keepdims=True)
    offset = jnp.sum(offset, axis=1, keepdims=True)
    place = iota((CAP, 128), 0).astype(F32) + offset
    freq = jnp.exp(
        lax.rem(lane, HD // 2).astype(F32) * (-2.0 * math.log(THETA) / HD)
    )
    angle = place * freq
    cosine = jnp.cos(angle)
    sine = jnp.where(lane < HD // 2, -jnp.sin(angle), jnp.sin(angle))

    recv_all(SCAN3, z, at_z, lambda p: s3.at[p])
    entering = nn(cm, s3[...].reshape(128, 256)) * exp_run
    gated = (mixed_near + entering) * gate
    mean_sq = jnp.sum(gated * gated, axis=1, keepdims=True) * (1.0 / 256)
    normed = (gated * lax.rsqrt(mean_sq + EPSILON) * ngain_ref[...]).astype(BF16)
    l_mo.wait()
    picked = tn(picker, normed).astype(BF16)
    span_part = nn(picked, mo_ref[...]).astype(BF16)
    for j in range(NHD):
        sp_send[j] = span_part[:, 128 * j : 128 * (j + 1)]
    send_all(SPAN_RS, hd, at_h, lambda p: sp_send.at[p], sp_recv.at[hd])
    sp_recv[hd] = sp_send[hd]

    rings(1, True)
    rings(2, False)

    enc_part = nn(normed, mo_ref[...]).astype(BF16)
    for j in range(NHD):
        en_send[j] = enc_part[:, 128 * j : 128 * (j + 1)]
    en_recv[hd] = en_send[hd]

    recv_all(SPAN_RS, hd, at_h, lambda p: sp_recv.at[p])
    span_share = (res_span + jnp.sum(sp_recv[...].astype(F32), axis=0)).astype(BF16)
    ag[hd] = span_share
    send_all(SPAN_AG, hd, at_h, lambda p: ag.at[hd], ag.at[hd])

    rings(2, True)
    rings(3, False)

    key = iota((512, 128), 0)
    key_y = lax.rem(y + 16 - (key // 128) * sy, NY)
    key_z = lax.rem(z + 16 - lax.rem(key // CAP, 4) * sz, NZ)
    expand = jnp.where(iota((512, 128), 1) == key_z, 1.0, 0.0).astype(BF16)
    per_row = nt(expand, jnp.concatenate([ytiles[:, 6, :], ytiles[:, 6, :]], axis=0).astype(BF16))
    lane16 = iota((512, 16), 1)
    key_count = jnp.sum(
        jnp.where(lane16 == lax.rem(y + 16 - (iota((512, 16), 0) // 128) * sy, NY), per_row, 0.0),
        axis=1,
        keepdims=True,
    )
    key_slot = lax.rem(key, CAP)
    key_rank = (key_y * NZ + key_z) * CAP + key_slot
    key_rank = jnp.where(key_slot.astype(F32) < key_count, key_rank, NY * NZ * CAP)
    key_ranks[...] = key_rank
    query = iota((1, 512), 1)
    query_rank = (
        ((y - py + query // 256) * NZ + z - pz + lax.rem(query // 128, 2)) * CAP
        + lax.rem(query, CAP)
    )

    recv_all(SPAN_AG, hd, at_h, lambda p: ag.at[p])
    sq = jnp.zeros((CAP, 1), F32)
    pieces = []
    for j in range(NHD):
        piece = ag[j].astype(F32)
        sq = sq + jnp.sum(piece * piece, axis=1, keepdims=True)
        pieces.append((piece * mg[j : j + 1, :]).astype(BF16))
    scale = lax.rsqrt((sq + pad_sq) * (1.0 / D_MAIN) + EPSILON)
    span_x = jnp.concatenate(pieces, axis=1)
    rings(3, True)
    proj = [nn(span_x, wbuf[ch].reshape(1024, 384)) for ch in range(2)]

    def column(i):
        part = proj[i // 3][:, 128 * (i % 3) : 128 * (i % 3 + 1)]
        return (part + pad_total[i : i + 1, :]) * scale

    def rotate(v):
        return (v * cosine + pltpu.roll(v, HD // 2, 1) * sine).astype(BF16)

    kvbuf[0, 0, 0] = rotate(column(2))
    kvbuf[0, 0, 1] = column(5).astype(BF16)

    def kv_copy(i, j):
        return pltpu.make_async_remote_copy(
            src_ref=kvbuf.at[0, 0],
            dst_ref=kvbuf.at[i, j],
            send_sem=kv_sem.at[0, 4 * i + j],
            recv_sem=kv_sem.at[1, 4 * i + j],
            device_id=at_slot(i, j),
            device_id_type=MESH,
        )

    kv_copies = [kv_copy(i, j) for i, j in SLOTS]
    for copy in kv_copies:
        copy.start()
        pending.append(copy)
    mine = 2 * py + pz
    qbuf[mine] = jnp.concatenate([rotate(column(i)) for i in (0, 1, 3, 4)], axis=0)

    def group_copy(i, e, src, dst):
        return pltpu.make_async_remote_copy(
            src_ref=src,
            dst_ref=dst,
            send_sem=group_sem.at[0, i, e],
            recv_sem=group_sem.at[1, i, e],
            device_id=member(e)[0],
            device_id_type=MESH,
        )

    for e in range(1, 4):
        copy = group_copy(0, e, qbuf.at[mine], qbuf.at[mine])
        copy.start()
        pending.append(copy)

    send_all(ENC_RS, hd, at_h, lambda p: en_send.at[p], en_recv.at[hd])

    for e in range(1, 4):
        slot = qbuf.at[member(e)[1]]
        group_copy(0, e, slot, slot).wait_recv()
    for copy in kv_copies:
        copy.wait_recv()

    kv = kvbuf[...]
    keys = kv[:, :, 0].reshape(512, HD)
    values = kv[:, :, 1].reshape(512, HD)
    ranks = key_ranks[...]
    unit = 1.0 / math.sqrt(HD)
    for m in range(4):
        scores = nt(keys, qbuf[m])
        allowed = ranks <= query_rank[:, 128 * m : 128 * (m + 1)]
        scores = jnp.where(allowed, scores * unit, -1e30)
        top = jnp.max(scores, axis=0, keepdims=True)
        weights = jnp.exp(scores - top)
        o_send[m] = tn(values, weights.astype(BF16)).astype(BF16)
        m_send[m, 0:1, :] = top
        m_send[m, 1:2, :] = jnp.sum(weights, axis=0, keepdims=True)

    for e in range(1, 4):
        place_e = member(e)[1]
        for i, (src, dst) in enumerate(((o_send, o_recv), (m_send, m_recv))):
            copy = group_copy(1 + i, e, src.at[place_e], dst.at[e])
            copy.start()
            pending.append(copy)
    o_recv[0] = o_send[mine]
    m_recv[0] = m_send[mine]

    for e in range(1, 4):
        group_copy(1, e, o_recv.at[e], o_recv.at[e]).wait_recv()
        group_copy(2, e, m_recv.at[e], m_recv.at[e]).wait_recv()

    tops = m_recv[:, 0, :]
    highest = jnp.max(tops, axis=0, keepdims=True)
    shrink = jnp.exp(tops - highest)
    total = jnp.sum(shrink * m_recv[:, 1, :], axis=0, keepdims=True)
    summed_o = jnp.zeros((HD, 128), F32)
    for e in range(4):
        summed_o = summed_o + shrink[e : e + 1, :] * o_recv[e].astype(F32)
    attended = (summed_o / total).T.astype(BF16)

    l_mw.wait()
    att = jnp.concatenate([attended[CAP * i : CAP * (i + 1), :] for i in range(4)], axis=1)
    main_part = nn(att, mw_ref[...]).astype(BF16)
    for j in range(NHD):
        mn_send[j] = main_part[:, 128 * j : 128 * (j + 1)]
    send_all(MAIN_RS, hd, at_h, lambda p: mn_send.at[p], mn_recv.at[hd])
    mn_recv[hd] = mn_send[hd]
    recv_all(ENC_RS, hd, at_h, lambda p: en_recv.at[p])
    encoded = (res.astype(F32) + jnp.sum(en_recv[...].astype(F32), axis=0)).astype(BF16)

    recv_all(MAIN_RS, hd, at_h, lambda p: mn_recv.at[p])
    main_rows = (span_share.astype(F32) + jnp.sum(mn_recv[...].astype(F32), axis=0)).astype(BF16)
    out_ref[...] = (encoded.astype(F32) + nn(spreader, main_rows)).astype(BF16)

    for copy in pending:
        copy.wait_send()

    @pl.when(y < 2)
    def _():
        for copy in w0_copies():
            copy.wait_send()

    @pl.when(z == NZ - 1)
    def _():
        for p in range(NZ):
            prev_copy(p).wait_send()


def shards(
    byte_stream,
    gate_stream,
    conv_weight,
    state_write,
    state_read,
    step_size,
    decay_coef,
    skip_gain,
    norm_gain,
    mixer_out,
    residual,
    boundaries,
    span_counts,
    span_offsets,
    pad_vector,
    main_gain,
    query_weight,
    key_value_weight,
    main_out_weight,
):
    far = pl.BlockSpec(memory_space=pl.ANY)
    near = pl.BlockSpec(memory_space=pltpu.VMEM)
    vm = pltpu.VMEM
    dma = pltpu.SemaphoreType.DMA
    return pl.pallas_call(
        kernel,
        out_shape=pltpu.VMEM((L, 128), BF16),
        in_specs=[far] * 17,
        out_specs=near,
        scratch_shapes=[
            vm((4, 256), F32),
            vm((HEADS, L), F32),
            vm((1, HEADS), F32),
            vm((1, HEADS), F32),
            vm((1, 256), F32),
            vm((1, CAP), jnp.int32),
            vm((24, 128), BF16),
            vm((32, 128), F32),
            vm((L, 256), BF16),
            vm((L, 256), BF16),
            vm((L, 128), BF16),
            vm((L, 128), BF16),
            vm((256, 1024), BF16),
            vm((L, 128), BF16),
            vm((64, 512), BF16),
            vm((64, 256), BF16),
            vm((512, 1024), BF16),
            vm((L + 16, 256), F32),
            vm((9, 8, 384), F32),
            vm((8, 8, 128), F32),
            vm((2, 2, 8, 4, 16, 384), BF16),
            vm((8, 16, 256), BF16),
            vm((8, 16, 256), BF16),
            vm((8, 16, 256), BF16),
            vm((8, 16, 256), BF16),
            vm((8, 16, 256), BF16),
            vm((8, CAP, 128), BF16),
            vm((8, CAP, 128), BF16),
            vm((8, CAP, 128), BF16),
            vm((8, L, 128), BF16),
            vm((8, L, 128), BF16),
            vm((4, 4, 2, CAP, 128), BF16),
            vm((4, 128, 128), BF16),
            vm((512, 128), jnp.int32),
            vm((4, 128, 128), BF16),
            vm((4, 8, 128), F32),
            vm((4, 128, 128), BF16),
            vm((4, 8, 128), F32),
            vm((8, CAP, 128), BF16),
            vm((8, CAP, 128), BF16),
            dma((17,)),
            dma((8,)),
            dma((1,)),
            dma((2, 8)),
            dma((2, 2)),
            dma((2, 16)),
            dma((2, 3, 4)),
            dma((N_EX, 8)),
            dma((N_EX, 8)),
        ],
        compiler_params=pltpu.CompilerParams(
            collective_id=0, has_side_effects=True, vmem_limit_bytes=56 * 1024 * 1024
        ),
        cost_estimate=pl.CostEstimate(flops=10**9, bytes_accessed=4 * 10**6, transcendentals=10**6),
    )(
        byte_stream,
        gate_stream,
        conv_weight,
        state_write,
        state_read,
        step_size.T,
        decay_coef.reshape(1, HEADS),
        skip_gain.reshape(1, HEADS),
        norm_gain.reshape(1, 256),
        mixer_out,
        residual,
        boundaries,
        pad_vector.reshape(24, 128),
        main_gain.reshape(32, 128),
        query_weight,
        key_value_weight,
        main_out_weight,
    )


def solution(mesh):
    in_specs = (
        P("seq", "head"),
        P("seq", "head"),
        P(None, "head"),
        P("seq", None),
        P("seq", None),
        P("seq", "head"),
        P("head"),
        P("head"),
        P("head"),
        P("head", None),
        P("seq", None),
        P("seq", None),
        P("seq"),
        P("seq"),
        P(),
        P(),
        P("seq", "head"),
        P("seq", "head"),
        P("head", None),
    )
    out_specs = P("seq", "head")
    return jax.shard_map(shards, mesh=mesh, in_specs=in_specs, out_specs=out_specs, check_vma=False)
```

```python
import functools
import math

import jax
import jax.numpy as jnp
from jax import lax
from jax.experimental import pallas as pl
from jax.experimental.pallas import tpu as pltpu
from jax.sharding import PartitionSpec as P

F32 = jnp.float32
BF16 = jnp.bfloat16
MESH = pl.DeviceIdType.MESH
EXACT = lax.Precision.HIGHEST

NY = 8
NZ = 8
NHD = 8
L = 128
HEADS = 4
HP = 64
CAP = 32
HD = 128
D_MAIN = 4096
THETA = 500000.0
EPSILON = 1e-05
FAR_FIRST = (4, 3, 5, 2, 6, 1, 7)
SLOTS = sorted(((i, j) for i in range(4) for j in range(4) if i + j > 0), key=lambda t: -t[0] - t[1])

(
    EDGE,
    STATS_Y,
    W_AZ,
    W_BY,
    RING_A,
    RING_B,
    SCAN1,
    SCAN2,
    SCAN3,
    SPAN_RS,
    SPAN_AG,
    ENC_RS,
    MAIN_RS,
    N_EX,
) = range(14)


def nn(a, b, precision=None):
    return lax.dot_general(
        a, b, (((1,), (0,)), ((), ())), precision=precision, preferred_element_type=F32
    )


def nt(a, b, precision=None):
    return lax.dot_general(
        a, b, (((1,), (1,)), ((), ())), precision=precision, preferred_element_type=F32
    )


def tn(a, b, precision=None):
    return lax.dot_general(
        a, b, (((0,), (0,)), ((), ())), precision=precision, preferred_element_type=F32
    )


def iota(shape, dim):
    return lax.broadcasted_iota(jnp.int32, shape, dim)


def silu(v):
    return v / (1.0 + jnp.exp(-v))


def one_minus_exp(u):
    series = u * (
        1.0
        - u
        * (
            1.0 / 2
            - u * (1.0 / 6 - u * (1.0 / 24 - u * (1.0 / 120 - u * (1.0 / 720 - u / 5040))))
        )
    )
    return jnp.where(u < 0.3, series, 1.0 - jnp.exp(-u))


def kernel(
    x_hbm,
    gate_hbm,
    convw_hbm,
    b_hbm,
    c_hbm,
    step_hbm,
    decay_hbm,
    skip_hbm,
    ngain_hbm,
    mo_hbm,
    res_hbm,
    bnd_hbm,
    pad_hbm,
    mgain_hbm,
    wq_hbm,
    wkv_hbm,
    mw_hbm,
    out_ref,
    convw_ref,
    step_ref,
    decay_ref,
    skip_ref,
    ngain_ref,
    bnd_ref,
    pad_ref,
    mgain_ref,
    x_ref,
    gate_ref,
    b_ref,
    c_ref,
    mo_ref,
    res_ref,
    wq_ref,
    wkv_ref,
    mw_ref,
    ext,
    ebuf,
    stats_y,
    wbuf,
    s1_send,
    s1,
    s2,
    s3_send,
    s3,
    sp_send,
    sp_recv,
    ag,
    en_send,
    en_recv,
    kvbuf,
    qbuf,
    key_ranks,
    o_send,
    m_send,
    o_recv,
    m_recv,
    mn_send,
    mn_recv,
    local_sem,
    prev_send,
    prev_recv,
    w0_send,
    w0_recv,
    kv_sem,
    group_sem,
    send_sem,
    recv_sem,
):
    s = lax.axis_index("seq")
    hd = lax.axis_index("head")
    y = s // NZ
    z = s % NZ

    def at_z(p):
        return (y * NZ + p, hd)

    def at_y(p):
        return (p * NZ + z, hd)

    def at_h(p):
        return (s, p)

    py, pz = lax.rem(y + hd, 2), lax.rem(z + hd, 2)
    sy, sz = 1 - 2 * py, 1 - 2 * pz

    def at_slot(i, j):
        yc = lax.rem(y + 8 + (0, -1, 2, -3)[i] * sy, NY)
        zc = lax.rem(z + 8 + (0, -1, 2, -3)[j] * sz, NZ)
        return (yc * NZ + zc, hd)

    def member(e):
        yc = lax.rem(y + 8 + sy, NY) if e // 2 else y
        zc = lax.rem(z + 8 + sz, NZ) if e % 2 else z
        return (yc * NZ + zc, hd), 2 * lax.rem(yc + hd, 2) + lax.rem(zc + hd, 2)

    barrier = pltpu.get_barrier_semaphore()
    greet = [(lax.rem(y + NY - 1, NY) * NZ + NZ - 1, hd)]
    for d in range(1, 8):
        greet += [at_z(lax.rem(z + d, NZ)), at_y(lax.rem(y + d, NY)), at_h(lax.rem(hd + d, NHD))]
    for to in greet:
        pl.semaphore_signal(barrier, inc=1, device_id=to, device_id_type=MESH)

    loads = [
        (step_hbm, step_ref),
        (decay_hbm, decay_ref),
        (x_hbm, x_ref),
        (convw_hbm, convw_ref),
        (b_hbm, b_ref),
        (wq_hbm, wq_ref),
        (wkv_hbm, wkv_ref),
        (pad_hbm, pad_ref),
        (mgain_hbm, mgain_ref),
        (bnd_hbm, bnd_ref),
        (c_hbm, c_ref),
        (gate_hbm, gate_ref),
        (skip_hbm, skip_ref),
        (ngain_hbm, ngain_ref),
        (res_hbm.at[:, pl.ds(pl.multiple_of(hd * 128, 128), 128)], res_ref),
        (mo_hbm, mo_ref),
        (mw_hbm, mw_ref),
    ]
    load = [pltpu.make_async_copy(a, b, local_sem.at[i]) for i, (a, b) in enumerate(loads)]
    for copy in load[:10]:
        copy.start()
    l_step, l_decay, l_x, l_convw, l_b, l_wq, l_wkv, l_pad, l_mgain, l_bnd = load[:10]
    l_c, l_gate, l_skip, l_ngain, l_res, l_mo, l_mw = load[10:]

    pending = []

    def send_all(ex, me, where, src, dst):
        for d in FAR_FIRST:
            p = lax.rem(me + d, 8)
            copy = pltpu.make_async_remote_copy(
                src_ref=src(p),
                dst_ref=dst,
                send_sem=send_sem.at[ex, d],
                recv_sem=recv_sem.at[ex, me],
                device_id=where(p),
                device_id_type=MESH,
            )
            copy.start()
            pending.append(copy)

    def recv_all(ex, me, where, slot):
        for d in range(1, 8):
            p = lax.rem(me + 8 - d, 8)
            pltpu.make_async_remote_copy(
                src_ref=slot(p),
                dst_ref=slot(p),
                send_sem=send_sem.at[ex, d],
                recv_sem=recv_sem.at[ex, p],
                device_id=where(p),
                device_id_type=MESH,
            ).wait_recv()

    l_step.wait()
    l_decay.wait()
    dec = decay_ref[...]
    row4 = iota((HEADS, L), 0)
    coef = jnp.zeros((HEADS, L), F32)
    for h in range(HEADS):
        coef = jnp.where(row4 == h, dec[:, h : h + 1], coef)
    rate = step_ref[...] * coef
    log_decay = -rate
    gain_row = jnp.sqrt(one_minus_exp(2.0 * rate))
    ti = iota((L, L), 0)
    si = iota((L, L), 1)
    causal = ti >= si
    tri = jnp.where(causal, 1.0, 0.0).astype(F32)
    run_row = nt(log_decay, tri, EXACT)
    run_col = [
        nt(tri, jnp.broadcast_to(log_decay[h : h + 1, :], (L, L)), EXACT) for h in range(HEADS)
    ]
    rem_row = jnp.exp(run_row[:, L - 1 : L] - run_row) * gain_row
    first = si < HP
    eye = jnp.where(ti == si, 1.0, 0.0).astype(BF16)
    top = ti < HP
    rem_x = [
        nt(
            eye,
            jnp.where(
                top,
                jnp.broadcast_to(rem_row[2 * i : 2 * i + 1, :], (L, L)),
                jnp.broadcast_to(rem_row[2 * i + 1 : 2 * i + 2, :], (L, L)),
            ).astype(BF16),
        )
        for i in range(2)
    ]
    run_x = jnp.concatenate(
        [jnp.where(first, run_col[2 * i], run_col[2 * i + 1]) for i in range(2)], axis=1
    )

    l_x.wait()
    l_convw.wait()
    l_b.wait()
    ext[0:8, :] = jnp.zeros((8, 256), F32)
    ext[8 : 8 + L, :] = x_ref[...].astype(F32)
    ext[8 + L :, :] = jnp.zeros((8, 256), F32)
    cw = convw_ref[...]
    summed = cw[0:1, :] * ext[5 : 13 + L, :]
    for k in range(1, 4):
        summed = summed + cw[k : k + 1, :] * ext[5 + k : 13 + k + L, :]
    conv_own = silu(summed[:L]).astype(BF16).astype(F32)

    bm = b_ref[...]
    inner = iota((L, 256), 0) >= 3
    weighted = jnp.where(inner, conv_own * jnp.concatenate(rem_x, axis=1), 0.0).astype(BF16)
    state = tn(bm, weighted).astype(BF16)
    s1_send[...] = state.reshape(8, 16, 256)
    head_b = bm[0:16, :].astype(F32)
    ebuf[1 + z, 0:3, 0:256] = summed[0:3]
    ebuf[1 + z, 3:6, 0:256] = summed[L : L + 3]
    ebuf[1 + z, 6:7, 0:128] = head_b[0:1, :]
    ebuf[1 + z, 6:7, 128:256] = head_b[1:2, :]
    ebuf[1 + z, 7:8, 0:128] = head_b[2:3, :]
    ebuf[1 + z, 7:8, 128:256] = jnp.zeros((1, 128), F32)

    l_wq.wait()
    l_wkv.wait()
    l_pad.wait()
    l_mgain.wait()
    l_bnd.wait()
    prow = s // 2 - 8
    padf = pad_ref[...].astype(F32)
    mg = mgain_ref[...]
    pad_one = jnp.sum(jnp.where(iota((24, 128), 0) == prow, padf, 0.0), axis=0, keepdims=True)
    gain_one = jnp.sum(jnp.where(iota((32, 128), 0) == s // 2, mg, 0.0), axis=0, keepdims=True)
    both = pad_one * gain_one
    half = jnp.where(s % 2 == 1, both[:, 64:], both[:, :64])
    half = jnp.broadcast_to(half, (16, 64)).astype(BF16)
    pq = nn(half, wq_ref[...])
    pkv = nn(half, wkv_ref[...])
    pad_sq = jnp.sum(jnp.sum(padf * padf, axis=1, keepdims=True), axis=0, keepdims=True)
    lane1 = iota((1, 128), 1)
    bounds = bnd_ref[...]
    count = jnp.sum(jnp.where(bounds < NY * NZ * L, 1.0, 0.0), axis=1, keepdims=True)
    last = jnp.zeros((1, 128), F32)
    for h in range(HEADS):
        last = jnp.where(lane1 == h, run_col[h][L - 1 : L, :], last)
        for t in range(3):
            last = jnp.where(lane1 == 16 + 4 * t + h, rem_row[h : h + 1, t : t + 1], last)
    rows = [
        pq[0:1, 0:128],
        pq[0:1, 128:256],
        pkv[0:1, 0:128],
        pq[0:1, 256:384],
        pq[0:1, 384:512],
        pkv[0:1, 128:256],
        jnp.where(lane1 == z, count, 0.0),
        last,
    ]
    for i, row in enumerate(rows):
        ebuf[1 + z, i : i + 1, 256:384] = row

    pl.semaphore_wait(barrier, jnp.where(z == NZ - 1, 21 + NZ, 21))

    send_all(EDGE, z, at_z, lambda p: ebuf.at[1 + z], ebuf.at[1 + z])

    def prev_copy(p):
        return pltpu.make_async_remote_copy(
            src_ref=ebuf.at[1 + z],
            dst_ref=ebuf.at[0],
            send_sem=prev_send.at[p],
            recv_sem=prev_recv.at[0],
            device_id=(lax.rem(y + 1, NY) * NZ + p, hd),
            device_id_type=MESH,
        )

    @pl.when(z == NZ - 1)
    def _():
        for p in range(NZ):
            prev_copy(p).start()

    send_all(SCAN1, z, at_z, lambda p: s1_send.at[p], s1.at[z])
    s1[z] = s1_send[z]

    def w0_parts(yp):
        rg = lax.rem(yp, 4)
        ch = yp // 4
        r = pl.ds(pl.multiple_of(16 * rg, 16), 16)
        return (
            (
                wq_hbm.at[r, pl.ds(pl.multiple_of(256 * ch, 256), 256)],
                wbuf.at[ch, y, z, rg, :, pl.ds(0, 256)],
            ),
            (
                wkv_hbm.at[r, pl.ds(pl.multiple_of(128 * ch, 128), 128)],
                wbuf.at[ch, y, z, rg, :, pl.ds(256, 128)],
            ),
        )

    def w0_copies():
        copies = []
        for d in FAR_FIRST:
            yp = lax.rem(y + d, NY)
            for i, (src, dst) in enumerate(w0_parts(yp)):
                copies.append(
                    pltpu.make_async_remote_copy(
                        src_ref=src,
                        dst_ref=dst,
                        send_sem=w0_send.at[i, d],
                        recv_sem=w0_recv.at[i, y],
                        device_id=at_y(yp),
                        device_id_type=MESH,
                    )
                )
        return copies

    @pl.when(y < 2)
    def _():
        for copy in w0_copies():
            copy.start()
        for i, (src, dst) in enumerate(w0_parts(y)):
            pltpu.make_async_copy(src, dst, w0_recv.at[i, y]).start()

    for copy in load[10:]:
        copy.start()

    l_c.wait()
    cm = c_ref[...]
    affinity = jnp.where(causal, nt(cm, bm), 0.0)
    mix = []
    for h in range(HEADS):
        spread = jnp.where(causal, run_col[h] - run_row[h : h + 1, :], 0.0)
        mix.append((jnp.exp(spread) * (affinity * gain_row[h : h + 1, :])).astype(BF16))

    recv_all(EDGE, z, at_z, lambda p: ebuf.at[1 + p])
    prev_copy(0).wait_recv()
    edges = ebuf[...]
    tiles = edges[1:, :, 256:384]
    stats_y[y] = jnp.sum(tiles, axis=0)
    send_all(STATS_Y, y, at_y, lambda p: stats_y.at[y], stats_y.at[y])

    col = iota((128, 1024), 1)
    part_of = col // 256
    lane_of = lax.rem(col, 256) // HP + jnp.where(part_of > 0, 12 + 4 * part_of, 0)
    spread_head = jnp.where(iota((128, 1024), 0) == lane_of, 1.0, 0.0).astype(F32)
    by_head = nn(tiles[:, 7, :], spread_head, EXACT)
    lz = by_head[:, 0:256]

    nothing = (iota((8, 256), 0) + y) == 0
    edge_x, edge_b = [], []
    for t in range(3):
        earlier = jnp.where(nothing, 0.0, edges[0:8, 3 + t, 0:256])
        conv_t = silu(edges[1:, t, 0:256] + earlier).astype(BF16).astype(F32)
        edge_x.append(conv_t * by_head[:, 256 * (1 + t) : 256 * (2 + t)])
        edge_b.append(edges[1:, 6 + t // 2, 128 * (t % 2) : 128 * (t % 2 + 1)])
    edge_x = jnp.concatenate(edge_x, axis=0).astype(BF16)
    edge_b = jnp.concatenate(edge_b, axis=0).astype(BF16)
    pick_n = jnp.where(si == 16 * z + lax.rem(ti, 16), 1.0, 0.0).astype(BF16)
    spots = nt(pick_n, edge_b)
    same = iota((L, 24), 0) // 16 == lax.rem(iota((L, 24), 1), 8)
    added = nn(jnp.where(same, spots, 0.0).astype(BF16), edge_x).reshape(8, 16, 256)
    recv_all(SCAN1, z, at_z, lambda p: s1.at[p])
    acc = jnp.zeros((16, 256), F32)
    cum = jnp.zeros((1, 256), F32)
    before, cums = [], []
    for j in range(NZ):
        before.append(acc)
        cums.append(cum)
        acc = jnp.exp(lz[j : j + 1, :]) * acc + (s1[j].astype(F32) + added[j])
        cum = cum + lz[j : j + 1, :]
    s2[y] = acc.astype(BF16)
    send_all(SCAN2, y, at_y, lambda p: s2.at[y], s2.at[y])

    for b in range(2):
        for i, (src, dst) in enumerate(w0_parts(y)):
            rg = lax.rem(y, 4)
            ch = y // 4
            cols = pl.ds(0, 256) if i == 0 else pl.ds(256, 128)
            slot = wbuf.at[ch, b, z, rg, :, cols]
            pltpu.make_async_copy(slot, slot, w0_recv.at[i, b]).wait()
    rg_me = lax.rem(y, 4)
    ch_me = y // 4
    send_all(
        W_AZ, z, at_z, lambda p: wbuf.at[ch_me, 0, z, rg_me], wbuf.at[ch_me, 0, z, rg_me]
    )
    send_all(
        W_BY, y, at_y, lambda p: wbuf.at[ch_me, 1, z, rg_me], wbuf.at[ch_me, 1, z, rg_me]
    )

    before_rows = pltpu.roll(ebuf[z, :, 0:256], 5, 0)
    lead = (iota((8, 256), 0) < 3) & (s > 0)
    top_rows = silu(summed[0:8] + jnp.where(lead, before_rows, 0.0)).astype(BF16).astype(F32)
    conv_f = jnp.concatenate([top_rows, conv_own[8:]], axis=0)
    conv = conv_f.astype(BF16)

    within = []
    zero = jnp.zeros((), BF16)
    for i in range(2):
        pair = conv[:, 128 * i : 128 * (i + 1)]
        stacked = jnp.concatenate(
            [jnp.where(first, pair, zero), jnp.where(first, zero, pair)], axis=0
        )
        within.append(nn(jnp.concatenate([mix[2 * i], mix[2 * i + 1]], axis=1), stacked))
    l_skip.wait()
    skip_v = skip_ref[...]
    skip = jnp.zeros((1, 256), F32)
    head_of = iota((1, 256), 1) // HP
    for h in range(HEADS):
        skip = jnp.where(head_of == h, skip_v[:, h : h + 1], skip)
    mixed_near = jnp.concatenate(within, axis=1) + skip * conv_f
    exp_run = jnp.exp(run_x)
    l_gate.wait()
    gate = silu(gate_ref[...].astype(F32))

    def block_a(p, lo=0, n=8):
        return wbuf.at[p // 4, 0, pl.ds(lo, n), lax.rem(p, 4)]

    def block_b(p, lo=0, n=2):
        return wbuf.at[pl.ds(lo, n), 1, p]

    def rings(step, wait):
        for ex, me, where, block, whole in (
            (RING_A, y, at_y, block_a, 8),
            (RING_B, z, at_z, block_b, 2),
        ):
            for way in range(2):
                ahead = lax.rem(me + (1 if way == 0 else 7), 8)
                moved = step + (1 if wait else 0)
                of = lax.rem(me + (8 - moved if way == 0 else moved), 8)
                if step == 3:
                    part = block(of, way * whole // 2, whole // 2)
                else:
                    part = block(of)
                copy = pltpu.make_async_remote_copy(
                    src_ref=part,
                    dst_ref=part,
                    send_sem=send_sem.at[ex, 2 * step + way],
                    recv_sem=recv_sem.at[ex, 2 * step + way],
                    device_id=where(ahead),
                    device_id_type=MESH,
                )
                if wait:
                    copy.wait_recv()
                else:
                    copy.start()
                    pending.append(copy)

    recv_all(STATS_Y, y, at_y, lambda p: stats_y.at[p])
    ytiles = stats_y[...]
    pad_total = jnp.sum(ytiles, axis=0)
    ly = nn(ytiles[:, 7, :], spread_head[:, 0:256], EXACT)

    recv_all(SCAN2, y, at_y, lambda p: s2.at[p])
    rows_before = jnp.zeros((16, 256), F32)
    for j in range(NY - 1):
        longer = jnp.exp(ly[j : j + 1, :]) * rows_before + s2[j].astype(F32)
        rows_before = jnp.where(j < y, longer, rows_before)
    for j in range(NZ):
        s3_send[j] = (before[j] + jnp.exp(cums[j]) * rows_before).astype(BF16)
    send_all(SCAN3, z, at_z, lambda p: s3_send.at[p], s3.at[z])
    s3[z] = s3_send[z]

    l_ngain.wait()
    bnd = bounds - s * L
    byte_at = iota((L, CAP), 0)
    slot_at = iota((L, CAP), 1)
    usable = bounds < NY * NZ * L
    picker = jnp.where((byte_at == bnd) & usable, 1.0, 0.0).astype(BF16)
    upto = jnp.where((bnd <= byte_at) & usable, 1.0, 0.0)
    newest = jnp.sum(upto, axis=1, keepdims=True) - 1.0
    spreader = jnp.where(slot_at.astype(F32) == newest, 1.0, 0.0).astype(BF16)
    l_res.wait()
    res = res_ref[...]
    res_span = tn(picker, res)

    lane = iota((CAP, 128), 1)
    counts = ytiles[:, 6, :]
    lane8 = iota((8, 128), 1)
    ahead = (lane8 < NZ) & (iota((8, 128), 0) * NZ + lane8 < s)
    offset = jnp.sum(jnp.where(ahead, counts, 0.0), axis=0, keepdims=True)
    offset = jnp.sum(offset, axis=1, keepdims=True)
    place = iota((CAP, 128), 0).astype(F32) + offset
    freq = jnp.exp(
        lax.rem(lane, HD // 2).astype(F32) * (-2.0 * math.log(THETA) / HD)
    )
    angle = place * freq
    cosine = jnp.cos(angle)
    sine = jnp.where(lane < HD // 2, -jnp.sin(angle), jnp.sin(angle))

    recv_all(W_AZ, z, at_z, lambda p: wbuf.at[ch_me, 0, p, rg_me])
    recv_all(W_BY, y, at_y, lambda p: wbuf.at[p // 4, 1, z, lax.rem(p, 4)])
    rings(0, False)

    recv_all(SCAN3, z, at_z, lambda p: s3.at[p])
    entering = nn(cm, s3[...].reshape(128, 256)) * exp_run
    gated = (mixed_near + entering) * gate
    mean_sq = jnp.sum(gated * gated, axis=1, keepdims=True) * (1.0 / 256)
    normed = (gated * lax.rsqrt(mean_sq + EPSILON) * ngain_ref[...]).astype(BF16)
    l_mo.wait()
    picked = tn(picker, normed).astype(BF16)
    span_part = nn(picked, mo_ref[...]).astype(BF16)
    for j in range(NHD):
        sp_send[j] = span_part[:, 128 * j : 128 * (j + 1)]
    send_all(SPAN_RS, hd, at_h, lambda p: sp_send.at[p], sp_recv.at[hd])
    sp_recv[hd] = sp_send[hd]

    rings(0, True)
    rings(1, False)

    enc_part = nn(normed, mo_ref[...]).astype(BF16)
    for j in range(NHD):
        en_send[j] = enc_part[:, 128 * j : 128 * (j + 1)]
    en_recv[hd] = en_send[hd]

    rings(1, True)
    rings(2, False)

    recv_all(SPAN_RS, hd, at_h, lambda p: sp_recv.at[p])
    span_share = (res_span + jnp.sum(sp_recv[...].astype(F32), axis=0)).astype(BF16)
    ag[hd] = span_share
    send_all(SPAN_AG, hd, at_h, lambda p: ag.at[hd], ag.at[hd])

    rings(2, True)
    rings(3, False)

    key = iota((512, 128), 0)
    key_y = lax.rem(y + 16 - (key // 128) * sy, NY)
    key_z = lax.rem(z + 16 - lax.rem(key // CAP, 4) * sz, NZ)
    expand = jnp.where(iota((512, 128), 1) == key_z, 1.0, 0.0).astype(BF16)
    per_row = nt(expand, jnp.concatenate([ytiles[:, 6, :], ytiles[:, 6, :]], axis=0).astype(BF16))
    lane16 = iota((512, 16), 1)
    key_count = jnp.sum(
        jnp.where(lane16 == lax.rem(y + 16 - (iota((512, 16), 0) // 128) * sy, NY), per_row, 0.0),
        axis=1,
        keepdims=True,
    )
    key_slot = lax.rem(key, CAP)
    key_rank = (key_y * NZ + key_z) * CAP + key_slot
    key_rank = jnp.where(key_slot.astype(F32) < key_count, key_rank, NY * NZ * CAP)
    key_ranks[...] = key_rank
    query = iota((1, 512), 1)
    query_rank = (
        (
            lax.rem(y + 8 - py + query // 256, NY) * NZ
            + lax.rem(z + 8 - pz + lax.rem(query // 128, 2), NZ)
        )
        * CAP
        + lax.rem(query, CAP)
    )

    recv_all(SPAN_AG, hd, at_h, lambda p: ag.at[p])
    sq = jnp.zeros((CAP, 1), F32)
    pieces = []
    for j in range(NHD):
        piece = ag[j].astype(F32)
        sq = sq + jnp.sum(piece * piece, axis=1, keepdims=True)
        pieces.append((piece * mg[j : j + 1, :]).astype(BF16))
    scale = lax.rsqrt((sq + pad_sq) * (1.0 / D_MAIN) + EPSILON)
    span_x = jnp.concatenate(pieces, axis=1)
    rings(3, True)
    proj = [nn(span_x, wbuf[ch].reshape(1024, 384)) for ch in range(2)]

    def column(i):
        part = proj[i // 3][:, 128 * (i % 3) : 128 * (i % 3 + 1)]
        return (part + pad_total[i : i + 1, :]) * scale

    def rotate(v):
        return (v * cosine + pltpu.roll(v, HD // 2, 1) * sine).astype(BF16)

    kvbuf[0, 0, 0] = rotate(column(2))
    kvbuf[0, 0, 1] = column(5).astype(BF16)

    def kv_copy(i, j):
        return pltpu.make_async_remote_copy(
            src_ref=kvbuf.at[0, 0],
            dst_ref=kvbuf.at[i, j],
            send_sem=kv_sem.at[0, 4 * i + j],
            recv_sem=kv_sem.at[1, 4 * i + j],
            device_id=at_slot(i, j),
            device_id_type=MESH,
        )

    kv_copies = [kv_copy(i, j) for i, j in SLOTS]
    for copy in kv_copies:
        copy.start()
        pending.append(copy)
    mine = 2 * py + pz
    qbuf[mine] = jnp.concatenate([rotate(column(i)) for i in (0, 1, 3, 4)], axis=0)

    def group_copy(i, e, src, dst):
        return pltpu.make_async_remote_copy(
            src_ref=src,
            dst_ref=dst,
            send_sem=group_sem.at[0, i, e],
            recv_sem=group_sem.at[1, i, e],
            device_id=member(e)[0],
            device_id_type=MESH,
        )

    for e in range(1, 4):
        copy = group_copy(0, e, qbuf.at[mine], qbuf.at[mine])
        copy.start()
        pending.append(copy)

    send_all(ENC_RS, hd, at_h, lambda p: en_send.at[p], en_recv.at[hd])

    for e in range(1, 4):
        slot = qbuf.at[member(e)[1]]
        group_copy(0, e, slot, slot).wait_recv()
    for copy in kv_copies:
        copy.wait_recv()

    kv = kvbuf[...]
    keys = kv[:, :, 0].reshape(512, HD)
    values = kv[:, :, 1].reshape(512, HD)
    ranks = key_ranks[...]
    unit = 1.0 / math.sqrt(HD)
    for m in range(4):
        scores = nt(keys, qbuf[m])
        allowed = ranks <= query_rank[:, 128 * m : 128 * (m + 1)]
        scores = jnp.where(allowed, scores * unit, -1e30)
        top = jnp.max(scores, axis=0, keepdims=True)
        weights = jnp.exp(scores - top)
        o_send[m] = tn(values, weights.astype(BF16)).astype(BF16)
        m_send[m, 0:1, :] = top
        m_send[m, 1:2, :] = jnp.sum(weights, axis=0, keepdims=True)

    for e in range(1, 4):
        place_e = member(e)[1]
        for i, (src, dst) in enumerate(((o_send, o_recv), (m_send, m_recv))):
            copy = group_copy(1 + i, e, src.at[place_e], dst.at[e])
            copy.start()
            pending.append(copy)
    o_recv[0] = o_send[mine]
    m_recv[0] = m_send[mine]

    for e in range(1, 4):
        group_copy(1, e, o_recv.at[e], o_recv.at[e]).wait_recv()
        group_copy(2, e, m_recv.at[e], m_recv.at[e]).wait_recv()

    tops = m_recv[:, 0, :]
    highest = jnp.max(tops, axis=0, keepdims=True)
    shrink = jnp.exp(tops - highest)
    total = jnp.sum(shrink * m_recv[:, 1, :], axis=0, keepdims=True)
    summed_o = jnp.zeros((HD, 128), F32)
    for e in range(4):
        summed_o = summed_o + shrink[e : e + 1, :] * o_recv[e].astype(F32)
    attended = (summed_o / total).T.astype(BF16)

    l_mw.wait()
    att = jnp.concatenate([attended[CAP * i : CAP * (i + 1), :] for i in range(4)], axis=1)
    main_part = nn(att, mw_ref[...]).astype(BF16)
    for j in range(NHD):
        mn_send[j] = main_part[:, 128 * j : 128 * (j + 1)]
    send_all(MAIN_RS, hd, at_h, lambda p: mn_send.at[p], mn_recv.at[hd])
    mn_recv[hd] = mn_send[hd]
    recv_all(ENC_RS, hd, at_h, lambda p: en_recv.at[p])
    encoded = (res.astype(F32) + jnp.sum(en_recv[...].astype(F32), axis=0)).astype(BF16)

    recv_all(MAIN_RS, hd, at_h, lambda p: mn_recv.at[p])
    main_rows = (span_share.astype(F32) + jnp.sum(mn_recv[...].astype(F32), axis=0)).astype(BF16)
    out_ref[...] = (encoded.astype(F32) + nn(spreader, main_rows)).astype(BF16)

    for copy in pending:
        copy.wait_send()

    @pl.when(y < 2)
    def _():
        for copy in w0_copies():
            copy.wait_send()

    @pl.when(z == NZ - 1)
    def _():
        for p in range(NZ):
            prev_copy(p).wait_send()


def shards(
    byte_stream,
    gate_stream,
    conv_weight,
    state_write,
    state_read,
    step_size,
    decay_coef,
    skip_gain,
    norm_gain,
    mixer_out,
    residual,
    boundaries,
    span_counts,
    span_offsets,
    pad_vector,
    main_gain,
    query_weight,
    key_value_weight,
    main_out_weight,
):
    far = pl.BlockSpec(memory_space=pl.ANY)
    near = pl.BlockSpec(memory_space=pltpu.VMEM)
    vm = pltpu.VMEM
    dma = pltpu.SemaphoreType.DMA
    return pl.pallas_call(
        kernel,
        out_shape=pltpu.VMEM((L, 128), BF16),
        in_specs=[far] * 17,
        out_specs=near,
        scratch_shapes=[
            vm((4, 256), F32),
            vm((HEADS, L), F32),
            vm((1, HEADS), F32),
            vm((1, HEADS), F32),
            vm((1, 256), F32),
            vm((1, CAP), jnp.int32),
            vm((24, 128), BF16),
            vm((32, 128), F32),
            vm((L, 256), BF16),
            vm((L, 256), BF16),
            vm((L, 128), BF16),
            vm((L, 128), BF16),
            vm((256, 1024), BF16),
            vm((L, 128), BF16),
            vm((64, 512), BF16),
            vm((64, 256), BF16),
            vm((512, 1024), BF16),
            vm((L + 16, 256), F32),
            vm((9, 8, 384), F32),
            vm((8, 8, 128), F32),
            vm((2, 2, 8, 4, 16, 384), BF16),
            vm((8, 16, 256), BF16),
            vm((8, 16, 256), BF16),
            vm((8, 16, 256), BF16),
            vm((8, 16, 256), BF16),
            vm((8, 16, 256), BF16),
            vm((8, CAP, 128), BF16),
            vm((8, CAP, 128), BF16),
            vm((8, CAP, 128), BF16),
            vm((8, L, 128), BF16),
            vm((8, L, 128), BF16),
            vm((4, 4, 2, CAP, 128), BF16),
            vm((4, 128, 128), BF16),
            vm((512, 128), jnp.int32),
            vm((4, 128, 128), BF16),
            vm((4, 8, 128), F32),
            vm((4, 128, 128), BF16),
            vm((4, 8, 128), F32),
            vm((8, CAP, 128), BF16),
            vm((8, CAP, 128), BF16),
            dma((17,)),
            dma((8,)),
            dma((1,)),
            dma((2, 8)),
            dma((2, 2)),
            dma((2, 16)),
            dma((2, 3, 4)),
            dma((N_EX, 8)),
            dma((N_EX, 8)),
        ],
        compiler_params=pltpu.CompilerParams(
            collective_id=0, has_side_effects=True, vmem_limit_bytes=56 * 1024 * 1024
        ),
        cost_estimate=pl.CostEstimate(flops=10**9, bytes_accessed=4 * 10**6, transcendentals=10**6),
    )(
        byte_stream,
        gate_stream,
        conv_weight,
        state_write,
        state_read,
        step_size.T,
        decay_coef.reshape(1, HEADS),
        skip_gain.reshape(1, HEADS),
        norm_gain.reshape(1, 256),
        mixer_out,
        residual,
        boundaries,
        pad_vector.reshape(24, 128),
        main_gain.reshape(32, 128),
        query_weight,
        key_value_weight,
        main_out_weight,
    )


def solution(mesh):
    in_specs = (
        P("seq", "head"),
        P("seq", "head"),
        P(None, "head"),
        P("seq", None),
        P("seq", None),
        P("seq", "head"),
        P("head"),
        P("head"),
        P("head"),
        P("head", None),
        P("seq", None),
        P("seq", None),
        P("seq"),
        P("seq"),
        P(),
        P(),
        P("seq", "head"),
        P("seq", "head"),
        P("head", None),
    )
    out_specs = P("seq", "head")
    return jax.shard_map(shards, mesh=mesh, in_specs=in_specs, out_specs=out_specs, check_vma=False)
```

```python
import functools
import math

import jax
import jax.numpy as jnp
from jax import lax
from jax.experimental import pallas as pl
from jax.experimental.pallas import tpu as pltpu
from jax.sharding import PartitionSpec as P

F32 = jnp.float32
BF16 = jnp.bfloat16
MESH = pl.DeviceIdType.MESH
EXACT = lax.Precision.HIGHEST

NY = 8
NZ = 8
NHD = 8
L = 128
HEADS = 4
HP = 64
CAP = 32
HD = 128
D_MAIN = 4096
THETA = 500000.0
EPSILON = 1e-05
FAR_FIRST = (4, 3, 5, 2, 6, 1, 7)
SLOTS = sorted(((i, j) for i in range(4) for j in range(4) if i + j > 0), key=lambda t: -t[0] - t[1])

(
    EDGE,
    STATS_Y,
    W_AZ,
    W_BY,
    RING_A_KV,
    RING_B_KV,
    RING_A_Q,
    RING_B_Q,
    SCAN1,
    SCAN2,
    SCAN3,
    SPAN_RS,
    SPAN_AG,
    ENC_RS,
    MAIN_RS,
    N_EX,
) = range(16)


def nn(a, b, precision=None):
    return lax.dot_general(
        a, b, (((1,), (0,)), ((), ())), precision=precision, preferred_element_type=F32
    )


def nt(a, b, precision=None):
    return lax.dot_general(
        a, b, (((1,), (1,)), ((), ())), precision=precision, preferred_element_type=F32
    )


def tn(a, b, precision=None):
    return lax.dot_general(
        a, b, (((0,), (0,)), ((), ())), precision=precision, preferred_element_type=F32
    )


def iota(shape, dim):
    return lax.broadcasted_iota(jnp.int32, shape, dim)


def silu(v):
    return v / (1.0 + jnp.exp(-v))


def one_minus_exp(u):
    series = u * (
        1.0
        - u
        * (
            1.0 / 2
            - u * (1.0 / 6 - u * (1.0 / 24 - u * (1.0 / 120 - u * (1.0 / 720 - u / 5040))))
        )
    )
    return jnp.where(u < 0.3, series, 1.0 - jnp.exp(-u))


def kernel(
    x_hbm,
    gate_hbm,
    convw_hbm,
    b_hbm,
    c_hbm,
    step_hbm,
    decay_hbm,
    skip_hbm,
    ngain_hbm,
    mo_hbm,
    res_hbm,
    bnd_hbm,
    pad_hbm,
    mgain_hbm,
    wq_hbm,
    wkv_hbm,
    mw_hbm,
    out_ref,
    convw_ref,
    step_ref,
    decay_ref,
    skip_ref,
    ngain_ref,
    bnd_ref,
    pad_ref,
    mgain_ref,
    x_ref,
    gate_ref,
    b_ref,
    c_ref,
    mo_ref,
    res_ref,
    wq_ref,
    wkv_ref,
    mw_ref,
    ext,
    ebuf,
    stats_y,
    wbuf,
    s1_send,
    s1,
    s2,
    s3_send,
    s3,
    sp_send,
    sp_recv,
    ag,
    en_send,
    en_recv,
    kvbuf,
    qbuf,
    key_ranks,
    o_send,
    m_send,
    o_recv,
    m_recv,
    mn_send,
    mn_recv,
    local_sem,
    prev_send,
    prev_recv,
    w0_send,
    w0_recv,
    kv_sem,
    group_sem,
    send_sem,
    recv_sem,
):
    s = lax.axis_index("seq")
    hd = lax.axis_index("head")
    y = s // NZ
    z = s % NZ

    def at_z(p):
        return (y * NZ + p, hd)

    def at_y(p):
        return (p * NZ + z, hd)

    def at_h(p):
        return (s, p)

    py, pz = lax.rem(y + hd, 2), lax.rem(z + hd, 2)
    sy, sz = 1 - 2 * py, 1 - 2 * pz

    def at_slot(i, j):
        yc = lax.rem(y + 8 + (0, -1, 2, -3)[i] * sy, NY)
        zc = lax.rem(z + 8 + (0, -1, 2, -3)[j] * sz, NZ)
        return (yc * NZ + zc, hd)

    def member(e):
        yc = lax.rem(y + 8 + sy, NY) if e // 2 else y
        zc = lax.rem(z + 8 + sz, NZ) if e % 2 else z
        return (yc * NZ + zc, hd), 2 * lax.rem(yc + hd, 2) + lax.rem(zc + hd, 2)

    barrier = pltpu.get_barrier_semaphore()
    greet = [(lax.rem(y + NY - 1, NY) * NZ + NZ - 1, hd)]
    for d in range(1, 8):
        greet += [at_z(lax.rem(z + d, NZ)), at_y(lax.rem(y + d, NY)), at_h(lax.rem(hd + d, NHD))]
    for to in greet:
        pl.semaphore_signal(barrier, inc=1, device_id=to, device_id_type=MESH)

    loads = [
        (step_hbm, step_ref),
        (decay_hbm, decay_ref),
        (x_hbm, x_ref),
        (convw_hbm, convw_ref),
        (b_hbm, b_ref),
        (wq_hbm, wq_ref),
        (wkv_hbm, wkv_ref),
        (pad_hbm, pad_ref),
        (mgain_hbm, mgain_ref),
        (bnd_hbm, bnd_ref),
        (c_hbm, c_ref),
        (gate_hbm, gate_ref),
        (skip_hbm, skip_ref),
        (ngain_hbm, ngain_ref),
        (res_hbm.at[:, pl.ds(pl.multiple_of(hd * 128, 128), 128)], res_ref),
        (mo_hbm, mo_ref),
        (mw_hbm, mw_ref),
    ]
    load = [pltpu.make_async_copy(a, b, local_sem.at[i]) for i, (a, b) in enumerate(loads)]
    for copy in load[:10]:
        copy.start()
    l_step, l_decay, l_x, l_convw, l_b, l_wq, l_wkv, l_pad, l_mgain, l_bnd = load[:10]
    l_c, l_gate, l_skip, l_ngain, l_res, l_mo, l_mw = load[10:]

    pending = []

    def send_all(ex, me, where, src, dst):
        for d in FAR_FIRST:
            p = lax.rem(me + d, 8)
            copy = pltpu.make_async_remote_copy(
                src_ref=src(p),
                dst_ref=dst,
                send_sem=send_sem.at[ex, d],
                recv_sem=recv_sem.at[ex, me],
                device_id=where(p),
                device_id_type=MESH,
            )
            copy.start()
            pending.append(copy)

    def recv_all(ex, me, where, slot):
        for d in range(1, 8):
            p = lax.rem(me + 8 - d, 8)
            pltpu.make_async_remote_copy(
                src_ref=slot(p),
                dst_ref=slot(p),
                send_sem=send_sem.at[ex, d],
                recv_sem=recv_sem.at[ex, p],
                device_id=where(p),
                device_id_type=MESH,
            ).wait_recv()

    l_step.wait()
    l_decay.wait()
    dec = decay_ref[...]
    row4 = iota((HEADS, L), 0)
    coef = jnp.zeros((HEADS, L), F32)
    for h in range(HEADS):
        coef = jnp.where(row4 == h, dec[:, h : h + 1], coef)
    rate = step_ref[...] * coef
    log_decay = -rate
    gain_row = jnp.sqrt(one_minus_exp(2.0 * rate))
    ti = iota((L, L), 0)
    si = iota((L, L), 1)
    causal = ti >= si
    tri = jnp.where(causal, 1.0, 0.0).astype(F32)
    run_row = nt(log_decay, tri, EXACT)
    run_col = [
        nt(tri, jnp.broadcast_to(log_decay[h : h + 1, :], (L, L)), EXACT) for h in range(HEADS)
    ]
    rem_row = jnp.exp(run_row[:, L - 1 : L] - run_row) * gain_row
    first = si < HP
    eye = jnp.where(ti == si, 1.0, 0.0).astype(BF16)
    top = ti < HP
    rem_x = [
        nt(
            eye,
            jnp.where(
                top,
                jnp.broadcast_to(rem_row[2 * i : 2 * i + 1, :], (L, L)),
                jnp.broadcast_to(rem_row[2 * i + 1 : 2 * i + 2, :], (L, L)),
            ).astype(BF16),
        )
        for i in range(2)
    ]
    run_x = jnp.concatenate(
        [jnp.where(first, run_col[2 * i], run_col[2 * i + 1]) for i in range(2)], axis=1
    )

    l_x.wait()
    l_convw.wait()
    l_b.wait()
    ext[0:8, :] = jnp.zeros((8, 256), F32)
    ext[8 : 8 + L, :] = x_ref[...].astype(F32)
    ext[8 + L :, :] = jnp.zeros((8, 256), F32)
    cw = convw_ref[...]
    summed = cw[0:1, :] * ext[5 : 13 + L, :]
    for k in range(1, 4):
        summed = summed + cw[k : k + 1, :] * ext[5 + k : 13 + k + L, :]
    conv_own = silu(summed[:L]).astype(BF16).astype(F32)

    bm = b_ref[...]
    inner = iota((L, 256), 0) >= 3
    weighted = jnp.where(inner, conv_own * jnp.concatenate(rem_x, axis=1), 0.0).astype(BF16)
    state = tn(bm, weighted).astype(BF16)
    s1_send[...] = state.reshape(8, 16, 256)
    head_b = bm[0:16, :].astype(F32)
    ebuf[1 + z, 0:3, 0:256] = summed[0:3]
    ebuf[1 + z, 3:6, 0:256] = summed[L : L + 3]
    ebuf[1 + z, 6:7, 0:128] = head_b[0:1, :]
    ebuf[1 + z, 6:7, 128:256] = head_b[1:2, :]
    ebuf[1 + z, 7:8, 0:128] = head_b[2:3, :]
    ebuf[1 + z, 7:8, 128:256] = jnp.zeros((1, 128), F32)

    l_wq.wait()
    l_wkv.wait()
    l_pad.wait()
    l_mgain.wait()
    l_bnd.wait()
    prow = s // 2 - 8
    padf = pad_ref[...].astype(F32)
    mg = mgain_ref[...]
    pad_one = jnp.sum(jnp.where(iota((24, 128), 0) == prow, padf, 0.0), axis=0, keepdims=True)
    gain_one = jnp.sum(jnp.where(iota((32, 128), 0) == s // 2, mg, 0.0), axis=0, keepdims=True)
    both = pad_one * gain_one
    half = jnp.where(s % 2 == 1, both[:, 64:], both[:, :64])
    half = jnp.broadcast_to(half, (16, 64)).astype(BF16)
    pq = nn(half, wq_ref[...])
    pkv = nn(half, wkv_ref[...])
    pad_sq = jnp.sum(jnp.sum(padf * padf, axis=1, keepdims=True), axis=0, keepdims=True)
    lane1 = iota((1, 128), 1)
    bounds = bnd_ref[...]
    count = jnp.sum(jnp.where(bounds < NY * NZ * L, 1.0, 0.0), axis=1, keepdims=True)
    last = jnp.zeros((1, 128), F32)
    for h in range(HEADS):
        last = jnp.where(lane1 == h, run_col[h][L - 1 : L, :], last)
        for t in range(3):
            last = jnp.where(lane1 == 16 + 4 * t + h, rem_row[h : h + 1, t : t + 1], last)
    rows = [
        pq[0:1, 0:128],
        pq[0:1, 128:256],
        pkv[0:1, 0:128],
        pq[0:1, 256:384],
        pq[0:1, 384:512],
        pkv[0:1, 128:256],
        jnp.where(lane1 == z, count, 0.0),
        last,
    ]
    for i, row in enumerate(rows):
        ebuf[1 + z, i : i + 1, 256:384] = row

    pl.semaphore_wait(barrier, jnp.where(z == NZ - 1, 21 + NZ, 21))

    def w0_parts(yp):
        rg = lax.rem(yp, 4)
        ch = yp // 4
        r = pl.ds(pl.multiple_of(16 * rg, 16), 16)
        return (
            (
                wq_hbm.at[r, pl.ds(pl.multiple_of(256 * ch, 256), 256)],
                wbuf.at[ch, y, z, rg, :, pl.ds(0, 256)],
            ),
            (
                wkv_hbm.at[r, pl.ds(pl.multiple_of(128 * ch, 128), 128)],
                wbuf.at[ch, y, z, rg, :, pl.ds(256, 128)],
            ),
        )

    def w0_copies():
        copies = []
        for d in FAR_FIRST:
            yp = lax.rem(y + d, NY)
            for i, (src, dst) in enumerate(w0_parts(yp)):
                copies.append(
                    pltpu.make_async_remote_copy(
                        src_ref=src,
                        dst_ref=dst,
                        send_sem=w0_send.at[i, d],
                        recv_sem=w0_recv.at[i, y],
                        device_id=at_y(yp),
                        device_id_type=MESH,
                    )
                )
        return copies

    @pl.when(y < 2)
    def _():
        for copy in w0_copies():
            copy.start()
        for i, (src, dst) in enumerate(w0_parts(y)):
            pltpu.make_async_copy(src, dst, w0_recv.at[i, y]).start()

    send_all(EDGE, z, at_z, lambda p: ebuf.at[1 + z], ebuf.at[1 + z])

    def prev_copy(p):
        return pltpu.make_async_remote_copy(
            src_ref=ebuf.at[1 + z],
            dst_ref=ebuf.at[0],
            send_sem=prev_send.at[p],
            recv_sem=prev_recv.at[0],
            device_id=(lax.rem(y + 1, NY) * NZ + p, hd),
            device_id_type=MESH,
        )

    @pl.when(z == NZ - 1)
    def _():
        for p in range(NZ):
            prev_copy(p).start()

    send_all(SCAN1, z, at_z, lambda p: s1_send.at[p], s1.at[z])
    s1[z] = s1_send[z]

    for copy in load[10:]:
        copy.start()

    l_c.wait()
    cm = c_ref[...]
    affinity = jnp.where(causal, nt(cm, bm), 0.0)
    mix = []
    for h in range(HEADS):
        spread = jnp.where(causal, run_col[h] - run_row[h : h + 1, :], 0.0)
        mix.append((jnp.exp(spread) * (affinity * gain_row[h : h + 1, :])).astype(BF16))

    recv_all(EDGE, z, at_z, lambda p: ebuf.at[1 + p])
    prev_copy(0).wait_recv()
    edges = ebuf[...]
    tiles = edges[1:, :, 256:384]
    stats_y[y] = jnp.sum(tiles, axis=0)
    send_all(STATS_Y, y, at_y, lambda p: stats_y.at[y], stats_y.at[y])

    col = iota((128, 1024), 1)
    part_of = col // 256
    lane_of = lax.rem(col, 256) // HP + jnp.where(part_of > 0, 12 + 4 * part_of, 0)
    spread_head = jnp.where(iota((128, 1024), 0) == lane_of, 1.0, 0.0).astype(F32)
    by_head = nn(tiles[:, 7, :], spread_head, EXACT)
    lz = by_head[:, 0:256]

    nothing = (iota((8, 256), 0) + y) == 0
    edge_x, edge_b = [], []
    for t in range(3):
        earlier = jnp.where(nothing, 0.0, edges[0:8, 3 + t, 0:256])
        conv_t = silu(edges[1:, t, 0:256] + earlier).astype(BF16).astype(F32)
        edge_x.append(conv_t * by_head[:, 256 * (1 + t) : 256 * (2 + t)])
        edge_b.append(edges[1:, 6 + t // 2, 128 * (t % 2) : 128 * (t % 2 + 1)])
    edge_x = jnp.concatenate(edge_x, axis=0).astype(BF16)
    edge_b = jnp.concatenate(edge_b, axis=0).astype(BF16)
    pick_n = jnp.where(si == 16 * z + lax.rem(ti, 16), 1.0, 0.0).astype(BF16)
    spots = nt(pick_n, edge_b)
    same = iota((L, 24), 0) // 16 == lax.rem(iota((L, 24), 1), 8)
    added = nn(jnp.where(same, spots, 0.0).astype(BF16), edge_x).reshape(8, 16, 256)
    recv_all(SCAN1, z, at_z, lambda p: s1.at[p])
    acc = jnp.zeros((16, 256), F32)
    cum = jnp.zeros((1, 256), F32)
    before, cums = [], []
    for j in range(NZ):
        before.append(acc)
        cums.append(cum)
        acc = jnp.exp(lz[j : j + 1, :]) * acc + (s1[j].astype(F32) + added[j])
        cum = cum + lz[j : j + 1, :]
    s2[y] = acc.astype(BF16)
    send_all(SCAN2, y, at_y, lambda p: s2.at[y], s2.at[y])

    for b in range(2):
        for i, (src, dst) in enumerate(w0_parts(y)):
            rg = lax.rem(y, 4)
            ch = y // 4
            cols = pl.ds(0, 256) if i == 0 else pl.ds(256, 128)
            slot = wbuf.at[ch, b, z, rg, :, cols]
            pltpu.make_async_copy(slot, slot, w0_recv.at[i, b]).wait()
    rg_me = lax.rem(y, 4)
    ch_me = y // 4
    send_all(
        W_AZ, z, at_z, lambda p: wbuf.at[ch_me, 0, z, rg_me], wbuf.at[ch_me, 0, z, rg_me]
    )
    send_all(
        W_BY, y, at_y, lambda p: wbuf.at[ch_me, 1, z, rg_me], wbuf.at[ch_me, 1, z, rg_me]
    )

    before_rows = pltpu.roll(ebuf[z, :, 0:256], 5, 0)
    lead = (iota((8, 256), 0) < 3) & (s > 0)
    top_rows = silu(summed[0:8] + jnp.where(lead, before_rows, 0.0)).astype(BF16).astype(F32)
    conv_f = jnp.concatenate([top_rows, conv_own[8:]], axis=0)
    conv = conv_f.astype(BF16)

    within = []
    zero = jnp.zeros((), BF16)
    for i in range(2):
        pair = conv[:, 128 * i : 128 * (i + 1)]
        stacked = jnp.concatenate(
            [jnp.where(first, pair, zero), jnp.where(first, zero, pair)], axis=0
        )
        within.append(nn(jnp.concatenate([mix[2 * i], mix[2 * i + 1]], axis=1), stacked))
    l_skip.wait()
    skip_v = skip_ref[...]
    skip = jnp.zeros((1, 256), F32)
    head_of = iota((1, 256), 1) // HP
    for h in range(HEADS):
        skip = jnp.where(head_of == h, skip_v[:, h : h + 1], skip)
    mixed_near = jnp.concatenate(within, axis=1) + skip * conv_f
    exp_run = jnp.exp(run_x)
    l_gate.wait()
    gate = silu(gate_ref[...].astype(F32))

    def block_a(p, cols, lo=0, n=8):
        return wbuf.at[p // 4, 0, pl.ds(lo, n), lax.rem(p, 4), :, cols]

    def block_b(p, cols, lo=0, n=2):
        return wbuf.at[pl.ds(lo, n), 1, p, :, :, cols]

    def rings(step, wait, kv):
        cols = pl.ds(256, 128) if kv else pl.ds(0, 256)
        for ex, me, where, block, whole in (
            (RING_A_KV if kv else RING_A_Q, y, at_y, block_a, 8),
            (RING_B_KV if kv else RING_B_Q, z, at_z, block_b, 2),
        ):
            for way in range(2):
                ahead = lax.rem(me + (1 if way == 0 else 7), 8)
                moved = step + (1 if wait else 0)
                of = lax.rem(me + (8 - moved if way == 0 else moved), 8)
                if step == 3:
                    part = block(of, cols, way * whole // 2, whole // 2)
                else:
                    part = block(of, cols)
                copy = pltpu.make_async_remote_copy(
                    src_ref=part,
                    dst_ref=part,
                    send_sem=send_sem.at[ex, 2 * step + way],
                    recv_sem=recv_sem.at[ex, 2 * step + way],
                    device_id=where(ahead),
                    device_id_type=MESH,
                )
                if wait:
                    copy.wait_recv()
                else:
                    copy.start()
                    pending.append(copy)

    recv_all(STATS_Y, y, at_y, lambda p: stats_y.at[p])
    ytiles = stats_y[...]
    pad_total = jnp.sum(ytiles, axis=0)
    ly = nn(ytiles[:, 7, :], spread_head[:, 0:256], EXACT)

    recv_all(SCAN2, y, at_y, lambda p: s2.at[p])
    rows_before = jnp.zeros((16, 256), F32)
    for j in range(NY - 1):
        longer = jnp.exp(ly[j : j + 1, :]) * rows_before + s2[j].astype(F32)
        rows_before = jnp.where(j < y, longer, rows_before)
    for j in range(NZ):
        s3_send[j] = (before[j] + jnp.exp(cums[j]) * rows_before).astype(BF16)
    send_all(SCAN3, z, at_z, lambda p: s3_send.at[p], s3.at[z])
    s3[z] = s3_send[z]

    l_ngain.wait()
    bnd = bounds - s * L
    byte_at = iota((L, CAP), 0)
    slot_at = iota((L, CAP), 1)
    usable = bounds < NY * NZ * L
    picker = jnp.where((byte_at == bnd) & usable, 1.0, 0.0).astype(BF16)
    upto = jnp.where((bnd <= byte_at) & usable, 1.0, 0.0)
    newest = jnp.sum(upto, axis=1, keepdims=True) - 1.0
    spreader = jnp.where(slot_at.astype(F32) == newest, 1.0, 0.0).astype(BF16)
    l_res.wait()
    res = res_ref[...]
    res_span = tn(picker, res)

    lane = iota((CAP, 128), 1)
    counts = ytiles[:, 6, :]
    lane8 = iota((8, 128), 1)
    ahead = (lane8 < NZ) & (iota((8, 128), 0) * NZ + lane8 < s)
    offset = jnp.sum(jnp.where(ahead, counts, 0.0), axis=0, keepdims=True)
    offset = jnp.sum(offset, axis=1, keepdims=True)
    place = iota((CAP, 128), 0).astype(F32) + offset
    freq = jnp.exp(
        lax.rem(lane, HD // 2).astype(F32) * (-2.0 * math.log(THETA) / HD)
    )
    angle = place * freq
    cosine = jnp.cos(angle)
    sine = jnp.where(lane < HD // 2, -jnp.sin(angle), jnp.sin(angle))

    recv_all(W_AZ, z, at_z, lambda p: wbuf.at[ch_me, 0, p, rg_me])
    recv_all(W_BY, y, at_y, lambda p: wbuf.at[p // 4, 1, z, lax.rem(p, 4)])
    rings(0, False, True)
    rings(0, False, False)

    recv_all(SCAN3, z, at_z, lambda p: s3.at[p])
    entering = nn(cm, s3[...].reshape(128, 256)) * exp_run
    gated = (mixed_near + entering) * gate
    mean_sq = jnp.sum(gated * gated, axis=1, keepdims=True) * (1.0 / 256)
    normed = (gated * lax.rsqrt(mean_sq + EPSILON) * ngain_ref[...]).astype(BF16)
    l_mo.wait()
    picked = tn(picker, normed).astype(BF16)
    span_part = nn(picked, mo_ref[...]).astype(BF16)
    for j in range(NHD):
        sp_send[j] = span_part[:, 128 * j : 128 * (j + 1)]
    send_all(SPAN_RS, hd, at_h, lambda p: sp_send.at[p], sp_recv.at[hd])
    sp_recv[hd] = sp_send[hd]

    rings(0, True, True)
    rings(1, False, True)
    rings(0, True, False)
    rings(1, False, False)

    enc_part = nn(normed, mo_ref[...]).astype(BF16)
    for j in range(NHD):
        en_send[j] = enc_part[:, 128 * j : 128 * (j + 1)]
    en_recv[hd] = en_send[hd]

    rings(1, True, True)
    rings(2, False, True)
    rings(1, True, False)
    rings(2, False, False)

    recv_all(SPAN_RS, hd, at_h, lambda p: sp_recv.at[p])
    span_share = (res_span + jnp.sum(sp_recv[...].astype(F32), axis=0)).astype(BF16)
    ag[hd] = span_share
    send_all(SPAN_AG, hd, at_h, lambda p: ag.at[hd], ag.at[hd])

    rings(2, True, True)
    rings(3, False, True)
    rings(2, True, False)
    rings(3, False, False)

    key = iota((512, 128), 0)
    key_y = lax.rem(y + 16 - (key // 128) * sy, NY)
    key_z = lax.rem(z + 16 - lax.rem(key // CAP, 4) * sz, NZ)
    expand = jnp.where(iota((512, 128), 1) == key_z, 1.0, 0.0).astype(BF16)
    per_row = nt(expand, jnp.concatenate([ytiles[:, 6, :], ytiles[:, 6, :]], axis=0).astype(BF16))
    lane16 = iota((512, 16), 1)
    key_count = jnp.sum(
        jnp.where(lane16 == lax.rem(y + 16 - (iota((512, 16), 0) // 128) * sy, NY), per_row, 0.0),
        axis=1,
        keepdims=True,
    )
    key_slot = lax.rem(key, CAP)
    key_rank = (key_y * NZ + key_z) * CAP + key_slot
    key_rank = jnp.where(key_slot.astype(F32) < key_count, key_rank, NY * NZ * CAP)
    key_ranks[...] = key_rank
    query = iota((1, 512), 1)
    query_rank = (
        (
            lax.rem(y + 8 - py + query // 256, NY) * NZ
            + lax.rem(z + 8 - pz + lax.rem(query // 128, 2), NZ)
        )
        * CAP
        + lax.rem(query, CAP)
    )

    recv_all(SPAN_AG, hd, at_h, lambda p: ag.at[p])
    sq = jnp.zeros((CAP, 1), F32)
    pieces = []
    for j in range(NHD):
        piece = ag[j].astype(F32)
        sq = sq + jnp.sum(piece * piece, axis=1, keepdims=True)
        pieces.append((piece * mg[j : j + 1, :]).astype(BF16))
    scale = lax.rsqrt((sq + pad_sq) * (1.0 / D_MAIN) + EPSILON)
    span_x = jnp.concatenate(pieces, axis=1)
    rings(3, True, True)
    def project(ch, lo, n):
        return nn(span_x, wbuf[ch, :, :, :, :, lo : lo + n].reshape(1024, n))

    def column(part, i):
        return (part + pad_total[i : i + 1, :]) * scale

    def rotate(v):
        return (v * cosine + pltpu.roll(v, HD // 2, 1) * sine).astype(BF16)

    kvbuf[0, 0, 0] = rotate(column(project(0, 256, 128), 2))
    kvbuf[0, 0, 1] = column(project(1, 256, 128), 5).astype(BF16)

    def kv_copy(i, j):
        return pltpu.make_async_remote_copy(
            src_ref=kvbuf.at[0, 0],
            dst_ref=kvbuf.at[i, j],
            send_sem=kv_sem.at[0, 4 * i + j],
            recv_sem=kv_sem.at[1, 4 * i + j],
            device_id=at_slot(i, j),
            device_id_type=MESH,
        )

    kv_copies = [kv_copy(i, j) for i, j in SLOTS]
    for copy in kv_copies:
        copy.start()
        pending.append(copy)
    mine = 2 * py + pz

    rings(3, True, False)
    for ch in range(2):
        pair = project(ch, 0, 256)
        for h in range(2):
            at = CAP * (2 * ch + h)
            part = pair[:, 128 * h : 128 * (h + 1)]
            qbuf[mine, at : at + CAP, :] = rotate(column(part, 3 * ch + h))

    def group_copy(i, e, src, dst):
        return pltpu.make_async_remote_copy(
            src_ref=src,
            dst_ref=dst,
            send_sem=group_sem.at[0, i, e],
            recv_sem=group_sem.at[1, i, e],
            device_id=member(e)[0],
            device_id_type=MESH,
        )

    for e in range(1, 4):
        copy = group_copy(0, e, qbuf.at[mine], qbuf.at[mine])
        copy.start()
        pending.append(copy)

    send_all(ENC_RS, hd, at_h, lambda p: en_send.at[p], en_recv.at[hd])

    for e in range(1, 4):
        slot = qbuf.at[member(e)[1]]
        group_copy(0, e, slot, slot).wait_recv()
    for copy in kv_copies:
        copy.wait_recv()

    kv = kvbuf[...]
    keys = kv[:, :, 0].reshape(512, HD)
    values = kv[:, :, 1].reshape(512, HD)
    ranks = key_ranks[...]
    unit = 1.0 / math.sqrt(HD)
    for m in range(4):
        scores = nt(keys, qbuf[m])
        allowed = ranks <= query_rank[:, 128 * m : 128 * (m + 1)]
        scores = jnp.where(allowed, scores * unit, -1e30)
        top = jnp.max(scores, axis=0, keepdims=True)
        weights = jnp.exp(scores - top)
        o_send[m] = tn(values, weights.astype(BF16)).astype(BF16)
        m_send[m, 0:1, :] = top
        m_send[m, 1:2, :] = jnp.sum(weights, axis=0, keepdims=True)

    for e in range(1, 4):
        place_e = member(e)[1]
        for i, (src, dst) in enumerate(((o_send, o_recv), (m_send, m_recv))):
            copy = group_copy(1 + i, e, src.at[place_e], dst.at[e])
            copy.start()
            pending.append(copy)
    o_recv[0] = o_send[mine]
    m_recv[0] = m_send[mine]

    for e in range(1, 4):
        group_copy(1, e, o_recv.at[e], o_recv.at[e]).wait_recv()
        group_copy(2, e, m_recv.at[e], m_recv.at[e]).wait_recv()

    tops = m_recv[:, 0, :]
    highest = jnp.max(tops, axis=0, keepdims=True)
    shrink = jnp.exp(tops - highest)
    total = jnp.sum(shrink * m_recv[:, 1, :], axis=0, keepdims=True)
    summed_o = jnp.zeros((HD, 128), F32)
    for e in range(4):
        summed_o = summed_o + shrink[e : e + 1, :] * o_recv[e].astype(F32)
    attended = (summed_o / total).T.astype(BF16)

    l_mw.wait()
    att = jnp.concatenate([attended[CAP * i : CAP * (i + 1), :] for i in range(4)], axis=1)
    main_part = nn(att, mw_ref[...]).astype(BF16)
    for j in range(NHD):
        mn_send[j] = main_part[:, 128 * j : 128 * (j + 1)]
    send_all(MAIN_RS, hd, at_h, lambda p: mn_send.at[p], mn_recv.at[hd])
    mn_recv[hd] = mn_send[hd]
    recv_all(ENC_RS, hd, at_h, lambda p: en_recv.at[p])
    encoded = (res.astype(F32) + jnp.sum(en_recv[...].astype(F32), axis=0)).astype(BF16)

    recv_all(MAIN_RS, hd, at_h, lambda p: mn_recv.at[p])
    main_rows = (span_share.astype(F32) + jnp.sum(mn_recv[...].astype(F32), axis=0)).astype(BF16)
    out_ref[...] = (encoded.astype(F32) + nn(spreader, main_rows)).astype(BF16)

    for copy in pending:
        copy.wait_send()

    @pl.when(y < 2)
    def _():
        for copy in w0_copies():
            copy.wait_send()

    @pl.when(z == NZ - 1)
    def _():
        for p in range(NZ):
            prev_copy(p).wait_send()


def shards(
    byte_stream,
    gate_stream,
    conv_weight,
    state_write,
    state_read,
    step_size,
    decay_coef,
    skip_gain,
    norm_gain,
    mixer_out,
    residual,
    boundaries,
    span_counts,
    span_offsets,
    pad_vector,
    main_gain,
    query_weight,
    key_value_weight,
    main_out_weight,
):
    far = pl.BlockSpec(memory_space=pl.ANY)
    near = pl.BlockSpec(memory_space=pltpu.VMEM)
    vm = pltpu.VMEM
    dma = pltpu.SemaphoreType.DMA
    return pl.pallas_call(
        kernel,
        out_shape=pltpu.VMEM((L, 128), BF16),
        in_specs=[far] * 17,
        out_specs=near,
        scratch_shapes=[
            vm((4, 256), F32),
            vm((HEADS, L), F32),
            vm((1, HEADS), F32),
            vm((1, HEADS), F32),
            vm((1, 256), F32),
            vm((1, CAP), jnp.int32),
            vm((24, 128), BF16),
            vm((32, 128), F32),
            vm((L, 256), BF16),
            vm((L, 256), BF16),
            vm((L, 128), BF16),
            vm((L, 128), BF16),
            vm((256, 1024), BF16),
            vm((L, 128), BF16),
            vm((64, 512), BF16),
            vm((64, 256), BF16),
            vm((512, 1024), BF16),
            vm((L + 16, 256), F32),
            vm((9, 8, 384), F32),
            vm((8, 8, 128), F32),
            vm((2, 2, 8, 4, 16, 384), BF16),
            vm((8, 16, 256), BF16),
            vm((8, 16, 256), BF16),
            vm((8, 16, 256), BF16),
            vm((8, 16, 256), BF16),
            vm((8, 16, 256), BF16),
            vm((8, CAP, 128), BF16),
            vm((8, CAP, 128), BF16),
            vm((8, CAP, 128), BF16),
            vm((8, L, 128), BF16),
            vm((8, L, 128), BF16),
            vm((4, 4, 2, CAP, 128), BF16),
            vm((4, 128, 128), BF16),
            vm((512, 128), jnp.int32),
            vm((4, 128, 128), BF16),
            vm((4, 8, 128), F32),
            vm((4, 128, 128), BF16),
            vm((4, 8, 128), F32),
            vm((8, CAP, 128), BF16),
            vm((8, CAP, 128), BF16),
            dma((17,)),
            dma((8,)),
            dma((1,)),
            dma((2, 8)),
            dma((2, 2)),
            dma((2, 16)),
            dma((2, 3, 4)),
            dma((N_EX, 8)),
            dma((N_EX, 8)),
        ],
        compiler_params=pltpu.CompilerParams(
            collective_id=0, has_side_effects=True, vmem_limit_bytes=56 * 1024 * 1024
        ),
        cost_estimate=pl.CostEstimate(flops=10**9, bytes_accessed=4 * 10**6, transcendentals=10**6),
    )(
        byte_stream,
        gate_stream,
        conv_weight,
        state_write,
        state_read,
        step_size.T,
        decay_coef.reshape(1, HEADS),
        skip_gain.reshape(1, HEADS),
        norm_gain.reshape(1, 256),
        mixer_out,
        residual,
        boundaries,
        pad_vector.reshape(24, 128),
        main_gain.reshape(32, 128),
        query_weight,
        key_value_weight,
        main_out_weight,
    )


def solution(mesh):
    in_specs = (
        P("seq", "head"),
        P("seq", "head"),
        P(None, "head"),
        P("seq", None),
        P("seq", None),
        P("seq", "head"),
        P("head"),
        P("head"),
        P("head"),
        P("head", None),
        P("seq", None),
        P("seq", None),
        P("seq"),
        P("seq"),
        P(),
        P(),
        P("seq", "head"),
        P("seq", "head"),
        P("head", None),
    )
    out_specs = P("seq", "head")
    return jax.shard_map(shards, mesh=mesh, in_specs=in_specs, out_specs=out_specs, check_vma=False)
```

```python
import functools
import math

import jax
import jax.numpy as jnp
from jax import lax
from jax.experimental import pallas as pl
from jax.experimental.pallas import tpu as pltpu
from jax.sharding import PartitionSpec as P

F32 = jnp.float32
BF16 = jnp.bfloat16
MESH = pl.DeviceIdType.MESH
EXACT = lax.Precision.HIGHEST

NY = 8
NZ = 8
NHD = 8
L = 128
HEADS = 4
HP = 64
CAP = 32
HD = 128
D_MAIN = 4096
THETA = 500000.0
EPSILON = 1e-05
FAR_FIRST = (4, 3, 5, 2, 6, 1, 7)
SLOTS = sorted(((i, j) for i in range(4) for j in range(4) if i + j > 0), key=lambda t: -t[0] - t[1])

(
    EDGE,
    STATS_Y,
    W_AZ,
    W_BY,
    SCAN1,
    SCAN2,
    SCAN3,
    SPAN_RS,
    SPAN_AG,
    ENC_RS,
    MAIN_RS,
    KV,
    QUERIES,
    OUT_SUMS,
    OUT_STATS,
    N_EX,
) = range(16)
RING_A_KV, RING_B_KV, RING_A_Q, RING_B_Q, N_SEM = (N_EX + 4 * i for i in range(5))


def nn(a, b, precision=None):
    return lax.dot_general(
        a, b, (((1,), (0,)), ((), ())), precision=precision, preferred_element_type=F32
    )


def nt(a, b, precision=None):
    return lax.dot_general(
        a, b, (((1,), (1,)), ((), ())), precision=precision, preferred_element_type=F32
    )


def tn(a, b, precision=None):
    return lax.dot_general(
        a, b, (((0,), (0,)), ((), ())), precision=precision, preferred_element_type=F32
    )


def iota(shape, dim):
    return lax.broadcasted_iota(jnp.int32, shape, dim)


def silu(v):
    return v / (1.0 + jnp.exp(-v))


def one_minus_exp(u):
    series = u * (
        1.0
        - u
        * (
            1.0 / 2
            - u * (1.0 / 6 - u * (1.0 / 24 - u * (1.0 / 120 - u * (1.0 / 720 - u / 5040))))
        )
    )
    return jnp.where(u < 0.3, series, 1.0 - jnp.exp(-u))


def kernel(
    x_hbm,
    gate_hbm,
    convw_hbm,
    b_hbm,
    c_hbm,
    step_hbm,
    decay_hbm,
    skip_hbm,
    ngain_hbm,
    mo_hbm,
    res_hbm,
    bnd_hbm,
    pad_hbm,
    mgain_hbm,
    wq_hbm,
    wkv_hbm,
    mw_hbm,
    out_ref,
    convw_ref,
    step_ref,
    decay_ref,
    skip_ref,
    ngain_ref,
    bnd_ref,
    pad_ref,
    mgain_ref,
    x_ref,
    gate_ref,
    b_ref,
    c_ref,
    mo_ref,
    res_ref,
    wq_ref,
    wkv_ref,
    mw_ref,
    ext,
    ebuf,
    stats_y,
    wbuf,
    s1_send,
    s1,
    s2,
    s3_send,
    s3,
    sp_send,
    sp_recv,
    ag,
    en_send,
    en_recv,
    kvbuf,
    qbuf,
    key_ranks,
    o_send,
    m_send,
    o_recv,
    m_recv,
    mn_send,
    mn_recv,
    local_sem,
    prev_sem,
    w0_sem,
    send_sem,
    recv_sem,
):
    s = lax.axis_index("seq")
    hd = lax.axis_index("head")
    y = s // NZ
    z = s % NZ

    def at_z(p):
        return (y * NZ + p, hd)

    def at_y(p):
        return (p * NZ + z, hd)

    def at_h(p):
        return (s, p)

    py, pz = lax.rem(y + hd, 2), lax.rem(z + hd, 2)
    sy, sz = 1 - 2 * py, 1 - 2 * pz

    def at_slot(i, j):
        yc = lax.rem(y + 8 + (0, -1, 2, -3)[i] * sy, NY)
        zc = lax.rem(z + 8 + (0, -1, 2, -3)[j] * sz, NZ)
        return (yc * NZ + zc, hd)

    def member(e):
        yc = lax.rem(y + 8 + sy, NY) if e // 2 else y
        zc = lax.rem(z + 8 + sz, NZ) if e % 2 else z
        return (yc * NZ + zc, hd), 2 * lax.rem(yc + hd, 2) + lax.rem(zc + hd, 2)

    barrier = pltpu.get_barrier_semaphore()
    greet = [(lax.rem(y + NY - 1, NY) * NZ + NZ - 1, hd)]
    for d in range(1, 8):
        greet += [at_z(lax.rem(z + d, NZ)), at_y(lax.rem(y + d, NY)), at_h(lax.rem(hd + d, NHD))]
    for to in greet:
        pl.semaphore_signal(barrier, inc=1, device_id=to, device_id_type=MESH)

    loads = [
        (step_hbm, step_ref),
        (decay_hbm, decay_ref),
        (x_hbm, x_ref),
        (convw_hbm, convw_ref),
        (b_hbm, b_ref),
        (wq_hbm, wq_ref),
        (wkv_hbm, wkv_ref),
        (pad_hbm, pad_ref),
        (mgain_hbm, mgain_ref),
        (bnd_hbm, bnd_ref),
        (c_hbm, c_ref),
        (gate_hbm, gate_ref),
        (skip_hbm, skip_ref),
        (ngain_hbm, ngain_ref),
        (res_hbm.at[:, pl.ds(pl.multiple_of(hd * 128, 128), 128)], res_ref),
        (mo_hbm, mo_ref),
        (mw_hbm, mw_ref),
    ]
    load = [pltpu.make_async_copy(a, b, local_sem.at[i]) for i, (a, b) in enumerate(loads)]
    for copy in load[:10]:
        copy.start()
    l_step, l_decay, l_x, l_convw, l_b, l_wq, l_wkv, l_pad, l_mgain, l_bnd = load[:10]
    l_c, l_gate, l_skip, l_ngain, l_res, l_mo, l_mw = load[10:]

    pending = []
    sizes = {}

    def finish(blocks, sem):
        pltpu.make_async_copy(blocks, blocks, sem).wait()

    def send_all(ex, me, where, src, dst, seven):
        for d in FAR_FIRST:
            p = lax.rem(me + d, 8)
            pltpu.make_async_remote_copy(
                src_ref=src(p),
                dst_ref=dst,
                send_sem=send_sem.at[ex],
                recv_sem=recv_sem.at[ex],
                device_id=where(p),
                device_id_type=MESH,
            ).start()
        pending.append((seven, send_sem.at[ex]))
        sizes[ex] = seven

    def recv_all(ex):
        finish(sizes[ex], recv_sem.at[ex])

    l_step.wait()
    l_decay.wait()
    dec = decay_ref[...]
    row4 = iota((HEADS, L), 0)
    coef = jnp.zeros((HEADS, L), F32)
    for h in range(HEADS):
        coef = jnp.where(row4 == h, dec[:, h : h + 1], coef)
    rate = step_ref[...] * coef
    log_decay = -rate
    gain_row = jnp.sqrt(one_minus_exp(2.0 * rate))
    ti = iota((L, L), 0)
    si = iota((L, L), 1)
    causal = ti >= si
    tri = jnp.where(causal, 1.0, 0.0).astype(F32)
    run_row = nt(log_decay, tri, EXACT)
    run_col = [
        nt(tri, jnp.broadcast_to(log_decay[h : h + 1, :], (L, L)), EXACT) for h in range(HEADS)
    ]
    rem_row = jnp.exp(run_row[:, L - 1 : L] - run_row) * gain_row
    first = si < HP
    eye = jnp.where(ti == si, 1.0, 0.0).astype(BF16)
    top = ti < HP
    rem_x = [
        nt(
            eye,
            jnp.where(
                top,
                jnp.broadcast_to(rem_row[2 * i : 2 * i + 1, :], (L, L)),
                jnp.broadcast_to(rem_row[2 * i + 1 : 2 * i + 2, :], (L, L)),
            ).astype(BF16),
        )
        for i in range(2)
    ]
    run_x = jnp.concatenate(
        [jnp.where(first, run_col[2 * i], run_col[2 * i + 1]) for i in range(2)], axis=1
    )

    l_x.wait()
    l_convw.wait()
    l_b.wait()
    ext[0:8, :] = jnp.zeros((8, 256), F32)
    ext[8 : 8 + L, :] = x_ref[...].astype(F32)
    ext[8 + L :, :] = jnp.zeros((8, 256), F32)
    cw = convw_ref[...]
    summed = cw[0:1, :] * ext[5 : 13 + L, :]
    for k in range(1, 4):
        summed = summed + cw[k : k + 1, :] * ext[5 + k : 13 + k + L, :]
    conv_own = silu(summed[:L]).astype(BF16).astype(F32)

    bm = b_ref[...]
    inner = iota((L, 256), 0) >= 3
    weighted = jnp.where(inner, conv_own * jnp.concatenate(rem_x, axis=1), 0.0).astype(BF16)
    state = tn(bm, weighted).astype(BF16)
    s1_send[...] = state.reshape(8, 16, 256)
    head_b = bm[0:16, :].astype(F32)
    ebuf[1 + z, 0:3, 0:256] = summed[0:3]
    ebuf[1 + z, 3:6, 0:256] = summed[L : L + 3]
    ebuf[1 + z, 6:7, 0:128] = head_b[0:1, :]
    ebuf[1 + z, 6:7, 128:256] = head_b[1:2, :]
    ebuf[1 + z, 7:8, 0:128] = head_b[2:3, :]
    ebuf[1 + z, 7:8, 128:256] = jnp.zeros((1, 128), F32)

    l_wq.wait()
    l_wkv.wait()
    l_pad.wait()
    l_mgain.wait()
    l_bnd.wait()
    prow = s // 2 - 8
    padf = pad_ref[...].astype(F32)
    mg = mgain_ref[...]
    pad_one = jnp.sum(jnp.where(iota((24, 128), 0) == prow, padf, 0.0), axis=0, keepdims=True)
    gain_one = jnp.sum(jnp.where(iota((32, 128), 0) == s // 2, mg, 0.0), axis=0, keepdims=True)
    both = pad_one * gain_one
    half = jnp.where(s % 2 == 1, both[:, 64:], both[:, :64])
    half = jnp.broadcast_to(half, (16, 64)).astype(BF16)
    pq = nn(half, wq_ref[...])
    pkv = nn(half, wkv_ref[...])
    pad_sq = jnp.sum(jnp.sum(padf * padf, axis=1, keepdims=True), axis=0, keepdims=True)
    lane1 = iota((1, 128), 1)
    bounds = bnd_ref[...]
    count = jnp.sum(jnp.where(bounds < NY * NZ * L, 1.0, 0.0), axis=1, keepdims=True)
    last = jnp.zeros((1, 128), F32)
    for h in range(HEADS):
        last = jnp.where(lane1 == h, run_col[h][L - 1 : L, :], last)
        for t in range(3):
            last = jnp.where(lane1 == 16 + 4 * t + h, rem_row[h : h + 1, t : t + 1], last)
    rows = [
        pq[0:1, 0:128],
        pq[0:1, 128:256],
        pkv[0:1, 0:128],
        pq[0:1, 256:384],
        pq[0:1, 384:512],
        pkv[0:1, 128:256],
        jnp.where(lane1 == z, count, 0.0),
        last,
    ]
    for i, row in enumerate(rows):
        ebuf[1 + z, i : i + 1, 256:384] = row

    pl.semaphore_wait(barrier, jnp.where(z == NZ - 1, 21 + NZ, 21))

    def w0_parts(yp):
        rg = lax.rem(yp, 4)
        ch = yp // 4
        r = pl.ds(pl.multiple_of(16 * rg, 16), 16)
        return (
            (
                wq_hbm.at[r, pl.ds(pl.multiple_of(256 * ch, 256), 256)],
                wbuf.at[ch, y, z, rg, :, pl.ds(0, 256)],
            ),
            (
                wkv_hbm.at[r, pl.ds(pl.multiple_of(128 * ch, 128), 128)],
                wbuf.at[ch, y, z, rg, :, pl.ds(256, 128)],
            ),
        )

    def w0_copies():
        copies = []
        for d in FAR_FIRST:
            yp = lax.rem(y + d, NY)
            for i, (src, dst) in enumerate(w0_parts(yp)):
                copies.append(
                    pltpu.make_async_remote_copy(
                        src_ref=src,
                        dst_ref=dst,
                        send_sem=w0_sem.at[0, i],
                        recv_sem=w0_sem.at[1, i],
                        device_id=at_y(yp),
                        device_id_type=MESH,
                    )
                )
        return copies

    @pl.when(y < 2)
    def _():
        for copy in w0_copies():
            copy.start()
        for i, (src, dst) in enumerate(w0_parts(y)):
            pltpu.make_async_copy(src, dst, w0_sem.at[1, i]).start()

    send_all(EDGE, z, at_z, lambda p: ebuf.at[1 + z], ebuf.at[1 + z], ebuf.at[pl.ds(1, 7)])

    def prev_copy(p):
        return pltpu.make_async_remote_copy(
            src_ref=ebuf.at[1 + z],
            dst_ref=ebuf.at[0],
            send_sem=prev_sem.at[0],
            recv_sem=prev_sem.at[1],
            device_id=(lax.rem(y + 1, NY) * NZ + p, hd),
            device_id_type=MESH,
        )

    @pl.when(z == NZ - 1)
    def _():
        for p in range(NZ):
            prev_copy(p).start()

    send_all(SCAN1, z, at_z, lambda p: s1_send.at[p], s1.at[z], s1.at[pl.ds(0, 7)])
    s1[z] = s1_send[z]

    for copy in load[10:]:
        copy.start()

    l_c.wait()
    cm = c_ref[...]
    affinity = jnp.where(causal, nt(cm, bm), 0.0)
    mix = []
    for h in range(HEADS):
        spread = jnp.where(causal, run_col[h] - run_row[h : h + 1, :], 0.0)
        mix.append((jnp.exp(spread) * (affinity * gain_row[h : h + 1, :])).astype(BF16))

    recv_all(EDGE)
    prev_copy(0).wait_recv()
    edges = ebuf[...]
    tiles = edges[1:, :, 256:384]
    stats_y[y] = jnp.sum(tiles, axis=0)
    send_all(STATS_Y, y, at_y, lambda p: stats_y.at[y], stats_y.at[y], stats_y.at[pl.ds(0, 7)])

    col = iota((128, 1024), 1)
    part_of = col // 256
    lane_of = lax.rem(col, 256) // HP + jnp.where(part_of > 0, 12 + 4 * part_of, 0)
    spread_head = jnp.where(iota((128, 1024), 0) == lane_of, 1.0, 0.0).astype(F32)
    by_head = nn(tiles[:, 7, :], spread_head, EXACT)
    lz = by_head[:, 0:256]

    nothing = (iota((8, 256), 0) + y) == 0
    edge_x, edge_b = [], []
    for t in range(3):
        earlier = jnp.where(nothing, 0.0, edges[0:8, 3 + t, 0:256])
        conv_t = silu(edges[1:, t, 0:256] + earlier).astype(BF16).astype(F32)
        edge_x.append(conv_t * by_head[:, 256 * (1 + t) : 256 * (2 + t)])
        edge_b.append(edges[1:, 6 + t // 2, 128 * (t % 2) : 128 * (t % 2 + 1)])
    edge_x = jnp.concatenate(edge_x, axis=0).astype(BF16)
    edge_b = jnp.concatenate(edge_b, axis=0).astype(BF16)
    pick_n = jnp.where(si == 16 * z + lax.rem(ti, 16), 1.0, 0.0).astype(BF16)
    spots = nt(pick_n, edge_b)
    same = iota((L, 24), 0) // 16 == lax.rem(iota((L, 24), 1), 8)
    added = nn(jnp.where(same, spots, 0.0).astype(BF16), edge_x).reshape(8, 16, 256)
    recv_all(SCAN1)
    acc = jnp.zeros((16, 256), F32)
    cum = jnp.zeros((1, 256), F32)
    before, cums = [], []
    for j in range(NZ):
        before.append(acc)
        cums.append(cum)
        acc = jnp.exp(lz[j : j + 1, :]) * acc + (s1[j].astype(F32) + added[j])
        cum = cum + lz[j : j + 1, :]
    s2[y] = acc.astype(BF16)
    send_all(SCAN2, y, at_y, lambda p: s2.at[y], s2.at[y], s2.at[pl.ds(0, 7)])

    for i, cols in enumerate((pl.ds(0, 256), pl.ds(256, 128))):
        finish(wbuf.at[0, :, z, 0, :, cols], w0_sem.at[1, i])
    rg_me = lax.rem(y, 4)
    ch_me = y // 4
    pieces7 = wbuf.at[ch_me, 0, pl.ds(0, 7), rg_me]
    own_a = wbuf.at[ch_me, 0, z, rg_me]
    own_b = wbuf.at[ch_me, 1, z, rg_me]
    send_all(W_AZ, z, at_z, lambda p: own_a, own_a, pieces7)
    send_all(W_BY, y, at_y, lambda p: own_b, own_b, pieces7)

    before_rows = pltpu.roll(ebuf[z, :, 0:256], 5, 0)
    lead = (iota((8, 256), 0) < 3) & (s > 0)
    top_rows = silu(summed[0:8] + jnp.where(lead, before_rows, 0.0)).astype(BF16).astype(F32)
    conv_f = jnp.concatenate([top_rows, conv_own[8:]], axis=0)
    conv = conv_f.astype(BF16)

    within = []
    zero = jnp.zeros((), BF16)
    for i in range(2):
        pair = conv[:, 128 * i : 128 * (i + 1)]
        stacked = jnp.concatenate(
            [jnp.where(first, pair, zero), jnp.where(first, zero, pair)], axis=0
        )
        within.append(nn(jnp.concatenate([mix[2 * i], mix[2 * i + 1]], axis=1), stacked))
    l_skip.wait()
    skip_v = skip_ref[...]
    skip = jnp.zeros((1, 256), F32)
    head_of = iota((1, 256), 1) // HP
    for h in range(HEADS):
        skip = jnp.where(head_of == h, skip_v[:, h : h + 1], skip)
    mixed_near = jnp.concatenate(within, axis=1) + skip * conv_f
    exp_run = jnp.exp(run_x)
    l_gate.wait()
    gate = silu(gate_ref[...].astype(F32))

    def block_a(p, cols, lo=0, n=8):
        return wbuf.at[p // 4, 0, pl.ds(lo, n), lax.rem(p, 4), :, cols]

    def block_b(p, cols, lo=0, n=2):
        return wbuf.at[pl.ds(lo, n), 1, p, :, :, cols]

    def rings(step, wait, kv):
        cols = pl.ds(256, 128) if kv else pl.ds(0, 256)
        for ex, me, where, block, whole in (
            (RING_A_KV if kv else RING_A_Q, y, at_y, block_a, 8),
            (RING_B_KV if kv else RING_B_Q, z, at_z, block_b, 2),
        ):
            sems = send_sem.at[ex + step], recv_sem.at[ex + step]
            if step == 3:
                moved = block(lax.rem(me + 4, 8), cols)
            elif block is block_a:
                moved = wbuf.at[:, 0, :, 0, :, cols]
            else:
                moved = wbuf.at[:, 1, pl.ds(0, 2), :, :, cols]
            if wait:
                finish(moved, sems[1])
                continue
            for way in range(2):
                ahead = lax.rem(me + (1 if way == 0 else 7), 8)
                of = lax.rem(me + (8 - step if way == 0 else step), 8)
                if step == 3:
                    part = block(of, cols, way * whole // 2, whole // 2)
                else:
                    part = block(of, cols)
                pltpu.make_async_remote_copy(
                    src_ref=part,
                    dst_ref=part,
                    send_sem=sems[0],
                    recv_sem=sems[1],
                    device_id=where(ahead),
                    device_id_type=MESH,
                ).start()
            pending.append((moved, sems[0]))

    recv_all(STATS_Y)
    ytiles = stats_y[...]
    pad_total = jnp.sum(ytiles, axis=0)
    ly = nn(ytiles[:, 7, :], spread_head[:, 0:256], EXACT)

    recv_all(SCAN2)
    rows_before = jnp.zeros((16, 256), F32)
    for j in range(NY - 1):
        longer = jnp.exp(ly[j : j + 1, :]) * rows_before + s2[j].astype(F32)
        rows_before = jnp.where(j < y, longer, rows_before)
    for j in range(NZ):
        s3_send[j] = (before[j] + jnp.exp(cums[j]) * rows_before).astype(BF16)
    send_all(SCAN3, z, at_z, lambda p: s3_send.at[p], s3.at[z], s3.at[pl.ds(0, 7)])
    s3[z] = s3_send[z]

    l_ngain.wait()
    bnd = bounds - s * L
    byte_at = iota((L, CAP), 0)
    slot_at = iota((L, CAP), 1)
    usable = bounds < NY * NZ * L
    picker = jnp.where((byte_at == bnd) & usable, 1.0, 0.0).astype(BF16)
    upto = jnp.where((bnd <= byte_at) & usable, 1.0, 0.0)
    newest = jnp.sum(upto, axis=1, keepdims=True) - 1.0
    spreader = jnp.where(slot_at.astype(F32) == newest, 1.0, 0.0).astype(BF16)
    l_res.wait()
    res = res_ref[...]
    res_span = tn(picker, res)

    lane = iota((CAP, 128), 1)
    counts = ytiles[:, 6, :]
    lane8 = iota((8, 128), 1)
    ahead = (lane8 < NZ) & (iota((8, 128), 0) * NZ + lane8 < s)
    offset = jnp.sum(jnp.where(ahead, counts, 0.0), axis=0, keepdims=True)
    offset = jnp.sum(offset, axis=1, keepdims=True)
    place = iota((CAP, 128), 0).astype(F32) + offset
    freq = jnp.exp(
        lax.rem(lane, HD // 2).astype(F32) * (-2.0 * math.log(THETA) / HD)
    )
    angle = place * freq
    cosine = jnp.cos(angle)
    sine = jnp.where(lane < HD // 2, -jnp.sin(angle), jnp.sin(angle))

    recv_all(W_AZ)
    recv_all(W_BY)
    rings(0, False, True)
    rings(0, False, False)

    recv_all(SCAN3)
    entering = nn(cm, s3[...].reshape(128, 256)) * exp_run
    gated = (mixed_near + entering) * gate
    mean_sq = jnp.sum(gated * gated, axis=1, keepdims=True) * (1.0 / 256)
    normed = (gated * lax.rsqrt(mean_sq + EPSILON) * ngain_ref[...]).astype(BF16)
    l_mo.wait()
    picked = tn(picker, normed).astype(BF16)
    span_part = nn(picked, mo_ref[...]).astype(BF16)
    for j in range(NHD):
        sp_send[j] = span_part[:, 128 * j : 128 * (j + 1)]
    send_all(SPAN_RS, hd, at_h, lambda p: sp_send.at[p], sp_recv.at[hd], sp_recv.at[pl.ds(0, 7)])
    sp_recv[hd] = sp_send[hd]

    rings(0, True, True)
    rings(1, False, True)
    rings(0, True, False)
    rings(1, False, False)

    enc_part = nn(normed, mo_ref[...]).astype(BF16)
    for j in range(NHD):
        en_send[j] = enc_part[:, 128 * j : 128 * (j + 1)]
    en_recv[hd] = en_send[hd]

    rings(1, True, True)
    rings(2, False, True)
    rings(1, True, False)
    rings(2, False, False)

    recv_all(SPAN_RS)
    span_share = (res_span + jnp.sum(sp_recv[...].astype(F32), axis=0)).astype(BF16)
    ag[hd] = span_share
    send_all(SPAN_AG, hd, at_h, lambda p: ag.at[hd], ag.at[hd], ag.at[pl.ds(0, 7)])

    rings(2, True, True)
    rings(3, False, True)
    rings(2, True, False)
    rings(3, False, False)

    key = iota((512, 128), 0)
    key_y = lax.rem(y + 16 - (key // 128) * sy, NY)
    key_z = lax.rem(z + 16 - lax.rem(key // CAP, 4) * sz, NZ)
    expand = jnp.where(iota((512, 128), 1) == key_z, 1.0, 0.0).astype(BF16)
    per_row = nt(expand, jnp.concatenate([ytiles[:, 6, :], ytiles[:, 6, :]], axis=0).astype(BF16))
    lane16 = iota((512, 16), 1)
    key_count = jnp.sum(
        jnp.where(lane16 == lax.rem(y + 16 - (iota((512, 16), 0) // 128) * sy, NY), per_row, 0.0),
        axis=1,
        keepdims=True,
    )
    key_slot = lax.rem(key, CAP)
    key_rank = (key_y * NZ + key_z) * CAP + key_slot
    key_rank = jnp.where(key_slot.astype(F32) < key_count, key_rank, NY * NZ * CAP)
    key_ranks[...] = key_rank
    query = iota((1, 512), 1)
    query_rank = (
        (
            lax.rem(y + 8 - py + query // 256, NY) * NZ
            + lax.rem(z + 8 - pz + lax.rem(query // 128, 2), NZ)
        )
        * CAP
        + lax.rem(query, CAP)
    )

    recv_all(SPAN_AG)
    sq = jnp.zeros((CAP, 128), F32)
    pieces = []
    for j in range(NHD):
        piece = ag[j].astype(F32)
        sq = sq + piece * piece
        pieces.append((piece * mg[j : j + 1, :]).astype(BF16))
    sq = jnp.sum(sq, axis=1, keepdims=True)
    scale = lax.rsqrt((sq + pad_sq) * (1.0 / D_MAIN) + EPSILON)
    span_x = jnp.concatenate(pieces, axis=1)
    rings(3, True, True)
    def project(ch, lo, n):
        return nn(span_x, wbuf[ch, :, :, :, :, lo : lo + n].reshape(1024, n))

    def column(part, i):
        return (part + pad_total[i : i + 1, :]) * scale

    def rotate(v):
        return (v * cosine + pltpu.roll(v, HD // 2, 1) * sine).astype(BF16)

    kvbuf[0, 0] = rotate(column(project(0, 256, 128), 2))
    kvbuf[0, 1] = column(project(1, 256, 128), 5).astype(BF16)

    def kv_copy(i, j):
        return pltpu.make_async_remote_copy(
            src_ref=kvbuf.at[0],
            dst_ref=kvbuf.at[4 * i + j],
            send_sem=send_sem.at[KV],
            recv_sem=recv_sem.at[KV],
            device_id=at_slot(i, j),
            device_id_type=MESH,
        )

    for i, j in SLOTS:
        kv_copy(i, j).start()
    pending.append((kvbuf.at[pl.ds(0, 15)], send_sem.at[KV]))
    mine = 2 * py + pz

    rings(3, True, False)
    for ch in range(2):
        pair = project(ch, 0, 256)
        for h in range(2):
            at = CAP * (2 * ch + h)
            part = pair[:, 128 * h : 128 * (h + 1)]
            qbuf[mine, at : at + CAP, :] = rotate(column(part, 3 * ch + h))

    def group_copy(i, e, src, dst):
        return pltpu.make_async_remote_copy(
            src_ref=src,
            dst_ref=dst,
            send_sem=send_sem.at[i],
            recv_sem=recv_sem.at[i],
            device_id=member(e)[0],
            device_id_type=MESH,
        )

    for e in range(1, 4):
        group_copy(QUERIES, e, qbuf.at[mine], qbuf.at[mine]).start()
    pending.append((qbuf.at[pl.ds(0, 3)], send_sem.at[QUERIES]))

    send_all(ENC_RS, hd, at_h, lambda p: en_send.at[p], en_recv.at[hd], en_recv.at[pl.ds(0, 7)])

    finish(qbuf.at[pl.ds(0, 3)], recv_sem.at[QUERIES])
    finish(kvbuf.at[pl.ds(0, 15)], recv_sem.at[KV])

    kv = kvbuf[...]
    keys = kv[:, 0].reshape(512, HD)
    values = kv[:, 1].reshape(512, HD)
    ranks = key_ranks[...]
    unit = 1.0 / math.sqrt(HD)
    for m in range(4):
        scores = nt(keys, qbuf[m])
        allowed = ranks <= query_rank[:, 128 * m : 128 * (m + 1)]
        scores = jnp.where(allowed, scores * unit, -1e30)
        top = jnp.max(scores, axis=0, keepdims=True)
        weights = jnp.exp(scores - top)
        o_send[m] = tn(values, weights.astype(BF16)).astype(BF16)
        m_send[m, 0:1, :] = top
        m_send[m, 1:2, :] = jnp.sum(weights, axis=0, keepdims=True)

    for e in range(1, 4):
        place_e = member(e)[1]
        group_copy(OUT_SUMS, e, o_send.at[place_e], o_recv.at[e]).start()
        group_copy(OUT_STATS, e, m_send.at[place_e], m_recv.at[e]).start()
    sums3, stats3 = o_recv.at[pl.ds(1, 3)], m_recv.at[pl.ds(1, 3)]
    pending.append((sums3, send_sem.at[OUT_SUMS]))
    pending.append((stats3, send_sem.at[OUT_STATS]))
    o_recv[0] = o_send[mine]
    m_recv[0] = m_send[mine]

    finish(sums3, recv_sem.at[OUT_SUMS])
    finish(stats3, recv_sem.at[OUT_STATS])

    tops = m_recv[:, 0, :]
    highest = jnp.max(tops, axis=0, keepdims=True)
    shrink = jnp.exp(tops - highest)
    total = jnp.sum(shrink * m_recv[:, 1, :], axis=0, keepdims=True)
    summed_o = jnp.zeros((HD, 128), F32)
    for e in range(4):
        summed_o = summed_o + shrink[e : e + 1, :] * o_recv[e].astype(F32)
    attended = (summed_o / total).T.astype(BF16)

    l_mw.wait()
    att = jnp.concatenate([attended[CAP * i : CAP * (i + 1), :] for i in range(4)], axis=1)
    main_part = nn(att, mw_ref[...]).astype(BF16)
    for j in range(NHD):
        mn_send[j] = main_part[:, 128 * j : 128 * (j + 1)]
    send_all(MAIN_RS, hd, at_h, lambda p: mn_send.at[p], mn_recv.at[hd], mn_recv.at[pl.ds(0, 7)])
    mn_recv[hd] = mn_send[hd]
    recv_all(ENC_RS)
    encoded = (res.astype(F32) + jnp.sum(en_recv[...].astype(F32), axis=0)).astype(BF16)

    recv_all(MAIN_RS)
    main_rows = (span_share.astype(F32) + jnp.sum(mn_recv[...].astype(F32), axis=0)).astype(BF16)
    out_ref[...] = (encoded.astype(F32) + nn(spreader, main_rows)).astype(BF16)

    for blocks, sem in pending:
        finish(blocks, sem)

    @pl.when(y < 2)
    def _():
        for i, cols in enumerate((pl.ds(0, 256), pl.ds(256, 128))):
            finish(wbuf.at[0, 0, pl.ds(0, 7), 0, :, cols], w0_sem.at[0, i])

    @pl.when(z == NZ - 1)
    def _():
        finish(ebuf.at[pl.ds(0, NZ)], prev_sem.at[0])


def shards(
    byte_stream,
    gate_stream,
    conv_weight,
    state_write,
    state_read,
    step_size,
    decay_coef,
    skip_gain,
    norm_gain,
    mixer_out,
    residual,
    boundaries,
    span_counts,
    span_offsets,
    pad_vector,
    main_gain,
    query_weight,
    key_value_weight,
    main_out_weight,
):
    far = pl.BlockSpec(memory_space=pl.ANY)
    near = pl.BlockSpec(memory_space=pltpu.VMEM)
    vm = pltpu.VMEM
    dma = pltpu.SemaphoreType.DMA
    return pl.pallas_call(
        kernel,
        out_shape=pltpu.VMEM((L, 128), BF16),
        in_specs=[far] * 17,
        out_specs=near,
        scratch_shapes=[
            vm((4, 256), F32),
            vm((HEADS, L), F32),
            vm((1, HEADS), F32),
            vm((1, HEADS), F32),
            vm((1, 256), F32),
            vm((1, CAP), jnp.int32),
            vm((24, 128), BF16),
            vm((32, 128), F32),
            vm((L, 256), BF16),
            vm((L, 256), BF16),
            vm((L, 128), BF16),
            vm((L, 128), BF16),
            vm((256, 1024), BF16),
            vm((L, 128), BF16),
            vm((64, 512), BF16),
            vm((64, 256), BF16),
            vm((512, 1024), BF16),
            vm((L + 16, 256), F32),
            vm((9, 8, 384), F32),
            vm((8, 8, 128), F32),
            vm((2, 2, 8, 4, 16, 384), BF16),
            vm((8, 16, 256), BF16),
            vm((8, 16, 256), BF16),
            vm((8, 16, 256), BF16),
            vm((8, 16, 256), BF16),
            vm((8, 16, 256), BF16),
            vm((8, CAP, 128), BF16),
            vm((8, CAP, 128), BF16),
            vm((8, CAP, 128), BF16),
            vm((8, L, 128), BF16),
            vm((8, L, 128), BF16),
            vm((16, 2, CAP, 128), BF16),
            vm((4, 128, 128), BF16),
            vm((512, 128), jnp.int32),
            vm((4, 128, 128), BF16),
            vm((4, 8, 128), F32),
            vm((4, 128, 128), BF16),
            vm((4, 8, 128), F32),
            vm((8, CAP, 128), BF16),
            vm((8, CAP, 128), BF16),
            dma((17,)),
            dma((2,)),
            dma((2, 2)),
            dma((N_SEM,)),
            dma((N_SEM,)),
        ],
        compiler_params=pltpu.CompilerParams(
            collective_id=0, has_side_effects=True, vmem_limit_bytes=56 * 1024 * 1024
        ),
        cost_estimate=pl.CostEstimate(flops=10**9, bytes_accessed=4 * 10**6, transcendentals=10**6),
    )(
        byte_stream,
        gate_stream,
        conv_weight,
        state_write,
        state_read,
        step_size.T,
        decay_coef.reshape(1, HEADS),
        skip_gain.reshape(1, HEADS),
        norm_gain.reshape(1, 256),
        mixer_out,
        residual,
        boundaries,
        pad_vector.reshape(24, 128),
        main_gain.reshape(32, 128),
        query_weight,
        key_value_weight,
        main_out_weight,
    )


def solution(mesh):
    in_specs = (
        P("seq", "head"),
        P("seq", "head"),
        P(None, "head"),
        P("seq", None),
        P("seq", None),
        P("seq", "head"),
        P("head"),
        P("head"),
        P("head"),
        P("head", None),
        P("seq", None),
        P("seq", None),
        P("seq"),
        P("seq"),
        P(),
        P(),
        P("seq", "head"),
        P("seq", "head"),
        P("head", None),
    )
    out_specs = P("seq", "head")
    return jax.shard_map(shards, mesh=mesh, in_specs=in_specs, out_specs=out_specs, check_vma=False)
```

```python
import functools
import math

import jax
import jax.numpy as jnp
from jax import lax
from jax.experimental import pallas as pl
from jax.experimental.pallas import tpu as pltpu
from jax.sharding import PartitionSpec as P

F32 = jnp.float32
BF16 = jnp.bfloat16
MESH = pl.DeviceIdType.MESH
EXACT = lax.Precision.HIGHEST

NY = 8
NZ = 8
NHD = 8
L = 128
HEADS = 4
HP = 64
CAP = 32
HD = 128
D_MAIN = 4096
THETA = 500000.0
EPSILON = 1e-05
FAR_FIRST = (4, 3, 5, 2, 6, 1, 7)
SLOTS = sorted(((i, j) for i in range(4) for j in range(4) if i + j > 0), key=lambda t: -t[0] - t[1])

(
    EDGE,
    STATS_Y,
    W_AZ,
    W_BY,
    SCAN1,
    SCAN2,
    SCAN3,
    SPAN_RS,
    SPAN_AG,
    ENC_RS,
    MAIN_RS,
    KV,
    QUERIES,
    OUT_SUMS,
    OUT_STATS,
    N_EX,
) = range(16)
RING_KV, RING_Q, N_SEM = (N_EX + 4 * i for i in range(3))


def nn(a, b, precision=None):
    return lax.dot_general(
        a, b, (((1,), (0,)), ((), ())), precision=precision, preferred_element_type=F32
    )


def nt(a, b, precision=None):
    return lax.dot_general(
        a, b, (((1,), (1,)), ((), ())), precision=precision, preferred_element_type=F32
    )


def tn(a, b, precision=None):
    return lax.dot_general(
        a, b, (((0,), (0,)), ((), ())), precision=precision, preferred_element_type=F32
    )


def iota(shape, dim):
    return lax.broadcasted_iota(jnp.int32, shape, dim)


def silu(v):
    return v / (1.0 + jnp.exp(-v))


def one_minus_exp(u):
    series = u * (
        1.0
        - u
        * (
            1.0 / 2
            - u * (1.0 / 6 - u * (1.0 / 24 - u * (1.0 / 120 - u * (1.0 / 720 - u / 5040))))
        )
    )
    return jnp.where(u < 0.3, series, 1.0 - jnp.exp(-u))


def kernel(
    x_hbm,
    gate_hbm,
    convw_hbm,
    b_hbm,
    c_hbm,
    step_hbm,
    decay_hbm,
    skip_hbm,
    ngain_hbm,
    mo_hbm,
    res_hbm,
    bnd_hbm,
    pad_hbm,
    mgain_hbm,
    wq_hbm,
    wkv_hbm,
    mw_hbm,
    out_ref,
    convw_ref,
    step_ref,
    decay_ref,
    skip_ref,
    ngain_ref,
    bnd_ref,
    pad_ref,
    mgain_ref,
    x_ref,
    gate_ref,
    b_ref,
    c_ref,
    mo_ref,
    res_ref,
    wq_ref,
    wkv_ref,
    mw_ref,
    ext,
    ebuf,
    stats_y,
    wbuf,
    s1_send,
    s1,
    s2,
    s3_send,
    s3,
    sp_send,
    sp_recv,
    ag,
    en_send,
    en_recv,
    kvbuf,
    qbuf,
    key_ranks,
    o_send,
    m_send,
    o_recv,
    m_recv,
    mn_send,
    mn_recv,
    local_sem,
    prev_sem,
    w0_sem,
    send_sem,
    recv_sem,
):
    s = lax.axis_index("seq")
    hd = lax.axis_index("head")
    y = s // NZ
    z = s % NZ

    def at_z(p):
        return (y * NZ + p, hd)

    def at_y(p):
        return (p * NZ + z, hd)

    def at_h(p):
        return (s, p)

    py, pz = lax.rem(y + hd, 2), lax.rem(z + hd, 2)
    sy, sz = 1 - 2 * py, 1 - 2 * pz

    def at_slot(i, j):
        yc = lax.rem(y + 8 + (0, -1, 2, -3)[i] * sy, NY)
        zc = lax.rem(z + 8 + (0, -1, 2, -3)[j] * sz, NZ)
        return (yc * NZ + zc, hd)

    def member(e):
        yc = lax.rem(y + 8 + sy, NY) if e // 2 else y
        zc = lax.rem(z + 8 + sz, NZ) if e % 2 else z
        return (yc * NZ + zc, hd), 2 * lax.rem(yc + hd, 2) + lax.rem(zc + hd, 2)

    barrier = pltpu.get_barrier_semaphore()
    greet = [(lax.rem(y + NY - 1, NY) * NZ + NZ - 1, hd)]
    for d in range(1, 8):
        greet += [at_z(lax.rem(z + d, NZ)), at_y(lax.rem(y + d, NY)), at_h(lax.rem(hd + d, NHD))]
    for to in greet:
        pl.semaphore_signal(barrier, inc=1, device_id=to, device_id_type=MESH)

    loads = [
        (step_hbm, step_ref),
        (decay_hbm, decay_ref),
        (x_hbm, x_ref),
        (convw_hbm, convw_ref),
        (b_hbm, b_ref),
        (wq_hbm, wq_ref),
        (wkv_hbm, wkv_ref),
        (pad_hbm, pad_ref),
        (mgain_hbm, mgain_ref),
        (bnd_hbm, bnd_ref),
        (c_hbm, c_ref),
        (gate_hbm, gate_ref),
        (skip_hbm, skip_ref),
        (ngain_hbm, ngain_ref),
        (res_hbm.at[:, pl.ds(pl.multiple_of(hd * 128, 128), 128)], res_ref),
        (mo_hbm, mo_ref),
        (mw_hbm, mw_ref),
    ]
    load = [pltpu.make_async_copy(a, b, local_sem.at[i]) for i, (a, b) in enumerate(loads)]
    for copy in load[:10]:
        copy.start()
    l_step, l_decay, l_x, l_convw, l_b, l_wq, l_wkv, l_pad, l_mgain, l_bnd = load[:10]
    l_c, l_gate, l_skip, l_ngain, l_res, l_mo, l_mw = load[10:]

    pending = []
    sizes = {}

    def finish(blocks, sem):
        pltpu.make_async_copy(blocks, blocks, sem).wait()

    def send_all(ex, me, where, src, dst, seven):
        for d in FAR_FIRST:
            p = lax.rem(me + d, 8)
            pltpu.make_async_remote_copy(
                src_ref=src(p),
                dst_ref=dst,
                send_sem=send_sem.at[ex],
                recv_sem=recv_sem.at[ex],
                device_id=where(p),
                device_id_type=MESH,
            ).start()
        pending.append((seven, send_sem.at[ex]))
        sizes[ex] = seven

    def recv_all(ex):
        finish(sizes[ex], recv_sem.at[ex])

    l_step.wait()
    l_decay.wait()
    dec = decay_ref[...]
    row4 = iota((HEADS, L), 0)
    coef = jnp.zeros((HEADS, L), F32)
    for h in range(HEADS):
        coef = jnp.where(row4 == h, dec[:, h : h + 1], coef)
    rate = step_ref[...] * coef
    log_decay = -rate
    gain_row = jnp.sqrt(one_minus_exp(2.0 * rate))
    ti = iota((L, L), 0)
    si = iota((L, L), 1)
    causal = ti >= si
    tri = jnp.where(causal, 1.0, 0.0).astype(F32)
    run_row = nt(log_decay, tri, EXACT)
    run_col = [
        nt(tri, jnp.broadcast_to(log_decay[h : h + 1, :], (L, L)), EXACT) for h in range(HEADS)
    ]
    rem_row = jnp.exp(run_row[:, L - 1 : L] - run_row) * gain_row
    first = si < HP
    eye = jnp.where(ti == si, 1.0, 0.0).astype(BF16)
    top = ti < HP
    rem_x = [
        nt(
            eye,
            jnp.where(
                top,
                jnp.broadcast_to(rem_row[2 * i : 2 * i + 1, :], (L, L)),
                jnp.broadcast_to(rem_row[2 * i + 1 : 2 * i + 2, :], (L, L)),
            ).astype(BF16),
        )
        for i in range(2)
    ]
    run_x = jnp.concatenate(
        [jnp.where(first, run_col[2 * i], run_col[2 * i + 1]) for i in range(2)], axis=1
    )

    l_x.wait()
    l_convw.wait()
    l_b.wait()
    ext[0:8, :] = jnp.zeros((8, 256), F32)
    ext[8 : 8 + L, :] = x_ref[...].astype(F32)
    ext[8 + L :, :] = jnp.zeros((8, 256), F32)
    cw = convw_ref[...]
    summed = cw[0:1, :] * ext[5 : 13 + L, :]
    for k in range(1, 4):
        summed = summed + cw[k : k + 1, :] * ext[5 + k : 13 + k + L, :]
    conv_own = silu(summed[:L]).astype(BF16).astype(F32)

    bm = b_ref[...]
    inner = iota((L, 256), 0) >= 3
    weighted = jnp.where(inner, conv_own * jnp.concatenate(rem_x, axis=1), 0.0).astype(BF16)
    state = tn(bm, weighted).astype(BF16)
    s1_send[...] = state.reshape(8, 16, 256)
    head_b = bm[0:16, :].astype(F32)
    ebuf[1 + z, 0:3, 0:256] = summed[0:3]
    ebuf[1 + z, 3:6, 0:256] = summed[L : L + 3]
    ebuf[1 + z, 6:7, 0:128] = head_b[0:1, :]
    ebuf[1 + z, 6:7, 128:256] = head_b[1:2, :]
    ebuf[1 + z, 7:8, 0:128] = head_b[2:3, :]
    ebuf[1 + z, 7:8, 128:256] = jnp.zeros((1, 128), F32)

    l_wq.wait()
    l_wkv.wait()
    l_pad.wait()
    l_mgain.wait()
    l_bnd.wait()
    prow = s // 2 - 8
    padf = pad_ref[...].astype(F32)
    mg = mgain_ref[...]
    pad_one = jnp.sum(jnp.where(iota((24, 128), 0) == prow, padf, 0.0), axis=0, keepdims=True)
    gain_one = jnp.sum(jnp.where(iota((32, 128), 0) == s // 2, mg, 0.0), axis=0, keepdims=True)
    both = pad_one * gain_one
    half = jnp.where(s % 2 == 1, both[:, 64:], both[:, :64])
    half = jnp.broadcast_to(half, (16, 64)).astype(BF16)
    pq = nn(half, wq_ref[...])
    pkv = nn(half, wkv_ref[...])
    pad_sq = jnp.sum(jnp.sum(padf * padf, axis=1, keepdims=True), axis=0, keepdims=True)
    lane1 = iota((1, 128), 1)
    bounds = bnd_ref[...]
    count = jnp.sum(jnp.where(bounds < NY * NZ * L, 1.0, 0.0), axis=1, keepdims=True)
    last = jnp.zeros((1, 128), F32)
    for h in range(HEADS):
        last = jnp.where(lane1 == h, run_col[h][L - 1 : L, :], last)
        for t in range(3):
            last = jnp.where(lane1 == 16 + 4 * t + h, rem_row[h : h + 1, t : t + 1], last)
    rows = [
        pq[0:1, 0:128],
        pq[0:1, 128:256],
        pkv[0:1, 0:128],
        pq[0:1, 256:384],
        pq[0:1, 384:512],
        pkv[0:1, 128:256],
        jnp.where(lane1 == z, count, 0.0),
        last,
    ]
    for i, row in enumerate(rows):
        ebuf[1 + z, i : i + 1, 256:384] = row

    pl.semaphore_wait(barrier, jnp.where(z == NZ - 1, 21 + NZ, 21))

    def w0_parts(yp):
        rg = lax.rem(yp, 4)
        ch = yp // 4
        r = pl.ds(pl.multiple_of(16 * rg, 16), 16)
        return (
            (
                wq_hbm.at[r, pl.ds(pl.multiple_of(256 * ch, 256), 256)],
                wbuf.at[ch, y, z, rg, :, pl.ds(0, 256)],
            ),
            (
                wkv_hbm.at[r, pl.ds(pl.multiple_of(128 * ch, 128), 128)],
                wbuf.at[ch, y, z, rg, :, pl.ds(256, 128)],
            ),
        )

    def w0_copies():
        copies = []
        for d in FAR_FIRST:
            yp = lax.rem(y + d, NY)
            for i, (src, dst) in enumerate(w0_parts(yp)):
                copies.append(
                    pltpu.make_async_remote_copy(
                        src_ref=src,
                        dst_ref=dst,
                        send_sem=w0_sem.at[0, i],
                        recv_sem=w0_sem.at[1, i],
                        device_id=at_y(yp),
                        device_id_type=MESH,
                    )
                )
        return copies

    @pl.when(y < 2)
    def _():
        for copy in w0_copies():
            copy.start()
        for i, (src, dst) in enumerate(w0_parts(y)):
            pltpu.make_async_copy(src, dst, w0_sem.at[1, i]).start()

    send_all(EDGE, z, at_z, lambda p: ebuf.at[1 + z], ebuf.at[1 + z], ebuf.at[pl.ds(1, 7)])

    def prev_copy(p):
        return pltpu.make_async_remote_copy(
            src_ref=ebuf.at[1 + z],
            dst_ref=ebuf.at[0],
            send_sem=prev_sem.at[0],
            recv_sem=prev_sem.at[1],
            device_id=(lax.rem(y + 1, NY) * NZ + p, hd),
            device_id_type=MESH,
        )

    @pl.when(z == NZ - 1)
    def _():
        for p in range(NZ):
            prev_copy(p).start()

    send_all(SCAN1, z, at_z, lambda p: s1_send.at[p], s1.at[z], s1.at[pl.ds(0, 7)])
    s1[z] = s1_send[z]

    for copy in load[10:]:
        copy.start()

    l_c.wait()
    cm = c_ref[...]
    affinity = jnp.where(causal, nt(cm, bm), 0.0)
    mix = []
    for h in range(HEADS):
        spread = jnp.where(causal, run_col[h] - run_row[h : h + 1, :], 0.0)
        mix.append((jnp.exp(spread) * (affinity * gain_row[h : h + 1, :])).astype(BF16))

    recv_all(EDGE)
    prev_copy(0).wait_recv()
    edges = ebuf[...]
    tiles = edges[1:, :, 256:384]
    stats_y[y] = jnp.sum(tiles, axis=0)
    send_all(STATS_Y, y, at_y, lambda p: stats_y.at[y], stats_y.at[y], stats_y.at[pl.ds(0, 7)])

    col = iota((128, 1024), 1)
    part_of = col // 256
    lane_of = lax.rem(col, 256) // HP + jnp.where(part_of > 0, 12 + 4 * part_of, 0)
    spread_head = jnp.where(iota((128, 1024), 0) == lane_of, 1.0, 0.0).astype(F32)
    by_head = nn(tiles[:, 7, :], spread_head, EXACT)
    lz = by_head[:, 0:256]

    nothing = (iota((8, 256), 0) + y) == 0
    edge_x, edge_b = [], []
    for t in range(3):
        earlier = jnp.where(nothing, 0.0, edges[0:8, 3 + t, 0:256])
        conv_t = silu(edges[1:, t, 0:256] + earlier).astype(BF16).astype(F32)
        edge_x.append(conv_t * by_head[:, 256 * (1 + t) : 256 * (2 + t)])
        edge_b.append(edges[1:, 6 + t // 2, 128 * (t % 2) : 128 * (t % 2 + 1)])
    edge_x = jnp.concatenate(edge_x, axis=0).astype(BF16)
    edge_b = jnp.concatenate(edge_b, axis=0).astype(BF16)
    pick_n = jnp.where(si == 16 * z + lax.rem(ti, 16), 1.0, 0.0).astype(BF16)
    spots = nt(pick_n, edge_b)
    same = iota((L, 24), 0) // 16 == lax.rem(iota((L, 24), 1), 8)
    added = nn(jnp.where(same, spots, 0.0).astype(BF16), edge_x).reshape(8, 16, 256)
    recv_all(SCAN1)
    acc = jnp.zeros((16, 256), F32)
    cum = jnp.zeros((1, 256), F32)
    before, cums = [], []
    for j in range(NZ):
        before.append(acc)
        cums.append(cum)
        acc = jnp.exp(lz[j : j + 1, :]) * acc + (s1[j].astype(F32) + added[j])
        cum = cum + lz[j : j + 1, :]
    s2[y] = acc.astype(BF16)
    send_all(SCAN2, y, at_y, lambda p: s2.at[y], s2.at[y], s2.at[pl.ds(0, 7)])

    for i, cols in enumerate((pl.ds(0, 256), pl.ds(256, 128))):
        finish(wbuf.at[0, :, z, 0, :, cols], w0_sem.at[1, i])
    rg_me = lax.rem(y, 4)
    ch_me = y // 4
    pieces7 = wbuf.at[ch_me, 0, pl.ds(0, 7), rg_me]
    own_a = wbuf.at[ch_me, 0, z, rg_me]
    own_b = wbuf.at[ch_me, 1, z, rg_me]
    send_all(W_AZ, z, at_z, lambda p: own_a, own_a, pieces7)
    send_all(W_BY, y, at_y, lambda p: own_b, own_b, pieces7)

    before_rows = pltpu.roll(ebuf[z, :, 0:256], 5, 0)
    lead = (iota((8, 256), 0) < 3) & (s > 0)
    top_rows = silu(summed[0:8] + jnp.where(lead, before_rows, 0.0)).astype(BF16).astype(F32)
    conv_f = jnp.concatenate([top_rows, conv_own[8:]], axis=0)
    conv = conv_f.astype(BF16)

    within = []
    zero = jnp.zeros((), BF16)
    for i in range(2):
        pair = conv[:, 128 * i : 128 * (i + 1)]
        stacked = jnp.concatenate(
            [jnp.where(first, pair, zero), jnp.where(first, zero, pair)], axis=0
        )
        within.append(nn(jnp.concatenate([mix[2 * i], mix[2 * i + 1]], axis=1), stacked))
    l_skip.wait()
    skip_v = skip_ref[...]
    skip = jnp.zeros((1, 256), F32)
    head_of = iota((1, 256), 1) // HP
    for h in range(HEADS):
        skip = jnp.where(head_of == h, skip_v[:, h : h + 1], skip)
    mixed_near = jnp.concatenate(within, axis=1) + skip * conv_f
    exp_run = jnp.exp(run_x)
    l_gate.wait()
    gate = silu(gate_ref[...].astype(F32))

    def block_a(p, cols, lo=0, n=8):
        return wbuf.at[p // 4, 0, pl.ds(lo, n), lax.rem(p, 4), :, cols]

    def block_b(p, cols, lo=0, n=2):
        return wbuf.at[pl.ds(lo, n), 1, p, :, :, cols]

    def rings(step, wait, kv):
        cols = pl.ds(256, 128) if kv else pl.ds(0, 256)
        ex = (RING_KV if kv else RING_Q) + step
        if step == 3:
            moved = wbuf.at[:, 0, pl.ds(0, 2), :, :, cols]
        else:
            moved = wbuf.at[:, :, pl.ds(0, 2), :, :, cols]
        if wait:
            finish(moved, recv_sem.at[ex])
            return
        pending.append((moved, send_sem.at[ex]))
        for me, where, block, whole in ((y, at_y, block_a, 8), (z, at_z, block_b, 2)):
            for way in range(2):
                ahead = lax.rem(me + (1 if way == 0 else 7), 8)
                of = lax.rem(me + (8 - step if way == 0 else step), 8)
                if step == 3:
                    part = block(of, cols, way * whole // 2, whole // 2)
                else:
                    part = block(of, cols)
                pltpu.make_async_remote_copy(
                    src_ref=part,
                    dst_ref=part,
                    send_sem=send_sem.at[ex],
                    recv_sem=recv_sem.at[ex],
                    device_id=where(ahead),
                    device_id_type=MESH,
                ).start()

    recv_all(STATS_Y)
    ytiles = stats_y[...]
    pad_total = jnp.sum(ytiles, axis=0)
    ly = nn(ytiles[:, 7, :], spread_head[:, 0:256], EXACT)

    recv_all(SCAN2)
    rows_before = jnp.zeros((16, 256), F32)
    for j in range(NY - 1):
        longer = jnp.exp(ly[j : j + 1, :]) * rows_before + s2[j].astype(F32)
        rows_before = jnp.where(j < y, longer, rows_before)
    for j in range(NZ):
        s3_send[j] = (before[j] + jnp.exp(cums[j]) * rows_before).astype(BF16)
    send_all(SCAN3, z, at_z, lambda p: s3_send.at[p], s3.at[z], s3.at[pl.ds(0, 7)])
    s3[z] = s3_send[z]

    recv_all(W_AZ)
    recv_all(W_BY)
    rings(0, False, True)
    rings(0, False, False)

    l_ngain.wait()
    bnd = bounds - s * L
    byte_at = iota((L, CAP), 0)
    slot_at = iota((L, CAP), 1)
    usable = bounds < NY * NZ * L
    picker = jnp.where((byte_at == bnd) & usable, 1.0, 0.0).astype(BF16)
    upto = jnp.where((bnd <= byte_at) & usable, 1.0, 0.0)
    newest = jnp.sum(upto, axis=1, keepdims=True) - 1.0
    spreader = jnp.where(slot_at.astype(F32) == newest, 1.0, 0.0).astype(BF16)
    l_res.wait()
    res = res_ref[...]
    res_span = tn(picker, res)

    span_pick = tn(picker, eye)
    span_c = nn(span_pick.astype(BF16), cm).astype(BF16)
    span_near = nn(span_pick, mixed_near, EXACT)
    span_run = nn(span_pick, exp_run, EXACT)
    span_gate = nn(span_pick, gate, EXACT)

    def normalize(near, read, run, opening, states):
        gated = (near + nn(read, states) * run) * opening
        mean_sq = jnp.sum(gated * gated, axis=1, keepdims=True) * (1.0 / 256)
        return (gated * lax.rsqrt(mean_sq + EPSILON) * ngain_ref[...]).astype(BF16)

    lane = iota((CAP, 128), 1)
    counts = ytiles[:, 6, :]
    lane8 = iota((8, 128), 1)
    ahead = (lane8 < NZ) & (iota((8, 128), 0) * NZ + lane8 < s)
    offset = jnp.sum(jnp.where(ahead, counts, 0.0), axis=0, keepdims=True)
    offset = jnp.sum(offset, axis=1, keepdims=True)
    place = iota((CAP, 128), 0).astype(F32) + offset
    freq = jnp.exp(
        lax.rem(lane, HD // 2).astype(F32) * (-2.0 * math.log(THETA) / HD)
    )
    angle = place * freq
    cosine = jnp.cos(angle)
    sine = jnp.where(lane < HD // 2, -jnp.sin(angle), jnp.sin(angle))

    recv_all(SCAN3)
    states = s3[...].reshape(128, 256)
    l_mo.wait()
    span_normed = normalize(span_near, span_c, span_run, span_gate, states)
    span_part = nn(span_normed, mo_ref[...]).astype(BF16)
    for j in range(NHD):
        sp_send[j] = span_part[:, 128 * j : 128 * (j + 1)]
    send_all(SPAN_RS, hd, at_h, lambda p: sp_send.at[p], sp_recv.at[hd], sp_recv.at[pl.ds(0, 7)])
    sp_recv[hd] = sp_send[hd]

    rings(0, True, True)
    rings(1, False, True)
    rings(0, True, False)
    rings(1, False, False)

    normed = normalize(mixed_near, cm, exp_run, gate, states)
    enc_part = nn(normed, mo_ref[...]).astype(BF16)
    for j in range(NHD):
        en_send[j] = enc_part[:, 128 * j : 128 * (j + 1)]
    en_recv[hd] = en_send[hd]

    rings(1, True, True)
    rings(2, False, True)
    rings(1, True, False)
    rings(2, False, False)

    recv_all(SPAN_RS)
    span_share = (res_span + jnp.sum(sp_recv[...].astype(F32), axis=0)).astype(BF16)
    ag[hd] = span_share
    send_all(SPAN_AG, hd, at_h, lambda p: ag.at[hd], ag.at[hd], ag.at[pl.ds(0, 7)])

    rings(2, True, True)
    rings(3, False, True)
    rings(2, True, False)
    rings(3, False, False)

    key = iota((512, 128), 0)
    key_y = lax.rem(y + 16 - (key // 128) * sy, NY)
    key_z = lax.rem(z + 16 - lax.rem(key // CAP, 4) * sz, NZ)
    expand = jnp.where(iota((512, 128), 1) == key_z, 1.0, 0.0).astype(BF16)
    per_row = nt(expand, jnp.concatenate([ytiles[:, 6, :], ytiles[:, 6, :]], axis=0).astype(BF16))
    lane16 = iota((512, 16), 1)
    key_count = jnp.sum(
        jnp.where(lane16 == lax.rem(y + 16 - (iota((512, 16), 0) // 128) * sy, NY), per_row, 0.0),
        axis=1,
        keepdims=True,
    )
    key_slot = lax.rem(key, CAP)
    key_rank = (key_y * NZ + key_z) * CAP + key_slot
    key_rank = jnp.where(key_slot.astype(F32) < key_count, key_rank, NY * NZ * CAP)
    key_ranks[...] = key_rank
    query = iota((1, 512), 1)
    query_rank = (
        (
            lax.rem(y + 8 - py + query // 256, NY) * NZ
            + lax.rem(z + 8 - pz + lax.rem(query // 128, 2), NZ)
        )
        * CAP
        + lax.rem(query, CAP)
    )

    recv_all(SPAN_AG)
    sq = jnp.zeros((CAP, 128), F32)
    pieces = []
    for j in range(NHD):
        piece = ag[j].astype(F32)
        sq = sq + piece * piece
        pieces.append((piece * mg[j : j + 1, :]).astype(BF16))
    sq = jnp.sum(sq, axis=1, keepdims=True)
    scale = lax.rsqrt((sq + pad_sq) * (1.0 / D_MAIN) + EPSILON)
    span_x = jnp.concatenate(pieces, axis=1)
    rings(3, True, True)
    def project(ch, lo, n):
        return nn(span_x, wbuf[ch, :, :, :, :, lo : lo + n].reshape(1024, n))

    def column(part, i):
        return (part + pad_total[i : i + 1, :]) * scale

    def rotate(v):
        return (v * cosine + pltpu.roll(v, HD // 2, 1) * sine).astype(BF16)

    kvbuf[0, 0] = rotate(column(project(0, 256, 128), 2))
    kvbuf[0, 1] = column(project(1, 256, 128), 5).astype(BF16)

    def kv_copy(i, j):
        return pltpu.make_async_remote_copy(
            src_ref=kvbuf.at[0],
            dst_ref=kvbuf.at[4 * i + j],
            send_sem=send_sem.at[KV],
            recv_sem=recv_sem.at[KV],
            device_id=at_slot(i, j),
            device_id_type=MESH,
        )

    for i, j in SLOTS:
        kv_copy(i, j).start()
    pending.append((kvbuf.at[pl.ds(0, 15)], send_sem.at[KV]))
    mine = 2 * py + pz

    rings(3, True, False)
    for ch in range(2):
        pair = project(ch, 0, 256)
        for h in range(2):
            at = CAP * (2 * ch + h)
            part = pair[:, 128 * h : 128 * (h + 1)]
            qbuf[mine, at : at + CAP, :] = rotate(column(part, 3 * ch + h))

    def group_copy(i, e, src, dst):
        return pltpu.make_async_remote_copy(
            src_ref=src,
            dst_ref=dst,
            send_sem=send_sem.at[i],
            recv_sem=recv_sem.at[i],
            device_id=member(e)[0],
            device_id_type=MESH,
        )

    for e in range(1, 4):
        group_copy(QUERIES, e, qbuf.at[mine], qbuf.at[mine]).start()
    pending.append((qbuf.at[pl.ds(0, 3)], send_sem.at[QUERIES]))

    send_all(ENC_RS, hd, at_h, lambda p: en_send.at[p], en_recv.at[hd], en_recv.at[pl.ds(0, 7)])

    finish(qbuf.at[pl.ds(0, 3)], recv_sem.at[QUERIES])
    finish(kvbuf.at[pl.ds(0, 15)], recv_sem.at[KV])

    kv = kvbuf[...]
    keys = kv[:, 0].reshape(512, HD)
    values = kv[:, 1].reshape(512, HD)
    ranks = key_ranks[...]
    unit = 1.0 / math.sqrt(HD)
    for m in range(4):
        scores = nt(keys, qbuf[m])
        allowed = ranks <= query_rank[:, 128 * m : 128 * (m + 1)]
        scores = jnp.where(allowed, scores * unit, -1e30)
        top = jnp.max(scores, axis=0, keepdims=True)
        weights = jnp.exp(scores - top)
        o_send[m] = tn(values, weights.astype(BF16)).astype(BF16)
        m_send[m, 0:1, :] = top
        m_send[m, 1:2, :] = jnp.sum(weights, axis=0, keepdims=True)

    for e in range(1, 4):
        place_e = member(e)[1]
        group_copy(OUT_SUMS, e, o_send.at[place_e], o_recv.at[e]).start()
        group_copy(OUT_STATS, e, m_send.at[place_e], m_recv.at[e]).start()
    sums3, stats3 = o_recv.at[pl.ds(1, 3)], m_recv.at[pl.ds(1, 3)]
    pending.append((sums3, send_sem.at[OUT_SUMS]))
    pending.append((stats3, send_sem.at[OUT_STATS]))
    o_recv[0] = o_send[mine]
    m_recv[0] = m_send[mine]

    finish(sums3, recv_sem.at[OUT_SUMS])
    finish(stats3, recv_sem.at[OUT_STATS])

    tops = m_recv[:, 0, :]
    highest = jnp.max(tops, axis=0, keepdims=True)
    shrink = jnp.exp(tops - highest)
    total = jnp.sum(shrink * m_recv[:, 1, :], axis=0, keepdims=True)
    summed_o = jnp.zeros((HD, 128), F32)
    for e in range(4):
        summed_o = summed_o + shrink[e : e + 1, :] * o_recv[e].astype(F32)
    attended = (summed_o / total).T.astype(BF16)

    l_mw.wait()
    att = jnp.concatenate([attended[CAP * i : CAP * (i + 1), :] for i in range(4)], axis=1)
    main_part = nn(att, mw_ref[...]).astype(BF16)
    for j in range(NHD):
        mn_send[j] = main_part[:, 128 * j : 128 * (j + 1)]
    send_all(MAIN_RS, hd, at_h, lambda p: mn_send.at[p], mn_recv.at[hd], mn_recv.at[pl.ds(0, 7)])
    mn_recv[hd] = mn_send[hd]
    recv_all(ENC_RS)
    encoded = (res.astype(F32) + jnp.sum(en_recv[...].astype(F32), axis=0)).astype(BF16)

    recv_all(MAIN_RS)
    main_rows = (span_share.astype(F32) + jnp.sum(mn_recv[...].astype(F32), axis=0)).astype(BF16)
    out_ref[...] = (encoded.astype(F32) + nn(spreader, main_rows)).astype(BF16)

    for blocks, sem in pending:
        finish(blocks, sem)

    @pl.when(y < 2)
    def _():
        for i, cols in enumerate((pl.ds(0, 256), pl.ds(256, 128))):
            finish(wbuf.at[0, 0, pl.ds(0, 7), 0, :, cols], w0_sem.at[0, i])

    @pl.when(z == NZ - 1)
    def _():
        finish(ebuf.at[pl.ds(0, NZ)], prev_sem.at[0])


def shards(
    byte_stream,
    gate_stream,
    conv_weight,
    state_write,
    state_read,
    step_size,
    decay_coef,
    skip_gain,
    norm_gain,
    mixer_out,
    residual,
    boundaries,
    span_counts,
    span_offsets,
    pad_vector,
    main_gain,
    query_weight,
    key_value_weight,
    main_out_weight,
):
    far = pl.BlockSpec(memory_space=pl.ANY)
    near = pl.BlockSpec(memory_space=pltpu.VMEM)
    vm = pltpu.VMEM
    dma = pltpu.SemaphoreType.DMA
    return pl.pallas_call(
        kernel,
        out_shape=pltpu.VMEM((L, 128), BF16),
        in_specs=[far] * 17,
        out_specs=near,
        scratch_shapes=[
            vm((4, 256), F32),
            vm((HEADS, L), F32),
            vm((1, HEADS), F32),
            vm((1, HEADS), F32),
            vm((1, 256), F32),
            vm((1, CAP), jnp.int32),
            vm((24, 128), BF16),
            vm((32, 128), F32),
            vm((L, 256), BF16),
            vm((L, 256), BF16),
            vm((L, 128), BF16),
            vm((L, 128), BF16),
            vm((256, 1024), BF16),
            vm((L, 128), BF16),
            vm((64, 512), BF16),
            vm((64, 256), BF16),
            vm((512, 1024), BF16),
            vm((L + 16, 256), F32),
            vm((9, 8, 384), F32),
            vm((8, 8, 128), F32),
            vm((2, 2, 8, 4, 16, 384), BF16),
            vm((8, 16, 256), BF16),
            vm((8, 16, 256), BF16),
            vm((8, 16, 256), BF16),
            vm((8, 16, 256), BF16),
            vm((8, 16, 256), BF16),
            vm((8, CAP, 128), BF16),
            vm((8, CAP, 128), BF16),
            vm((8, CAP, 128), BF16),
            vm((8, L, 128), BF16),
            vm((8, L, 128), BF16),
            vm((16, 2, CAP, 128), BF16),
            vm((4, 128, 128), BF16),
            vm((512, 128), jnp.int32),
            vm((4, 128, 128), BF16),
            vm((4, 8, 128), F32),
            vm((4, 128, 128), BF16),
            vm((4, 8, 128), F32),
            vm((8, CAP, 128), BF16),
            vm((8, CAP, 128), BF16),
            dma((17,)),
            dma((2,)),
            dma((2, 2)),
            dma((N_SEM,)),
            dma((N_SEM,)),
        ],
        compiler_params=pltpu.CompilerParams(
            collective_id=0, has_side_effects=True, vmem_limit_bytes=56 * 1024 * 1024
        ),
        cost_estimate=pl.CostEstimate(flops=10**9, bytes_accessed=4 * 10**6, transcendentals=10**6),
    )(
        byte_stream,
        gate_stream,
        conv_weight,
        state_write,
        state_read,
        step_size.T,
        decay_coef.reshape(1, HEADS),
        skip_gain.reshape(1, HEADS),
        norm_gain.reshape(1, 256),
        mixer_out,
        residual,
        boundaries,
        pad_vector.reshape(24, 128),
        main_gain.reshape(32, 128),
        query_weight,
        key_value_weight,
        main_out_weight,
    )


def solution(mesh):
    in_specs = (
        P("seq", "head"),
        P("seq", "head"),
        P(None, "head"),
        P("seq", None),
        P("seq", None),
        P("seq", "head"),
        P("head"),
        P("head"),
        P("head"),
        P("head", None),
        P("seq", None),
        P("seq", None),
        P("seq"),
        P("seq"),
        P(),
        P(),
        P("seq", "head"),
        P("seq", "head"),
        P("head", None),
    )
    out_specs = P("seq", "head")
    return jax.shard_map(shards, mesh=mesh, in_specs=in_specs, out_specs=out_specs, check_vma=False)
```

```python
import functools
import math

import jax
import jax.numpy as jnp
from jax import lax
from jax.experimental import pallas as pl
from jax.experimental.pallas import tpu as pltpu
from jax.sharding import PartitionSpec as P

F32 = jnp.float32
BF16 = jnp.bfloat16
MESH = pl.DeviceIdType.MESH
EXACT = lax.Precision.HIGHEST

NY = 8
NZ = 8
NHD = 8
L = 128
HEADS = 4
HP = 64
CAP = 32
HD = 128
D_MAIN = 4096
THETA = 500000.0
EPSILON = 1e-05
FAR_FIRST = (4, 3, 5, 2, 6, 1, 7)
SLOTS = sorted(((i, j) for i in range(4) for j in range(4) if i + j > 0), key=lambda t: -t[0] - t[1])

(
    EDGE,
    STATS_Y,
    W_AZ,
    W_BY,
    SCAN1,
    SCAN2,
    SCAN3,
    SPAN_RS,
    SPAN_AG,
    ENC_RS,
    MAIN_RS,
    KV,
    QUERIES,
    OUT_SUMS,
    OUT_STATS,
    N_EX,
) = range(16)
RING_KV, RING_Q, N_SEM = (N_EX + 4 * i for i in range(3))


def nn(a, b, precision=None):
    return lax.dot_general(
        a, b, (((1,), (0,)), ((), ())), precision=precision, preferred_element_type=F32
    )


def nt(a, b, precision=None):
    return lax.dot_general(
        a, b, (((1,), (1,)), ((), ())), precision=precision, preferred_element_type=F32
    )


def tn(a, b, precision=None):
    return lax.dot_general(
        a, b, (((0,), (0,)), ((), ())), precision=precision, preferred_element_type=F32
    )


def iota(shape, dim):
    return lax.broadcasted_iota(jnp.int32, shape, dim)


def silu(v):
    return v / (1.0 + jnp.exp(-v))


def one_minus_exp(u):
    series = u * (
        1.0
        - u
        * (
            1.0 / 2
            - u * (1.0 / 6 - u * (1.0 / 24 - u * (1.0 / 120 - u * (1.0 / 720 - u / 5040))))
        )
    )
    return jnp.where(u < 0.3, series, 1.0 - jnp.exp(-u))


def kernel(
    x_hbm,
    gate_hbm,
    convw_hbm,
    b_hbm,
    c_hbm,
    step_hbm,
    decay_hbm,
    skip_hbm,
    ngain_hbm,
    mo_hbm,
    res_hbm,
    bnd_hbm,
    pad_hbm,
    mgain_hbm,
    wq_hbm,
    wkv_hbm,
    mw_hbm,
    out_ref,
    convw_ref,
    step_ref,
    decay_ref,
    skip_ref,
    ngain_ref,
    bnd_ref,
    pad_ref,
    mgain_ref,
    x_ref,
    gate_ref,
    b_ref,
    c_ref,
    mo_ref,
    res_ref,
    wq_ref,
    wkv_ref,
    mw_ref,
    ext,
    ebuf,
    stats_y,
    wbuf,
    s1_send,
    s1,
    s2,
    s3_send,
    s3,
    sp_send,
    sp_recv,
    ag,
    en_send,
    en_recv,
    kvbuf,
    qbuf,
    key_ranks,
    o_send,
    m_send,
    o_recv,
    m_recv,
    mn_send,
    mn_recv,
    local_sem,
    prev_sem,
    w0_sem,
    send_sem,
    recv_sem,
):
    s = lax.axis_index("seq")
    hd = lax.axis_index("head")
    y = s // NZ
    z = s % NZ

    def at_z(p):
        return (y * NZ + p, hd)

    def at_y(p):
        return (p * NZ + z, hd)

    def at_h(p):
        return (s, p)

    py, pz = lax.rem(y + hd, 2), lax.rem(z + hd, 2)
    sy, sz = 1 - 2 * py, 1 - 2 * pz

    def at_slot(i, j):
        yc = lax.rem(y + 8 + (0, -1, 2, -3)[i] * sy, NY)
        zc = lax.rem(z + 8 + (0, -1, 2, -3)[j] * sz, NZ)
        return (yc * NZ + zc, hd)

    def member(e):
        yc = lax.rem(y + 8 + sy, NY) if e // 2 else y
        zc = lax.rem(z + 8 + sz, NZ) if e % 2 else z
        return (yc * NZ + zc, hd), 2 * lax.rem(yc + hd, 2) + lax.rem(zc + hd, 2)

    barrier = pltpu.get_barrier_semaphore()
    greet = [(lax.rem(y + NY - 1, NY) * NZ + NZ - 1, hd)]
    for d in range(1, 8):
        greet += [at_z(lax.rem(z + d, NZ)), at_y(lax.rem(y + d, NY)), at_h(lax.rem(hd + d, NHD))]
    for to in greet:
        pl.semaphore_signal(barrier, inc=1, device_id=to, device_id_type=MESH)

    loads = [
        (step_hbm, step_ref),
        (decay_hbm, decay_ref),
        (x_hbm, x_ref),
        (convw_hbm, convw_ref),
        (b_hbm, b_ref),
        (wq_hbm, wq_ref),
        (wkv_hbm, wkv_ref),
        (pad_hbm, pad_ref),
        (mgain_hbm, mgain_ref),
        (bnd_hbm, bnd_ref),
        (c_hbm, c_ref),
        (gate_hbm, gate_ref),
        (skip_hbm, skip_ref),
        (ngain_hbm, ngain_ref),
        (res_hbm.at[:, pl.ds(pl.multiple_of(hd * 128, 128), 128)], res_ref),
        (mo_hbm, mo_ref),
        (mw_hbm, mw_ref),
    ]
    load = [pltpu.make_async_copy(a, b, local_sem.at[i]) for i, (a, b) in enumerate(loads)]
    for copy in load[:10]:
        copy.start()
    l_step, l_decay, l_x, l_convw, l_b, l_wq, l_wkv, l_pad, l_mgain, l_bnd = load[:10]
    l_c, l_gate, l_skip, l_ngain, l_res, l_mo, l_mw = load[10:]

    pending = []
    sizes = {}

    def finish(blocks, sem):
        pltpu.make_async_copy(blocks, blocks, sem).wait()

    def send_all(ex, me, where, src, dst, seven):
        for d in FAR_FIRST:
            p = lax.rem(me + d, 8)
            pltpu.make_async_remote_copy(
                src_ref=src(p),
                dst_ref=dst,
                send_sem=send_sem.at[ex],
                recv_sem=recv_sem.at[ex],
                device_id=where(p),
                device_id_type=MESH,
            ).start()
        pending.append((seven, send_sem.at[ex]))
        sizes[ex] = seven

    def recv_all(ex):
        finish(sizes[ex], recv_sem.at[ex])

    l_step.wait()
    l_decay.wait()
    dec = decay_ref[...]
    row4 = iota((HEADS, L), 0)
    coef = jnp.zeros((HEADS, L), F32)
    for h in range(HEADS):
        coef = jnp.where(row4 == h, dec[:, h : h + 1], coef)
    rate = step_ref[...] * coef
    log_decay = -rate
    gain_row = jnp.sqrt(one_minus_exp(2.0 * rate))
    ti = iota((L, L), 0)
    si = iota((L, L), 1)
    causal = ti >= si
    tri = jnp.where(causal, 1.0, 0.0).astype(F32)
    run_row = nt(log_decay, tri, EXACT)
    run_col = [
        nt(tri, jnp.broadcast_to(log_decay[h : h + 1, :], (L, L)), EXACT) for h in range(HEADS)
    ]
    rem_row = jnp.exp(run_row[:, L - 1 : L] - run_row) * gain_row
    first = si < HP
    eye = jnp.where(ti == si, 1.0, 0.0).astype(BF16)
    top = ti < HP
    rem_x = [
        nt(
            eye,
            jnp.where(
                top,
                jnp.broadcast_to(rem_row[2 * i : 2 * i + 1, :], (L, L)),
                jnp.broadcast_to(rem_row[2 * i + 1 : 2 * i + 2, :], (L, L)),
            ).astype(BF16),
        )
        for i in range(2)
    ]
    run_x = jnp.concatenate(
        [jnp.where(first, run_col[2 * i], run_col[2 * i + 1]) for i in range(2)], axis=1
    )

    l_x.wait()
    l_convw.wait()
    l_b.wait()
    ext[0:8, :] = jnp.zeros((8, 256), F32)
    ext[8 : 8 + L, :] = x_ref[...].astype(F32)
    ext[8 + L :, :] = jnp.zeros((8, 256), F32)
    cw = convw_ref[...]
    summed = cw[0:1, :] * ext[5 : 13 + L, :]
    for k in range(1, 4):
        summed = summed + cw[k : k + 1, :] * ext[5 + k : 13 + k + L, :]
    conv_own = silu(summed[:L]).astype(BF16).astype(F32)

    bm = b_ref[...]
    inner = iota((L, 256), 0) >= 3
    weighted = jnp.where(inner, conv_own * jnp.concatenate(rem_x, axis=1), 0.0).astype(BF16)
    state = tn(bm, weighted).astype(BF16)
    s1_send[...] = state.reshape(8, 16, 256)
    head_b = bm[0:16, :].astype(F32)
    ebuf[1 + z, 0:3, 0:256] = summed[0:3]
    ebuf[1 + z, 3:6, 0:256] = summed[L : L + 3]
    ebuf[1 + z, 6:7, 0:128] = head_b[0:1, :]
    ebuf[1 + z, 6:7, 128:256] = head_b[1:2, :]
    ebuf[1 + z, 7:8, 0:128] = head_b[2:3, :]
    ebuf[1 + z, 7:8, 128:256] = jnp.zeros((1, 128), F32)

    l_wq.wait()
    l_wkv.wait()
    l_pad.wait()
    l_mgain.wait()
    l_bnd.wait()
    prow = s // 2 - 8
    padf = pad_ref[...].astype(F32)
    mg = mgain_ref[...]
    pad_one = jnp.sum(jnp.where(iota((24, 128), 0) == prow, padf, 0.0), axis=0, keepdims=True)
    gain_one = jnp.sum(jnp.where(iota((32, 128), 0) == s // 2, mg, 0.0), axis=0, keepdims=True)
    both = pad_one * gain_one
    half = jnp.where(s % 2 == 1, both[:, 64:], both[:, :64])
    half = jnp.broadcast_to(half, (16, 64)).astype(BF16)
    pq = nn(half, wq_ref[...])
    pkv = nn(half, wkv_ref[...])
    pad_sq = jnp.sum(jnp.sum(padf * padf, axis=1, keepdims=True), axis=0, keepdims=True)
    lane1 = iota((1, 128), 1)
    bounds = bnd_ref[...]
    count = jnp.sum(jnp.where(bounds < NY * NZ * L, 1.0, 0.0), axis=1, keepdims=True)
    last = jnp.zeros((1, 128), F32)
    for h in range(HEADS):
        last = jnp.where(lane1 == h, run_col[h][L - 1 : L, :], last)
        for t in range(3):
            last = jnp.where(lane1 == 16 + 4 * t + h, rem_row[h : h + 1, t : t + 1], last)
    rows = [
        pq[0:1, 0:128],
        pq[0:1, 128:256],
        pkv[0:1, 0:128],
        pq[0:1, 256:384],
        pq[0:1, 384:512],
        pkv[0:1, 128:256],
        jnp.where(lane1 == z, count, 0.0),
        last,
    ]
    for i, row in enumerate(rows):
        ebuf[1 + z, i : i + 1, 256:384] = row

    pl.semaphore_wait(barrier, jnp.where(z == NZ - 1, 21 + NZ, 21))

    send_all(EDGE, z, at_z, lambda p: ebuf.at[1 + z], ebuf.at[1 + z], ebuf.at[pl.ds(1, 7)])

    def prev_copy(p):
        return pltpu.make_async_remote_copy(
            src_ref=ebuf.at[1 + z],
            dst_ref=ebuf.at[0],
            send_sem=prev_sem.at[0],
            recv_sem=prev_sem.at[1],
            device_id=(lax.rem(y + 1, NY) * NZ + p, hd),
            device_id_type=MESH,
        )

    @pl.when(z == NZ - 1)
    def _():
        for p in range(NZ):
            prev_copy(p).start()

    send_all(SCAN1, z, at_z, lambda p: s1_send.at[p], s1.at[z], s1.at[pl.ds(0, 7)])
    s1[z] = s1_send[z]

    def w0_parts(yp):
        rg = lax.rem(yp, 4)
        ch = yp // 4
        r = pl.ds(pl.multiple_of(16 * rg, 16), 16)
        return (
            (
                wq_hbm.at[r, pl.ds(pl.multiple_of(256 * ch, 256), 256)],
                wbuf.at[ch, y, z, rg, :, pl.ds(0, 256)],
            ),
            (
                wkv_hbm.at[r, pl.ds(pl.multiple_of(128 * ch, 128), 128)],
                wbuf.at[ch, y, z, rg, :, pl.ds(256, 128)],
            ),
        )

    def w0_copies():
        copies = []
        for d in FAR_FIRST:
            yp = lax.rem(y + d, NY)
            for i, (src, dst) in enumerate(w0_parts(yp)):
                copies.append(
                    pltpu.make_async_remote_copy(
                        src_ref=src,
                        dst_ref=dst,
                        send_sem=w0_sem.at[0, i],
                        recv_sem=w0_sem.at[1, i],
                        device_id=at_y(yp),
                        device_id_type=MESH,
                    )
                )
        return copies

    @pl.when(y < 2)
    def _():
        for copy in w0_copies():
            copy.start()
        for i, (src, dst) in enumerate(w0_parts(y)):
            pltpu.make_async_copy(src, dst, w0_sem.at[1, i]).start()

    for copy in load[10:]:
        copy.start()

    l_c.wait()
    cm = c_ref[...]
    affinity = jnp.where(causal, nt(cm, bm), 0.0)
    mix = []
    for h in range(HEADS):
        spread = jnp.where(causal, run_col[h] - run_row[h : h + 1, :], 0.0)
        mix.append((jnp.exp(spread) * (affinity * gain_row[h : h + 1, :])).astype(BF16))

    col = iota((128, 1024), 1)
    part_of = col // 256
    lane_of = lax.rem(col, 256) // HP + jnp.where(part_of > 0, 12 + 4 * part_of, 0)
    spread_head = jnp.where(iota((128, 1024), 0) == lane_of, 1.0, 0.0).astype(F32)
    pick_n = jnp.where(si == 16 * z + lax.rem(ti, 16), 1.0, 0.0).astype(BF16)
    same = iota((L, 24), 0) // 16 == lax.rem(iota((L, 24), 1), 8)
    nothing = (iota((8, 256), 0) + y) == 0

    recv_all(EDGE)
    prev_copy(0).wait_recv()
    edges = ebuf[...]
    tiles = edges[1:, :, 256:384]
    stats_y[y] = jnp.sum(tiles, axis=0)
    send_all(STATS_Y, y, at_y, lambda p: stats_y.at[y], stats_y.at[y], stats_y.at[pl.ds(0, 7)])

    by_head = nn(tiles[:, 7, :], spread_head, EXACT)
    lz = by_head[:, 0:256]

    edge_x, edge_b = [], []
    for t in range(3):
        earlier = jnp.where(nothing, 0.0, edges[0:8, 3 + t, 0:256])
        conv_t = silu(edges[1:, t, 0:256] + earlier).astype(BF16).astype(F32)
        edge_x.append(conv_t * by_head[:, 256 * (1 + t) : 256 * (2 + t)])
        edge_b.append(edges[1:, 6 + t // 2, 128 * (t % 2) : 128 * (t % 2 + 1)])
    edge_x = jnp.concatenate(edge_x, axis=0).astype(BF16)
    edge_b = jnp.concatenate(edge_b, axis=0).astype(BF16)
    spots = nt(pick_n, edge_b)
    added = nn(jnp.where(same, spots, 0.0).astype(BF16), edge_x).reshape(8, 16, 256)
    recv_all(SCAN1)
    acc = jnp.zeros((16, 256), F32)
    cum = jnp.zeros((1, 256), F32)
    before, cums = [], []
    for j in range(NZ):
        before.append(acc)
        cums.append(cum)
        acc = jnp.exp(lz[j : j + 1, :]) * acc + (s1[j].astype(F32) + added[j])
        cum = cum + lz[j : j + 1, :]
    s2[y] = acc.astype(BF16)
    send_all(SCAN2, y, at_y, lambda p: s2.at[y], s2.at[y], s2.at[pl.ds(0, 7)])

    for i, cols in enumerate((pl.ds(0, 256), pl.ds(256, 128))):
        finish(wbuf.at[0, :, z, 0, :, cols], w0_sem.at[1, i])
    rg_me = lax.rem(y, 4)
    ch_me = y // 4
    pieces7 = wbuf.at[ch_me, 0, pl.ds(0, 7), rg_me]
    own_a = wbuf.at[ch_me, 0, z, rg_me]
    own_b = wbuf.at[ch_me, 1, z, rg_me]
    send_all(W_BY, y, at_y, lambda p: own_b, own_b, pieces7)
    send_all(W_AZ, z, at_z, lambda p: own_a, own_a, pieces7)

    before_rows = pltpu.roll(ebuf[z, :, 0:256], 5, 0)
    lead = (iota((8, 256), 0) < 3) & (s > 0)
    top_rows = silu(summed[0:8] + jnp.where(lead, before_rows, 0.0)).astype(BF16).astype(F32)
    conv_f = jnp.concatenate([top_rows, conv_own[8:]], axis=0)
    conv = conv_f.astype(BF16)

    within = []
    zero = jnp.zeros((), BF16)
    for i in range(2):
        pair = conv[:, 128 * i : 128 * (i + 1)]
        stacked = jnp.concatenate(
            [jnp.where(first, pair, zero), jnp.where(first, zero, pair)], axis=0
        )
        within.append(nn(jnp.concatenate([mix[2 * i], mix[2 * i + 1]], axis=1), stacked))
    l_skip.wait()
    skip_v = skip_ref[...]
    skip = jnp.zeros((1, 256), F32)
    head_of = iota((1, 256), 1) // HP
    for h in range(HEADS):
        skip = jnp.where(head_of == h, skip_v[:, h : h + 1], skip)
    mixed_near = jnp.concatenate(within, axis=1) + skip * conv_f
    exp_run = jnp.exp(run_x)
    l_gate.wait()
    gate = silu(gate_ref[...].astype(F32))

    def block_a(p, cols, lo=0, n=8):
        return wbuf.at[p // 4, 0, pl.ds(lo, n), lax.rem(p, 4), :, cols]

    def block_b(p, cols, lo=0, n=2):
        return wbuf.at[pl.ds(lo, n), 1, p, :, :, cols]

    def rings(step, wait, kv):
        cols = pl.ds(256, 128) if kv else pl.ds(0, 256)
        ex = (RING_KV if kv else RING_Q) + step
        if step == 3:
            moved = wbuf.at[:, 0, pl.ds(0, 2), :, :, cols]
        elif step == 0:
            moved = wbuf.at[:, :, pl.ds(0, 4), :, :, cols]
        else:
            moved = wbuf.at[:, :, pl.ds(0, 2), :, :, cols]
        if wait:
            finish(moved, recv_sem.at[ex])
            return
        pending.append((moved, send_sem.at[ex]))
        for me, where, block, whole in ((y, at_y, block_a, 8), (z, at_z, block_b, 2)):
            for way, hops in ((0, 2), (1, 2), (0, 1), (1, 1)) if step == 0 else ((0, 1), (1, 1)):
                ahead = lax.rem(me + (hops if way == 0 else 8 - hops), 8)
                of = lax.rem(me + (8 - step if way == 0 else step), 8)
                if step == 3:
                    part = block(of, cols, way * whole // 2, whole // 2)
                else:
                    part = block(of, cols)
                pltpu.make_async_remote_copy(
                    src_ref=part,
                    dst_ref=part,
                    send_sem=send_sem.at[ex],
                    recv_sem=recv_sem.at[ex],
                    device_id=where(ahead),
                    device_id_type=MESH,
                ).start()

    recv_all(STATS_Y)
    ytiles = stats_y[...]
    pad_total = jnp.sum(ytiles, axis=0)
    ly = nn(ytiles[:, 7, :], spread_head[:, 0:256], EXACT)

    recv_all(SCAN2)
    rows_before = jnp.zeros((16, 256), F32)
    for j in range(NY - 1):
        longer = jnp.exp(ly[j : j + 1, :]) * rows_before + s2[j].astype(F32)
        rows_before = jnp.where(j < y, longer, rows_before)
    for j in range(NZ):
        s3_send[j] = (before[j] + jnp.exp(cums[j]) * rows_before).astype(BF16)
    send_all(SCAN3, z, at_z, lambda p: s3_send.at[p], s3.at[z], s3.at[pl.ds(0, 7)])
    s3[z] = s3_send[z]

    recv_all(W_AZ)
    recv_all(W_BY)
    rings(0, False, True)
    rings(0, False, False)

    l_ngain.wait()
    bnd = bounds - s * L
    byte_at = iota((L, CAP), 0)
    slot_at = iota((L, CAP), 1)
    usable = bounds < NY * NZ * L
    picker = jnp.where((byte_at == bnd) & usable, 1.0, 0.0).astype(BF16)
    upto = jnp.where((bnd <= byte_at) & usable, 1.0, 0.0)
    newest = jnp.sum(upto, axis=1, keepdims=True) - 1.0
    spreader = jnp.where(slot_at.astype(F32) == newest, 1.0, 0.0).astype(BF16)
    l_res.wait()
    res = res_ref[...]
    res_span = tn(picker, res)

    span_pick = tn(picker, eye)
    span_c = nn(span_pick.astype(BF16), cm).astype(BF16)
    span_near = nn(span_pick, mixed_near, EXACT)
    span_run = nn(span_pick, exp_run, EXACT)
    span_gate = nn(span_pick, gate, EXACT)

    def normalize(near, read, run, opening, states):
        gated = (near + nn(read, states) * run) * opening
        mean_sq = jnp.sum(gated * gated, axis=1, keepdims=True) * (1.0 / 256)
        return (gated * lax.rsqrt(mean_sq + EPSILON) * ngain_ref[...]).astype(BF16)

    lane = iota((CAP, 128), 1)
    counts = ytiles[:, 6, :]
    lane8 = iota((8, 128), 1)
    ahead = (lane8 < NZ) & (iota((8, 128), 0) * NZ + lane8 < s)
    offset = jnp.sum(jnp.where(ahead, counts, 0.0), axis=0, keepdims=True)
    offset = jnp.sum(offset, axis=1, keepdims=True)
    place = iota((CAP, 128), 0).astype(F32) + offset
    freq = jnp.exp(
        lax.rem(lane, HD // 2).astype(F32) * (-2.0 * math.log(THETA) / HD)
    )
    angle = place * freq
    cosine = jnp.cos(angle)
    sine = jnp.where(lane < HD // 2, -jnp.sin(angle), jnp.sin(angle))

    recv_all(SCAN3)
    states = s3[...].reshape(128, 256)
    l_mo.wait()
    span_normed = normalize(span_near, span_c, span_run, span_gate, states)
    span_part = nn(span_normed, mo_ref[...]).astype(BF16)
    for j in range(NHD):
        sp_send[j] = span_part[:, 128 * j : 128 * (j + 1)]
    send_all(SPAN_RS, hd, at_h, lambda p: sp_send.at[p], sp_recv.at[hd], sp_recv.at[pl.ds(0, 7)])
    sp_recv[hd] = sp_send[hd]

    rings(0, True, True)
    rings(2, False, True)
    rings(0, True, False)
    rings(2, False, False)

    normed = normalize(mixed_near, cm, exp_run, gate, states)
    enc_part = nn(normed, mo_ref[...]).astype(BF16)
    for j in range(NHD):
        en_send[j] = enc_part[:, 128 * j : 128 * (j + 1)]
    en_recv[hd] = en_send[hd]

    recv_all(SPAN_RS)
    span_share = (res_span + jnp.sum(sp_recv[...].astype(F32), axis=0)).astype(BF16)
    ag[hd] = span_share
    send_all(SPAN_AG, hd, at_h, lambda p: ag.at[hd], ag.at[hd], ag.at[pl.ds(0, 7)])

    rings(2, True, True)
    rings(3, False, True)
    rings(2, True, False)
    rings(3, False, False)

    key = iota((512, 128), 0)
    key_y = lax.rem(y + 16 - (key // 128) * sy, NY)
    key_z = lax.rem(z + 16 - lax.rem(key // CAP, 4) * sz, NZ)
    expand = jnp.where(iota((512, 128), 1) == key_z, 1.0, 0.0).astype(BF16)
    per_row = nt(expand, jnp.concatenate([ytiles[:, 6, :], ytiles[:, 6, :]], axis=0).astype(BF16))
    lane16 = iota((512, 16), 1)
    key_count = jnp.sum(
        jnp.where(lane16 == lax.rem(y + 16 - (iota((512, 16), 0) // 128) * sy, NY), per_row, 0.0),
        axis=1,
        keepdims=True,
    )
    key_slot = lax.rem(key, CAP)
    key_rank = (key_y * NZ + key_z) * CAP + key_slot
    key_rank = jnp.where(key_slot.astype(F32) < key_count, key_rank, NY * NZ * CAP)
    key_ranks[...] = key_rank
    query = iota((1, 512), 1)
    query_rank = (
        (
            lax.rem(y + 8 - py + query // 256, NY) * NZ
            + lax.rem(z + 8 - pz + lax.rem(query // 128, 2), NZ)
        )
        * CAP
        + lax.rem(query, CAP)
    )

    recv_all(SPAN_AG)
    sq = jnp.zeros((CAP, 128), F32)
    pieces = []
    for j in range(NHD):
        piece = ag[j].astype(F32)
        sq = sq + piece * piece
        pieces.append((piece * mg[j : j + 1, :]).astype(BF16))
    sq = jnp.sum(sq, axis=1, keepdims=True)
    scale = lax.rsqrt((sq + pad_sq) * (1.0 / D_MAIN) + EPSILON)
    span_x = jnp.concatenate(pieces, axis=1)
    rings(3, True, True)
    def project(ch, lo, n):
        return nn(span_x, wbuf[ch, :, :, :, :, lo : lo + n].reshape(1024, n))

    def column(part, i):
        return (part + pad_total[i : i + 1, :]) * scale

    def rotate(v):
        return (v * cosine + pltpu.roll(v, HD // 2, 1) * sine).astype(BF16)

    kvbuf[0, 0] = rotate(column(project(0, 256, 128), 2))
    kvbuf[0, 1] = column(project(1, 256, 128), 5).astype(BF16)

    def kv_copy(i, j):
        return pltpu.make_async_remote_copy(
            src_ref=kvbuf.at[0],
            dst_ref=kvbuf.at[4 * i + j],
            send_sem=send_sem.at[KV],
            recv_sem=recv_sem.at[KV],
            device_id=at_slot(i, j),
            device_id_type=MESH,
        )

    for i, j in SLOTS:
        kv_copy(i, j).start()
    pending.append((kvbuf.at[pl.ds(0, 15)], send_sem.at[KV]))
    mine = 2 * py + pz

    rings(3, True, False)
    for ch in range(2):
        pair = project(ch, 0, 256)
        for h in range(2):
            at = CAP * (2 * ch + h)
            part = pair[:, 128 * h : 128 * (h + 1)]
            qbuf[mine, at : at + CAP, :] = rotate(column(part, 3 * ch + h))

    def group_copy(i, e, src, dst):
        return pltpu.make_async_remote_copy(
            src_ref=src,
            dst_ref=dst,
            send_sem=send_sem.at[i],
            recv_sem=recv_sem.at[i],
            device_id=member(e)[0],
            device_id_type=MESH,
        )

    for e in range(1, 4):
        group_copy(QUERIES, e, qbuf.at[mine], qbuf.at[mine]).start()
    pending.append((qbuf.at[pl.ds(0, 3)], send_sem.at[QUERIES]))

    send_all(ENC_RS, hd, at_h, lambda p: en_send.at[p], en_recv.at[hd], en_recv.at[pl.ds(0, 7)])

    finish(qbuf.at[pl.ds(0, 3)], recv_sem.at[QUERIES])
    finish(kvbuf.at[pl.ds(0, 15)], recv_sem.at[KV])

    kv = kvbuf[...]
    keys = kv[:, 0].reshape(512, HD)
    values = kv[:, 1].reshape(512, HD)
    ranks = key_ranks[...]
    unit = 1.0 / math.sqrt(HD)
    for m in range(4):
        scores = nt(keys, qbuf[m])
        allowed = ranks <= query_rank[:, 128 * m : 128 * (m + 1)]
        scores = jnp.where(allowed, scores * unit, -1e30)
        top = jnp.max(scores, axis=0, keepdims=True)
        weights = jnp.exp(scores - top)
        o_send[m] = tn(values, weights.astype(BF16)).astype(BF16)
        m_send[m, 0:1, :] = top
        m_send[m, 1:2, :] = jnp.sum(weights, axis=0, keepdims=True)

    for e in range(1, 4):
        place_e = member(e)[1]
        group_copy(OUT_SUMS, e, o_send.at[place_e], o_recv.at[e]).start()
        group_copy(OUT_STATS, e, m_send.at[place_e], m_recv.at[e]).start()
    sums3, stats3 = o_recv.at[pl.ds(1, 3)], m_recv.at[pl.ds(1, 3)]
    pending.append((sums3, send_sem.at[OUT_SUMS]))
    pending.append((stats3, send_sem.at[OUT_STATS]))
    o_recv[0] = o_send[mine]
    m_recv[0] = m_send[mine]

    finish(sums3, recv_sem.at[OUT_SUMS])
    finish(stats3, recv_sem.at[OUT_STATS])

    tops = m_recv[:, 0, :]
    highest = jnp.max(tops, axis=0, keepdims=True)
    shrink = jnp.exp(tops - highest)
    total = jnp.sum(shrink * m_recv[:, 1, :], axis=0, keepdims=True)
    summed_o = jnp.zeros((HD, 128), F32)
    for e in range(4):
        summed_o = summed_o + shrink[e : e + 1, :] * o_recv[e].astype(F32)
    attended = (summed_o / total).T.astype(BF16)

    l_mw.wait()
    att = jnp.concatenate([attended[CAP * i : CAP * (i + 1), :] for i in range(4)], axis=1)
    main_part = nn(att, mw_ref[...]).astype(BF16)
    for j in range(NHD):
        mn_send[j] = main_part[:, 128 * j : 128 * (j + 1)]
    send_all(MAIN_RS, hd, at_h, lambda p: mn_send.at[p], mn_recv.at[hd], mn_recv.at[pl.ds(0, 7)])
    mn_recv[hd] = mn_send[hd]
    recv_all(ENC_RS)
    encoded = (res.astype(F32) + jnp.sum(en_recv[...].astype(F32), axis=0)).astype(BF16)

    recv_all(MAIN_RS)
    main_rows = (span_share.astype(F32) + jnp.sum(mn_recv[...].astype(F32), axis=0)).astype(BF16)
    out_ref[...] = (encoded.astype(F32) + nn(spreader, main_rows)).astype(BF16)

    for blocks, sem in pending:
        finish(blocks, sem)

    @pl.when(y < 2)
    def _():
        for i, cols in enumerate((pl.ds(0, 256), pl.ds(256, 128))):
            finish(wbuf.at[0, 0, pl.ds(0, 7), 0, :, cols], w0_sem.at[0, i])

    @pl.when(z == NZ - 1)
    def _():
        finish(ebuf.at[pl.ds(0, NZ)], prev_sem.at[0])


def shards(
    byte_stream,
    gate_stream,
    conv_weight,
    state_write,
    state_read,
    step_size,
    decay_coef,
    skip_gain,
    norm_gain,
    mixer_out,
    residual,
    boundaries,
    span_counts,
    span_offsets,
    pad_vector,
    main_gain,
    query_weight,
    key_value_weight,
    main_out_weight,
):
    far = pl.BlockSpec(memory_space=pl.ANY)
    near = pl.BlockSpec(memory_space=pltpu.VMEM)
    vm = pltpu.VMEM
    dma = pltpu.SemaphoreType.DMA
    return pl.pallas_call(
        kernel,
        out_shape=pltpu.VMEM((L, 128), BF16),
        in_specs=[far] * 17,
        out_specs=near,
        scratch_shapes=[
            vm((4, 256), F32),
            vm((HEADS, L), F32),
            vm((1, HEADS), F32),
            vm((1, HEADS), F32),
            vm((1, 256), F32),
            vm((1, CAP), jnp.int32),
            vm((24, 128), BF16),
            vm((32, 128), F32),
            vm((L, 256), BF16),
            vm((L, 256), BF16),
            vm((L, 128), BF16),
            vm((L, 128), BF16),
            vm((256, 1024), BF16),
            vm((L, 128), BF16),
            vm((64, 512), BF16),
            vm((64, 256), BF16),
            vm((512, 1024), BF16),
            vm((L + 16, 256), F32),
            vm((9, 8, 384), F32),
            vm((8, 8, 128), F32),
            vm((2, 2, 8, 4, 16, 384), BF16),
            vm((8, 16, 256), BF16),
            vm((8, 16, 256), BF16),
            vm((8, 16, 256), BF16),
            vm((8, 16, 256), BF16),
            vm((8, 16, 256), BF16),
            vm((8, CAP, 128), BF16),
            vm((8, CAP, 128), BF16),
            vm((8, CAP, 128), BF16),
            vm((8, L, 128), BF16),
            vm((8, L, 128), BF16),
            vm((16, 2, CAP, 128), BF16),
            vm((4, 128, 128), BF16),
            vm((512, 128), jnp.int32),
            vm((4, 128, 128), BF16),
            vm((4, 8, 128), F32),
            vm((4, 128, 128), BF16),
            vm((4, 8, 128), F32),
            vm((8, CAP, 128), BF16),
            vm((8, CAP, 128), BF16),
            dma((17,)),
            dma((2,)),
            dma((2, 2)),
            dma((N_SEM,)),
            dma((N_SEM,)),
        ],
        compiler_params=pltpu.CompilerParams(
            collective_id=0, has_side_effects=True, vmem_limit_bytes=56 * 1024 * 1024
        ),
        cost_estimate=pl.CostEstimate(flops=10**9, bytes_accessed=4 * 10**6, transcendentals=10**6),
    )(
        byte_stream,
        gate_stream,
        conv_weight,
        state_write,
        state_read,
        step_size.T,
        decay_coef.reshape(1, HEADS),
        skip_gain.reshape(1, HEADS),
        norm_gain.reshape(1, 256),
        mixer_out,
        residual,
        boundaries,
        pad_vector.reshape(24, 128),
        main_gain.reshape(32, 128),
        query_weight,
        key_value_weight,
        main_out_weight,
    )


def solution(mesh):
    in_specs = (
        P("seq", "head"),
        P("seq", "head"),
        P(None, "head"),
        P("seq", None),
        P("seq", None),
        P("seq", "head"),
        P("head"),
        P("head"),
        P("head"),
        P("head", None),
        P("seq", None),
        P("seq", None),
        P("seq"),
        P("seq"),
        P(),
        P(),
        P("seq", "head"),
        P("seq", "head"),
        P("head", None),
    )
    out_specs = P("seq", "head")
    return jax.shard_map(shards, mesh=mesh, in_specs=in_specs, out_specs=out_specs, check_vma=False)
```

```python
import functools
import math

import jax
import jax.numpy as jnp
from jax import lax
from jax.experimental import pallas as pl
from jax.experimental.pallas import tpu as pltpu
from jax.sharding import PartitionSpec as P

F32 = jnp.float32
BF16 = jnp.bfloat16
MESH = pl.DeviceIdType.MESH
EXACT = lax.Precision.HIGHEST

NY = 8
NZ = 8
NHD = 8
L = 128
HEADS = 4
HP = 64
CAP = 32
HD = 128
D_MAIN = 4096
THETA = 500000.0
EPSILON = 1e-05
FAR_FIRST = (4, 3, 5, 2, 6, 1, 7)
SLOTS = sorted(((i, j) for i in range(4) for j in range(4) if i + j > 0), key=lambda t: -t[0] - t[1])

(
    EDGE,
    STATS_Y,
    W_AZ,
    W_BY,
    SCAN1,
    SCAN2,
    SCAN3,
    SPAN_RS,
    SPAN_AG,
    ENC_RS,
    MAIN_RS,
    KEYS,
    VALUES,
    QUERIES,
    OUT_SUMS,
    OUT_STATS,
    N_EX,
) = range(17)
RING_KV, RING_Q, N_SEM = (N_EX + 4 * i for i in range(3))


def nn(a, b, precision=None):
    return lax.dot_general(
        a, b, (((1,), (0,)), ((), ())), precision=precision, preferred_element_type=F32
    )


def nt(a, b, precision=None):
    return lax.dot_general(
        a, b, (((1,), (1,)), ((), ())), precision=precision, preferred_element_type=F32
    )


def tn(a, b, precision=None):
    return lax.dot_general(
        a, b, (((0,), (0,)), ((), ())), precision=precision, preferred_element_type=F32
    )


def iota(shape, dim):
    return lax.broadcasted_iota(jnp.int32, shape, dim)


def silu(v):
    return v / (1.0 + jnp.exp(-v))


def one_minus_exp(u):
    series = u * (
        1.0
        - u
        * (
            1.0 / 2
            - u * (1.0 / 6 - u * (1.0 / 24 - u * (1.0 / 120 - u * (1.0 / 720 - u / 5040))))
        )
    )
    return jnp.where(u < 0.3, series, 1.0 - jnp.exp(-u))


def kernel(
    x_hbm,
    gate_hbm,
    convw_hbm,
    b_hbm,
    c_hbm,
    step_hbm,
    decay_hbm,
    skip_hbm,
    ngain_hbm,
    mo_hbm,
    res_hbm,
    bnd_hbm,
    pad_hbm,
    mgain_hbm,
    wq_hbm,
    wkv_hbm,
    mw_hbm,
    out_ref,
    convw_ref,
    step_ref,
    decay_ref,
    skip_ref,
    ngain_ref,
    bnd_ref,
    pad_ref,
    mgain_ref,
    x_ref,
    gate_ref,
    b_ref,
    c_ref,
    mo_ref,
    res_ref,
    wq_ref,
    wkv_ref,
    mw_ref,
    ext,
    ebuf,
    stats_y,
    wbuf,
    s1_send,
    s1,
    s2,
    s3_send,
    s3,
    sp_send,
    sp_recv,
    ag,
    en_send,
    en_recv,
    kbuf,
    vbuf,
    qbuf,
    key_ranks,
    o_send,
    m_send,
    o_recv,
    m_recv,
    mn_send,
    mn_recv,
    local_sem,
    prev_sem,
    w0_sem,
    send_sem,
    recv_sem,
):
    s = lax.axis_index("seq")
    hd = lax.axis_index("head")
    y = s // NZ
    z = s % NZ

    def at_z(p):
        return (y * NZ + p, hd)

    def at_y(p):
        return (p * NZ + z, hd)

    def at_h(p):
        return (s, p)

    py, pz = lax.rem(y + hd, 2), lax.rem(z + hd, 2)
    sy, sz = 1 - 2 * py, 1 - 2 * pz

    def at_slot(i, j):
        yc = lax.rem(y + 8 + (0, -1, 2, -3)[i] * sy, NY)
        zc = lax.rem(z + 8 + (0, -1, 2, -3)[j] * sz, NZ)
        return (yc * NZ + zc, hd)

    def member(e):
        yc = lax.rem(y + 8 + sy, NY) if e // 2 else y
        zc = lax.rem(z + 8 + sz, NZ) if e % 2 else z
        return (yc * NZ + zc, hd), 2 * lax.rem(yc + hd, 2) + lax.rem(zc + hd, 2)

    barrier = pltpu.get_barrier_semaphore()
    greet = [(lax.rem(y + NY - 1, NY) * NZ + NZ - 1, hd)]
    for d in range(1, 8):
        greet += [at_z(lax.rem(z + d, NZ)), at_y(lax.rem(y + d, NY)), at_h(lax.rem(hd + d, NHD))]
    for to in greet:
        pl.semaphore_signal(barrier, inc=1, device_id=to, device_id_type=MESH)

    loads = [
        (step_hbm, step_ref),
        (decay_hbm, decay_ref),
        (x_hbm, x_ref),
        (convw_hbm, convw_ref),
        (b_hbm, b_ref),
        (wq_hbm, wq_ref),
        (wkv_hbm, wkv_ref),
        (pad_hbm, pad_ref),
        (mgain_hbm, mgain_ref),
        (bnd_hbm, bnd_ref),
        (c_hbm, c_ref),
        (gate_hbm, gate_ref),
        (skip_hbm, skip_ref),
        (ngain_hbm, ngain_ref),
        (res_hbm.at[:, pl.ds(pl.multiple_of(hd * 128, 128), 128)], res_ref),
        (mo_hbm, mo_ref),
        (mw_hbm, mw_ref),
    ]
    load = [pltpu.make_async_copy(a, b, local_sem.at[i]) for i, (a, b) in enumerate(loads)]
    for copy in load[:10]:
        copy.start()
    l_step, l_decay, l_x, l_convw, l_b, l_wq, l_wkv, l_pad, l_mgain, l_bnd = load[:10]
    l_c, l_gate, l_skip, l_ngain, l_res, l_mo, l_mw = load[10:]

    pending = []
    sizes = {}

    def finish(blocks, sem):
        pltpu.make_async_copy(blocks, blocks, sem).wait()

    def send_all(ex, me, where, src, dst, seven):
        for d in FAR_FIRST:
            p = lax.rem(me + d, 8)
            pltpu.make_async_remote_copy(
                src_ref=src(p),
                dst_ref=dst,
                send_sem=send_sem.at[ex],
                recv_sem=recv_sem.at[ex],
                device_id=where(p),
                device_id_type=MESH,
            ).start()
        pending.append((seven, send_sem.at[ex]))
        sizes[ex] = seven

    def recv_all(ex):
        finish(sizes[ex], recv_sem.at[ex])

    l_step.wait()
    l_decay.wait()
    dec = decay_ref[...]
    row4 = iota((HEADS, L), 0)
    coef = jnp.zeros((HEADS, L), F32)
    for h in range(HEADS):
        coef = jnp.where(row4 == h, dec[:, h : h + 1], coef)
    rate = step_ref[...] * coef
    log_decay = -rate
    gain_row = jnp.sqrt(one_minus_exp(2.0 * rate))
    ti = iota((L, L), 0)
    si = iota((L, L), 1)
    causal = ti >= si
    tri = jnp.where(causal, 1.0, 0.0).astype(F32)
    run_row = nt(log_decay, tri, EXACT)
    run_col = [
        nt(tri, jnp.broadcast_to(log_decay[h : h + 1, :], (L, L)), EXACT) for h in range(HEADS)
    ]
    rem_row = jnp.exp(run_row[:, L - 1 : L] - run_row) * gain_row
    first = si < HP
    eye = jnp.where(ti == si, 1.0, 0.0).astype(BF16)
    top = ti < HP
    rem_x = [
        nt(
            eye,
            jnp.where(
                top,
                jnp.broadcast_to(rem_row[2 * i : 2 * i + 1, :], (L, L)),
                jnp.broadcast_to(rem_row[2 * i + 1 : 2 * i + 2, :], (L, L)),
            ).astype(BF16),
        )
        for i in range(2)
    ]
    run_x = jnp.concatenate(
        [jnp.where(first, run_col[2 * i], run_col[2 * i + 1]) for i in range(2)], axis=1
    )

    l_x.wait()
    l_convw.wait()
    l_b.wait()
    ext[0:8, :] = jnp.zeros((8, 256), F32)
    ext[8 : 8 + L, :] = x_ref[...].astype(F32)
    ext[8 + L :, :] = jnp.zeros((8, 256), F32)
    cw = convw_ref[...]
    summed = cw[0:1, :] * ext[5 : 13 + L, :]
    for k in range(1, 4):
        summed = summed + cw[k : k + 1, :] * ext[5 + k : 13 + k + L, :]
    conv_own = silu(summed[:L]).astype(BF16).astype(F32)

    bm = b_ref[...]
    inner = iota((L, 256), 0) >= 3
    weighted = jnp.where(inner, conv_own * jnp.concatenate(rem_x, axis=1), 0.0).astype(BF16)
    state = tn(bm, weighted).astype(BF16)
    s1_send[...] = state.reshape(8, 16, 256)
    head_b = bm[0:16, :].astype(F32)
    ebuf[1 + z, 0:3, 0:256] = summed[0:3]
    ebuf[1 + z, 3:6, 0:256] = summed[L : L + 3]
    ebuf[1 + z, 6:7, 0:128] = head_b[0:1, :]
    ebuf[1 + z, 6:7, 128:256] = head_b[1:2, :]
    ebuf[1 + z, 7:8, 0:128] = head_b[2:3, :]
    ebuf[1 + z, 7:8, 128:256] = jnp.zeros((1, 128), F32)

    l_wq.wait()
    l_wkv.wait()
    l_pad.wait()
    l_mgain.wait()
    l_bnd.wait()
    prow = s // 2 - 8
    padf = pad_ref[...].astype(F32)
    mg = mgain_ref[...]
    pad_one = jnp.sum(jnp.where(iota((24, 128), 0) == prow, padf, 0.0), axis=0, keepdims=True)
    gain_one = jnp.sum(jnp.where(iota((32, 128), 0) == s // 2, mg, 0.0), axis=0, keepdims=True)
    both = pad_one * gain_one
    half = jnp.where(s % 2 == 1, both[:, 64:], both[:, :64])
    half = jnp.broadcast_to(half, (16, 64)).astype(BF16)
    pq = nn(half, wq_ref[...])
    pkv = nn(half, wkv_ref[...])
    pad_sq = jnp.sum(jnp.sum(padf * padf, axis=1, keepdims=True), axis=0, keepdims=True)
    lane1 = iota((1, 128), 1)
    bounds = bnd_ref[...]
    count = jnp.sum(jnp.where(bounds < NY * NZ * L, 1.0, 0.0), axis=1, keepdims=True)
    last = jnp.zeros((1, 128), F32)
    for h in range(HEADS):
        last = jnp.where(lane1 == h, run_col[h][L - 1 : L, :], last)
        for t in range(3):
            last = jnp.where(lane1 == 16 + 4 * t + h, rem_row[h : h + 1, t : t + 1], last)
    rows = [
        pq[0:1, 0:128],
        pq[0:1, 128:256],
        pkv[0:1, 0:128],
        pq[0:1, 256:384],
        pq[0:1, 384:512],
        pkv[0:1, 128:256],
        jnp.where(lane1 == z, count, 0.0),
        last,
    ]
    for i, row in enumerate(rows):
        ebuf[1 + z, i : i + 1, 256:384] = row

    pl.semaphore_wait(barrier, jnp.where(z == NZ - 1, 21 + NZ, 21))

    send_all(EDGE, z, at_z, lambda p: ebuf.at[1 + z], ebuf.at[1 + z], ebuf.at[pl.ds(1, 7)])

    def prev_copy(p):
        return pltpu.make_async_remote_copy(
            src_ref=ebuf.at[1 + z],
            dst_ref=ebuf.at[0],
            send_sem=prev_sem.at[0],
            recv_sem=prev_sem.at[1],
            device_id=(lax.rem(y + 1, NY) * NZ + p, hd),
            device_id_type=MESH,
        )

    @pl.when(z == NZ - 1)
    def _():
        for p in range(NZ):
            prev_copy(p).start()

    send_all(SCAN1, z, at_z, lambda p: s1_send.at[p], s1.at[z], s1.at[pl.ds(0, 7)])
    s1[z] = s1_send[z]

    def w0_parts(yp):
        rg = lax.rem(yp, 4)
        ch = yp // 4
        r = pl.ds(pl.multiple_of(16 * rg, 16), 16)
        return (
            (
                wq_hbm.at[r, pl.ds(pl.multiple_of(256 * ch, 256), 256)],
                wbuf.at[ch, y, z, rg, :, pl.ds(0, 256)],
            ),
            (
                wkv_hbm.at[r, pl.ds(pl.multiple_of(128 * ch, 128), 128)],
                wbuf.at[ch, y, z, rg, :, pl.ds(256, 128)],
            ),
        )

    def w0_copies():
        copies = []
        for d in FAR_FIRST:
            yp = lax.rem(y + d, NY)
            for i, (src, dst) in enumerate(w0_parts(yp)):
                copies.append(
                    pltpu.make_async_remote_copy(
                        src_ref=src,
                        dst_ref=dst,
                        send_sem=w0_sem.at[0, i],
                        recv_sem=w0_sem.at[1, i],
                        device_id=at_y(yp),
                        device_id_type=MESH,
                    )
                )
        return copies

    @pl.when(y < 2)
    def _():
        for copy in w0_copies():
            copy.start()
        for i, (src, dst) in enumerate(w0_parts(y)):
            pltpu.make_async_copy(src, dst, w0_sem.at[1, i]).start()

    for copy in load[10:]:
        copy.start()

    l_c.wait()
    cm = c_ref[...]
    affinity = jnp.where(causal, nt(cm, bm), 0.0)
    mix = []
    for h in range(HEADS):
        spread = jnp.where(causal, run_col[h] - run_row[h : h + 1, :], 0.0)
        mix.append((jnp.exp(spread) * (affinity * gain_row[h : h + 1, :])).astype(BF16))

    col = iota((128, 1024), 1)
    part_of = col // 256
    lane_of = lax.rem(col, 256) // HP + jnp.where(part_of > 0, 12 + 4 * part_of, 0)
    spread_head = jnp.where(iota((128, 1024), 0) == lane_of, 1.0, 0.0).astype(F32)
    pick_n = jnp.where(si == 16 * z + lax.rem(ti, 16), 1.0, 0.0).astype(BF16)
    same = iota((L, 24), 0) // 16 == lax.rem(iota((L, 24), 1), 8)
    nothing = (iota((8, 256), 0) + y) == 0

    recv_all(EDGE)
    prev_copy(0).wait_recv()
    edges = ebuf[...]
    tiles = edges[1:, :, 256:384]
    stats_y[y] = jnp.sum(tiles, axis=0)
    send_all(STATS_Y, y, at_y, lambda p: stats_y.at[y], stats_y.at[y], stats_y.at[pl.ds(0, 7)])

    by_head = nn(tiles[:, 7, :], spread_head, EXACT)
    lz = by_head[:, 0:256]

    edge_x, edge_b = [], []
    for t in range(3):
        earlier = jnp.where(nothing, 0.0, edges[0:8, 3 + t, 0:256])
        conv_t = silu(edges[1:, t, 0:256] + earlier).astype(BF16).astype(F32)
        edge_x.append(conv_t * by_head[:, 256 * (1 + t) : 256 * (2 + t)])
        edge_b.append(edges[1:, 6 + t // 2, 128 * (t % 2) : 128 * (t % 2 + 1)])
    edge_x = jnp.concatenate(edge_x, axis=0).astype(BF16)
    edge_b = jnp.concatenate(edge_b, axis=0).astype(BF16)
    spots = nt(pick_n, edge_b)
    added = nn(jnp.where(same, spots, 0.0).astype(BF16), edge_x).reshape(8, 16, 256)
    recv_all(SCAN1)
    acc = jnp.zeros((16, 256), F32)
    cum = jnp.zeros((1, 256), F32)
    before, cums = [], []
    for j in range(NZ):
        before.append(acc)
        cums.append(cum)
        acc = jnp.exp(lz[j : j + 1, :]) * acc + (s1[j].astype(F32) + added[j])
        cum = cum + lz[j : j + 1, :]
    s2[y] = acc.astype(BF16)
    send_all(SCAN2, y, at_y, lambda p: s2.at[y], s2.at[y], s2.at[pl.ds(0, 7)])

    for i, cols in enumerate((pl.ds(0, 256), pl.ds(256, 128))):
        finish(wbuf.at[0, :, z, 0, :, cols], w0_sem.at[1, i])
    rg_me = lax.rem(y, 4)
    ch_me = y // 4
    pieces7 = wbuf.at[ch_me, 0, pl.ds(0, 7), rg_me]
    own_a = wbuf.at[ch_me, 0, z, rg_me]
    own_b = wbuf.at[ch_me, 1, z, rg_me]
    send_all(W_BY, y, at_y, lambda p: own_b, own_b, pieces7)
    send_all(W_AZ, z, at_z, lambda p: own_a, own_a, pieces7)

    before_rows = pltpu.roll(ebuf[z, :, 0:256], 5, 0)
    lead = (iota((8, 256), 0) < 3) & (s > 0)
    top_rows = silu(summed[0:8] + jnp.where(lead, before_rows, 0.0)).astype(BF16).astype(F32)
    conv_f = jnp.concatenate([top_rows, conv_own[8:]], axis=0)
    conv = conv_f.astype(BF16)

    within = []
    zero = jnp.zeros((), BF16)
    for i in range(2):
        pair = conv[:, 128 * i : 128 * (i + 1)]
        stacked = jnp.concatenate(
            [jnp.where(first, pair, zero), jnp.where(first, zero, pair)], axis=0
        )
        within.append(nn(jnp.concatenate([mix[2 * i], mix[2 * i + 1]], axis=1), stacked))
    l_skip.wait()
    skip_v = skip_ref[...]
    skip = jnp.zeros((1, 256), F32)
    head_of = iota((1, 256), 1) // HP
    for h in range(HEADS):
        skip = jnp.where(head_of == h, skip_v[:, h : h + 1], skip)
    mixed_near = jnp.concatenate(within, axis=1) + skip * conv_f
    exp_run = jnp.exp(run_x)
    l_gate.wait()
    gate = silu(gate_ref[...].astype(F32))

    def block_a(p, cols, lo=0, n=8):
        return wbuf.at[p // 4, 0, pl.ds(lo, n), lax.rem(p, 4), :, cols]

    def block_b(p, cols, lo=0, n=2):
        return wbuf.at[pl.ds(lo, n), 1, p, :, :, cols]

    def rings(step, wait, kv):
        cols = pl.ds(256, 128) if kv else pl.ds(0, 256)
        ex = (RING_KV if kv else RING_Q) + step
        if step == 3:
            moved = wbuf.at[:, 0, pl.ds(0, 2), :, :, cols]
        elif step == 0:
            moved = wbuf.at[:, :, pl.ds(0, 4), :, :, cols]
        else:
            moved = wbuf.at[:, :, pl.ds(0, 2), :, :, cols]
        if wait:
            finish(moved, recv_sem.at[ex])
            return
        pending.append((moved, send_sem.at[ex]))
        for me, where, block, whole in ((y, at_y, block_a, 8), (z, at_z, block_b, 2)):
            for way, hops in ((0, 2), (1, 2), (0, 1), (1, 1)) if step == 0 else ((0, 1), (1, 1)):
                ahead = lax.rem(me + (hops if way == 0 else 8 - hops), 8)
                of = lax.rem(me + (8 - step if way == 0 else step), 8)
                if step == 3:
                    part = block(of, cols, way * whole // 2, whole // 2)
                else:
                    part = block(of, cols)
                pltpu.make_async_remote_copy(
                    src_ref=part,
                    dst_ref=part,
                    send_sem=send_sem.at[ex],
                    recv_sem=recv_sem.at[ex],
                    device_id=where(ahead),
                    device_id_type=MESH,
                ).start()

    recv_all(STATS_Y)
    ytiles = stats_y[...]
    pad_total = jnp.sum(ytiles, axis=0)
    ly = nn(ytiles[:, 7, :], spread_head[:, 0:256], EXACT)

    recv_all(SCAN2)
    rows_before = jnp.zeros((16, 256), F32)
    for j in range(NY - 1):
        longer = jnp.exp(ly[j : j + 1, :]) * rows_before + s2[j].astype(F32)
        rows_before = jnp.where(j < y, longer, rows_before)
    for j in range(NZ):
        s3_send[j] = (before[j] + jnp.exp(cums[j]) * rows_before).astype(BF16)
    send_all(SCAN3, z, at_z, lambda p: s3_send.at[p], s3.at[z], s3.at[pl.ds(0, 7)])
    s3[z] = s3_send[z]

    recv_all(W_AZ)
    recv_all(W_BY)
    rings(0, False, True)
    rings(0, False, False)

    l_ngain.wait()
    bnd = bounds - s * L
    byte_at = iota((L, CAP), 0)
    slot_at = iota((L, CAP), 1)
    usable = bounds < NY * NZ * L
    picker = jnp.where((byte_at == bnd) & usable, 1.0, 0.0).astype(BF16)
    upto = jnp.where((bnd <= byte_at) & usable, 1.0, 0.0)
    newest = jnp.sum(upto, axis=1, keepdims=True) - 1.0
    spreader = jnp.where(slot_at.astype(F32) == newest, 1.0, 0.0).astype(BF16)
    l_res.wait()
    res = res_ref[...]
    res_span = tn(picker, res)

    span_pick = tn(picker, eye)
    span_c = nn(span_pick.astype(BF16), cm).astype(BF16)
    span_near = nn(span_pick, mixed_near, EXACT)
    span_run = nn(span_pick, exp_run, EXACT)
    span_gate = nn(span_pick, gate, EXACT)

    def normalize(near, read, run, opening, states):
        gated = (near + nn(read, states) * run) * opening
        mean_sq = jnp.sum(gated * gated, axis=1, keepdims=True) * (1.0 / 256)
        return (gated * lax.rsqrt(mean_sq + EPSILON) * ngain_ref[...]).astype(BF16)

    lane = iota((CAP, 128), 1)
    counts = ytiles[:, 6, :]
    lane8 = iota((8, 128), 1)
    ahead = (lane8 < NZ) & (iota((8, 128), 0) * NZ + lane8 < s)
    offset = jnp.sum(jnp.where(ahead, counts, 0.0), axis=0, keepdims=True)
    offset = jnp.sum(offset, axis=1, keepdims=True)
    place = iota((CAP, 128), 0).astype(F32) + offset
    freq = jnp.exp(
        lax.rem(lane, HD // 2).astype(F32) * (-2.0 * math.log(THETA) / HD)
    )
    angle = place * freq
    cosine = jnp.cos(angle)
    sine = jnp.where(lane < HD // 2, -jnp.sin(angle), jnp.sin(angle))

    recv_all(SCAN3)
    states = s3[...].reshape(128, 256)
    l_mo.wait()
    span_normed = normalize(span_near, span_c, span_run, span_gate, states)
    span_part = nn(span_normed, mo_ref[...]).astype(BF16)
    for j in range(NHD):
        sp_send[j] = span_part[:, 128 * j : 128 * (j + 1)]
    send_all(SPAN_RS, hd, at_h, lambda p: sp_send.at[p], sp_recv.at[hd], sp_recv.at[pl.ds(0, 7)])
    sp_recv[hd] = sp_send[hd]

    rings(0, True, True)
    rings(2, False, True)
    rings(0, True, False)
    rings(2, False, False)

    normed = normalize(mixed_near, cm, exp_run, gate, states)
    enc_part = nn(normed, mo_ref[...]).astype(BF16)
    for j in range(NHD):
        en_send[j] = enc_part[:, 128 * j : 128 * (j + 1)]
    en_recv[hd] = en_send[hd]


    recv_all(SPAN_RS)
    span_share = (res_span + jnp.sum(sp_recv[...].astype(F32), axis=0)).astype(BF16)
    ag[hd] = span_share
    send_all(SPAN_AG, hd, at_h, lambda p: ag.at[hd], ag.at[hd], ag.at[pl.ds(0, 7)])

    rings(2, True, True)
    rings(3, False, True)
    rings(2, True, False)
    rings(3, False, False)

    key = iota((512, 128), 0)
    key_y = lax.rem(y + 16 - (key // 128) * sy, NY)
    key_z = lax.rem(z + 16 - lax.rem(key // CAP, 4) * sz, NZ)
    expand = jnp.where(iota((512, 128), 1) == key_z, 1.0, 0.0).astype(BF16)
    per_row = nt(expand, jnp.concatenate([ytiles[:, 6, :], ytiles[:, 6, :]], axis=0).astype(BF16))
    lane16 = iota((512, 16), 1)
    key_count = jnp.sum(
        jnp.where(lane16 == lax.rem(y + 16 - (iota((512, 16), 0) // 128) * sy, NY), per_row, 0.0),
        axis=1,
        keepdims=True,
    )
    key_slot = lax.rem(key, CAP)
    key_rank = (key_y * NZ + key_z) * CAP + key_slot
    key_rank = jnp.where(key_slot.astype(F32) < key_count, key_rank, NY * NZ * CAP)
    key_ranks[...] = key_rank
    query = iota((1, 512), 1)
    query_rank = (
        (
            lax.rem(y + 8 - py + query // 256, NY) * NZ
            + lax.rem(z + 8 - pz + lax.rem(query // 128, 2), NZ)
        )
        * CAP
        + lax.rem(query, CAP)
    )

    recv_all(SPAN_AG)
    sq = jnp.zeros((CAP, 128), F32)
    pieces = []
    for j in range(NHD):
        piece = ag[j].astype(F32)
        sq = sq + piece * piece
        pieces.append((piece * mg[j : j + 1, :]).astype(BF16))
    sq = jnp.sum(sq, axis=1, keepdims=True)
    scale = lax.rsqrt((sq + pad_sq) * (1.0 / D_MAIN) + EPSILON)
    span_x = jnp.concatenate(pieces, axis=1)
    rings(3, True, True)
    def project(ch, lo, n):
        return nn(span_x, wbuf[ch, :, :, :, :, lo : lo + n].reshape(1024, n))

    def column(part, i):
        return (part + pad_total[i : i + 1, :]) * scale

    def rotate(v):
        return (v * cosine + pltpu.roll(v, HD // 2, 1) * sine).astype(BF16)

    def slot_sends(ex, buf):
        for i, j in SLOTS:
            pltpu.make_async_remote_copy(
                src_ref=buf.at[0],
                dst_ref=buf.at[4 * i + j],
                send_sem=send_sem.at[ex],
                recv_sem=recv_sem.at[ex],
                device_id=at_slot(i, j),
                device_id_type=MESH,
            ).start()
        pending.append((buf.at[pl.ds(0, 15)], send_sem.at[ex]))

    kbuf[0] = rotate(column(project(0, 256, 128), 2))
    slot_sends(KEYS, kbuf)
    vbuf[0] = column(project(1, 256, 128), 5).astype(BF16)
    slot_sends(VALUES, vbuf)
    mine = 2 * py + pz

    rings(3, True, False)
    for ch in range(2):
        pair = project(ch, 0, 256)
        for h in range(2):
            at = CAP * (2 * ch + h)
            part = pair[:, 128 * h : 128 * (h + 1)]
            qbuf[mine, at : at + CAP, :] = rotate(column(part, 3 * ch + h))

    def group_copy(i, e, src, dst):
        return pltpu.make_async_remote_copy(
            src_ref=src,
            dst_ref=dst,
            send_sem=send_sem.at[i],
            recv_sem=recv_sem.at[i],
            device_id=member(e)[0],
            device_id_type=MESH,
        )

    for e in range(1, 4):
        group_copy(QUERIES, e, qbuf.at[mine], qbuf.at[mine]).start()
    pending.append((qbuf.at[pl.ds(0, 3)], send_sem.at[QUERIES]))

    send_all(ENC_RS, hd, at_h, lambda p: en_send.at[p], en_recv.at[hd], en_recv.at[pl.ds(0, 7)])

    finish(qbuf.at[pl.ds(0, 3)], recv_sem.at[QUERIES])
    finish(kbuf.at[pl.ds(0, 15)], recv_sem.at[KEYS])

    keys = kbuf[...].reshape(512, HD)
    ranks = key_ranks[...]
    unit = 1.0 / math.sqrt(HD)
    weights = []
    for m in range(4):
        scores = nt(keys, qbuf[m])
        allowed = ranks <= query_rank[:, 128 * m : 128 * (m + 1)]
        scores = jnp.where(allowed, scores * unit, -1e30)
        top = jnp.max(scores, axis=0, keepdims=True)
        part = jnp.exp(scores - top)
        weights.append(part.astype(BF16))
        m_send[m, 0:1, :] = top
        m_send[m, 1:2, :] = jnp.sum(part, axis=0, keepdims=True)
    for e in range(1, 4):
        group_copy(OUT_STATS, e, m_send.at[member(e)[1]], m_recv.at[e]).start()

    finish(vbuf.at[pl.ds(0, 15)], recv_sem.at[VALUES])
    values = vbuf[...].reshape(512, HD)
    for m in range(4):
        o_send[m] = tn(values, weights[m]).astype(BF16)

    for e in range(1, 4):
        group_copy(OUT_SUMS, e, o_send.at[member(e)[1]], o_recv.at[e]).start()
    sums3, stats3 = o_recv.at[pl.ds(1, 3)], m_recv.at[pl.ds(1, 3)]
    pending.append((sums3, send_sem.at[OUT_SUMS]))
    pending.append((stats3, send_sem.at[OUT_STATS]))
    o_recv[0] = o_send[mine]
    m_recv[0] = m_send[mine]

    finish(sums3, recv_sem.at[OUT_SUMS])
    finish(stats3, recv_sem.at[OUT_STATS])

    tops = m_recv[:, 0, :]
    highest = jnp.max(tops, axis=0, keepdims=True)
    shrink = jnp.exp(tops - highest)
    total = jnp.sum(shrink * m_recv[:, 1, :], axis=0, keepdims=True)
    summed_o = jnp.zeros((HD, 128), F32)
    for e in range(4):
        summed_o = summed_o + shrink[e : e + 1, :] * o_recv[e].astype(F32)
    attended = (summed_o / total).T.astype(BF16)

    l_mw.wait()
    att = jnp.concatenate([attended[CAP * i : CAP * (i + 1), :] for i in range(4)], axis=1)
    main_part = nn(att, mw_ref[...]).astype(BF16)
    for j in range(NHD):
        mn_send[j] = main_part[:, 128 * j : 128 * (j + 1)]
    send_all(MAIN_RS, hd, at_h, lambda p: mn_send.at[p], mn_recv.at[hd], mn_recv.at[pl.ds(0, 7)])
    mn_recv[hd] = mn_send[hd]
    recv_all(ENC_RS)
    encoded = (res.astype(F32) + jnp.sum(en_recv[...].astype(F32), axis=0)).astype(BF16)

    recv_all(MAIN_RS)
    main_rows = (span_share.astype(F32) + jnp.sum(mn_recv[...].astype(F32), axis=0)).astype(BF16)
    out_ref[...] = (encoded.astype(F32) + nn(spreader, main_rows)).astype(BF16)

    for blocks, sem in pending:
        finish(blocks, sem)

    @pl.when(y < 2)
    def _():
        for i, cols in enumerate((pl.ds(0, 256), pl.ds(256, 128))):
            finish(wbuf.at[0, 0, pl.ds(0, 7), 0, :, cols], w0_sem.at[0, i])

    @pl.when(z == NZ - 1)
    def _():
        finish(ebuf.at[pl.ds(0, NZ)], prev_sem.at[0])


def shards(
    byte_stream,
    gate_stream,
    conv_weight,
    state_write,
    state_read,
    step_size,
    decay_coef,
    skip_gain,
    norm_gain,
    mixer_out,
    residual,
    boundaries,
    span_counts,
    span_offsets,
    pad_vector,
    main_gain,
    query_weight,
    key_value_weight,
    main_out_weight,
):
    far = pl.BlockSpec(memory_space=pl.ANY)
    near = pl.BlockSpec(memory_space=pltpu.VMEM)
    vm = pltpu.VMEM
    dma = pltpu.SemaphoreType.DMA
    return pl.pallas_call(
        kernel,
        out_shape=pltpu.VMEM((L, 128), BF16),
        in_specs=[far] * 17,
        out_specs=near,
        scratch_shapes=[
            vm((4, 256), F32),
            vm((HEADS, L), F32),
            vm((1, HEADS), F32),
            vm((1, HEADS), F32),
            vm((1, 256), F32),
            vm((1, CAP), jnp.int32),
            vm((24, 128), BF16),
            vm((32, 128), F32),
            vm((L, 256), BF16),
            vm((L, 256), BF16),
            vm((L, 128), BF16),
            vm((L, 128), BF16),
            vm((256, 1024), BF16),
            vm((L, 128), BF16),
            vm((64, 512), BF16),
            vm((64, 256), BF16),
            vm((512, 1024), BF16),
            vm((L + 16, 256), F32),
            vm((9, 8, 384), F32),
            vm((8, 8, 128), F32),
            vm((2, 2, 8, 4, 16, 384), BF16),
            vm((8, 16, 256), BF16),
            vm((8, 16, 256), BF16),
            vm((8, 16, 256), BF16),
            vm((8, 16, 256), BF16),
            vm((8, 16, 256), BF16),
            vm((8, CAP, 128), BF16),
            vm((8, CAP, 128), BF16),
            vm((8, CAP, 128), BF16),
            vm((8, L, 128), BF16),
            vm((8, L, 128), BF16),
            vm((16, CAP, 128), BF16),
            vm((16, CAP, 128), BF16),
            vm((4, 128, 128), BF16),
            vm((512, 128), jnp.int32),
            vm((4, 128, 128), BF16),
            vm((4, 8, 128), F32),
            vm((4, 128, 128), BF16),
            vm((4, 8, 128), F32),
            vm((8, CAP, 128), BF16),
            vm((8, CAP, 128), BF16),
            dma((17,)),
            dma((2,)),
            dma((2, 2)),
            dma((N_SEM,)),
            dma((N_SEM,)),
        ],
        compiler_params=pltpu.CompilerParams(
            collective_id=0, has_side_effects=True, vmem_limit_bytes=56 * 1024 * 1024
        ),
        cost_estimate=pl.CostEstimate(flops=10**9, bytes_accessed=4 * 10**6, transcendentals=10**6),
    )(
        byte_stream,
        gate_stream,
        conv_weight,
        state_write,
        state_read,
        step_size.T,
        decay_coef.reshape(1, HEADS),
        skip_gain.reshape(1, HEADS),
        norm_gain.reshape(1, 256),
        mixer_out,
        residual,
        boundaries,
        pad_vector.reshape(24, 128),
        main_gain.reshape(32, 128),
        query_weight,
        key_value_weight,
        main_out_weight,
    )


def solution(mesh):
    in_specs = (
        P("seq", "head"),
        P("seq", "head"),
        P(None, "head"),
        P("seq", None),
        P("seq", None),
        P("seq", "head"),
        P("head"),
        P("head"),
        P("head"),
        P("head", None),
        P("seq", None),
        P("seq", None),
        P("seq"),
        P("seq"),
        P(),
        P(),
        P("seq", "head"),
        P("seq", "head"),
        P("head", None),
    )
    out_specs = P("seq", "head")
    return jax.shard_map(shards, mesh=mesh, in_specs=in_specs, out_specs=out_specs, check_vma=False)
```
